32 devices in a mesh: seq: 16 (over z, y, x), head: 2 (over core).
Axes of the slice: x: 2, y: 2, z: 4, core: 2. Of those that a mesh axis runs over, the one named last changes fastest.
Arguments:
- block_input: bfloat16 [12, 1024, 1024], P(None, 'seq'), may hold values from -6 to 6
- seq_lengths: int32 [12], replicated, may hold values from 128 to 1024, as said below
- attn_gain: float32 [1024], replicated, may hold values from 0.5 to 1.5
- query_heads: bfloat16 [1024, 96], P(None, 'head'), may hold values from -1 to 1
- query_basis: bfloat16 [1024, 384], replicated, may hold values from -0.1875 to 0.1875
- key_heads: bfloat16 [1024, 32], P(None, 'head'), may hold values from -0.1875 to 0.1875
- key_basis: bfloat16 [1024, 128], replicated, may hold values from -0.1875 to 0.1875
- value_heads: bfloat16 [1024, 32], P(None, 'head'), may hold values from -0.1875 to 0.1875
- value_basis: bfloat16 [1024, 128], replicated, may hold values from -0.1875 to 0.1875
- out_project: bfloat16 [1024, 1024], P('head'), may hold values from -1.5 to 1.5
- ffn_gain: float32 [1024], replicated, may hold values from 0.5 to 1.5
- gate_weight: bfloat16 [1024, 2816], P(None, 'head'), may hold values from -0.1875 to 0.1875
- up_weight: bfloat16 [1024, 2816], P(None, 'head'), may hold values from -0.1875 to 0.1875
- down_weight: bfloat16 [2816, 1024], P('head'), may hold values from -0.109375 to 0.109375
- out_cotangent: bfloat16 [12, 1024, 1024], P(None, 'seq'), may hold values from -6 to 6
Outputs:
- block_output: bfloat16 [12, 1024, 1024], P(None, 'seq')
- input_grad: float32 [12, 1024, 1024], P(None, 'seq')
- attn_gain_grad: float32 [1024], replicated
- query_heads_grad: float32 [1024, 96], P(None, 'head')
- query_basis_grad: float32 [1024, 384], replicated
- key_heads_grad: float32 [1024, 32], P(None, 'head')
- key_basis_grad: float32 [1024, 128], replicated
- value_heads_grad: float32 [1024, 32], P(None, 'head')
- value_basis_grad: float32 [1024, 128], replicated
- out_project_grad: float32 [1024, 1024], P('head')
- ffn_gain_grad: float32 [1024], replicated
- gate_grad: float32 [1024, 2816], P(None, 'head')
- up_grad: float32 [1024, 2816], P(None, 'head')
- down_grad: float32 [2816, 1024], P('head')
The draws below stay inside these ranges and needn't reach their ends.
Inputs may be any that keep to these rules, and one draw needn't show every extreme that they name: `seq_lengths`: at least one row, drawn from the seed, has the full length 1024.
All inputs are finite; a program needn't handle non-finite values.
Results may differ from the reference program's by a relative error of at most 0.025.
The reference program's roundings to bfloat16 on the way count: a program that leaves them out, or rounds other values in their place, can miss the bound.
Values may be sent and summed in bfloat16 or wider, within the bound.
A program may use at most 384 MiB of HBM per device.

```python
import math
import jax
import jax.numpy as jnp
from jax import lax

D = 1024
H = 16
DH = 64
RQ = 6
RK = 2
RV = 2
FF = 2816
ROWS = 12
MIN_LEN = 128
SEQ_LEN = 1024


def draw_seq_lengths(key, part):
    key = jax.random.fold_in(key, 7)
    pick_key, first_key, second_key = jax.random.split(key, 3)
    span = SEQ_LEN - MIN_LEN
    first_draw = jax.random.randint(first_key, (ROWS,), 0, span + 1)
    second_draw = jax.random.randint(second_key, (ROWS,), 0, span + 1)
    extra = first_draw * second_draw // max(span, 1)
    lengths = MIN_LEN + extra
    chosen = jax.random.randint(pick_key, (), 0, ROWS)
    return jnp.where(jnp.arange(ROWS) == chosen, SEQ_LEN, lengths).astype(jnp.int32)


def level_of(stream_key, shape, shards, least, high):
    factor_of, own = 1.0, jax.random.fold_in(stream_key, 6)
    for dim, parts in shards:
        draws = jnp.exp(jax.random.uniform(jax.random.fold_in(own, dim), (parts,), jnp.float32, least / len(shards), high / len(shards)))
        factor_of = factor_of * jnp.repeat(draws, shape[dim] // parts).reshape([-1 if axis == dim else 1 for axis in range(len(shape))])
    return factor_of


def noise(stream_key, dims, scale, reach, cuts=(), dtype=jnp.bfloat16):
    drawn = jax.random.normal(stream_key, dims, jnp.float32) * scale
    if len(cuts) > 0:
        drawn = level_of(stream_key, dims, cuts, -0.22, 0.18) * drawn
    return jnp.clip(drawn, min=-reach, max=reach).astype(dtype)


def setup_inputs(seed: int = 0) -> dict:
    keys = jax.random.split(jax.random.key(seed), 16)
    return {
        "block_input": noise(keys[0], (ROWS, SEQ_LEN, D), 1.0, 6.0, ((1, 16),)),
        "seq_lengths": draw_seq_lengths(jax.random.fold_in(keys[15], 71), 0),
        "attn_gain": jnp.clip(1.0 + 0.1 * jax.random.normal(keys[2], (D,), jnp.float32), 0.5, 1.5),
        "query_heads": noise(keys[3], (D, H * RQ), (D // 36) ** -0.5, 1.0, ((1, 2),)),
        "query_basis": noise(keys[4], (D, RQ * DH), D ** -0.5, 0.1875),
        "key_heads": noise(keys[5], (D, H * RK), D ** -0.5, 0.1875, ((1, 2),)),
        "key_basis": noise(keys[6], (D, RK * DH), D ** -0.5, 0.1875),
        "value_heads": noise(keys[7], (D, H * RV), D ** -0.5, 0.1875, ((1, 2),)),
        "value_basis": noise(keys[8], (D, RV * DH), D ** -0.5, 0.1875),
        "out_project": noise(keys[9], (H * DH, D), (H * DH // 64) ** -0.5, 1.5, ((0, 2),)),
        "ffn_gain": jnp.clip(1.0 + 0.1 * jax.random.normal(keys[10], (D,), jnp.float32), 0.5, 1.5),
        "gate_weight": noise(keys[11], (D, FF), D ** -0.5, 0.1875, ((1, 2),)),
        "up_weight": noise(keys[12], (D, FF), D ** -0.5, 0.1875, ((1, 2),)),
        "down_weight": noise(keys[13], (FF, D), FF ** -0.5, 0.109375, ((0, 2),)),
        "out_cotangent": noise(keys[14], (ROWS, SEQ_LEN, D), 1.0, 6.0, ((1, 16),)),
    }


@jax.custom_vjp
def low(v):
    return lax.optimization_barrier(v.astype(jnp.bfloat16)).astype(jnp.float32)

@jax.custom_vjp
def low_back(v):
    return v

def low_keep(v):
    return (low(v), None)

def low_pass(kept, grad):
    return (grad,)

def back_keep(v):
    return (v, None)

def back_low(kept, grad):
    return (low(grad),)
low.defvjp(low_keep, low_pass)
low_back.defvjp(back_keep, back_low)
highest = lax.Precision.HIGHEST
epsilon = 1e-06

def rope_angles(position):
    half_dim = DH // 2
    frequency = jnp.exp(jnp.arange(half_dim).astype(jnp.float32) * (-2.0 * math.log(10000.0) / DH))
    angles = position[:, None] * frequency[None, :]
    return (jnp.cos(angles), jnp.sin(angles))

def rotate(basis, cos_table, sin_table):
    half_dim = basis.shape[-1] // 2
    first_half = basis[..., :half_dim]
    second_half = basis[..., half_dim:]
    cos_rows = cos_table[:, None, :]
    sin_rows = sin_table[:, None, :]
    return jnp.concatenate([first_half * cos_rows - second_half * sin_rows, first_half * sin_rows + second_half * cos_rows], axis=-1)

def rms_scale(tensor):
    return lax.rsqrt(lax.optimization_barrier(jnp.mean(tensor * tensor, axis=-1, keepdims=True)) + epsilon)

def project(activations, weight):
    return jnp.einsum('gld,de->gle', activations, weight, precision=highest)

def attend(queries, key_rows, value_rows, row_lens):
    groups, length = (queries.shape[0], queries.shape[1])
    block_size = math.gcd(length, 512)
    block_count = length // block_size
    score_scale = 1.0 / math.sqrt(DH)
    key_pos = jnp.arange(length)
    stacked = queries.reshape(groups, block_count, block_size, H, DH).transpose(1, 0, 2, 3, 4)

    @jax.checkpoint
    def one_block(block_item):
        q_part, block_index = block_item
        query_pos = block_index * block_size + jnp.arange(block_size)
        raw_scores = jnp.einsum('gqhd,gkhd->ghqk', q_part, key_rows, precision=highest)
        scores = low_back(raw_scores * score_scale)
        valid_mask = (key_pos[None, None, None, :] <= query_pos[None, None, :, None]) & (key_pos[None, None, None, :] < row_lens[:, None, None, None])
        scores = jnp.where(valid_mask, scores, -1e+30)
        row_peak = lax.optimization_barrier(jnp.max(scores, axis=-1, keepdims=True))
        exp_scores = jnp.exp(scores - row_peak)
        attn_weights = low(exp_scores / lax.optimization_barrier(jnp.sum(exp_scores, axis=-1, keepdims=True)))
        return jnp.einsum('ghqk,gkhd->gqhd', attn_weights, value_rows, precision=highest)
    attended = lax.map(one_block, (stacked, jnp.arange(block_count)))
    return attended.transpose(1, 0, 2, 3, 4).reshape(groups, length, H, DH)

def block_forward(params, inputs, row_lens):
    attn_gain, query_heads, query_basis, key_heads, key_basis, value_heads, value_basis, out_project, ffn_gain, gate_weight, up_weight, down_weight = params
    groups, length = (inputs.shape[0], inputs.shape[1])
    cos_table, sin_table = rope_angles(jnp.arange(length).astype(jnp.float32))
    normed = low(inputs * rms_scale(inputs) * attn_gain)
    q_heads = low_back(project(normed, query_heads)).reshape(groups, length, H, RQ)
    q_basis = rotate(low_back(project(normed, query_basis)).reshape(groups, length, RQ, DH), cos_table, sin_table)
    k_heads = low(low_back(project(normed, key_heads))).reshape(groups, length, H, RK)
    k_basis = low(rotate(low_back(project(normed, key_basis)).reshape(groups, length, RK, DH), cos_table, sin_table))
    v_heads = low(low_back(project(normed, value_heads))).reshape(groups, length, H, RV)
    v_basis = low(low_back(project(normed, value_basis))).reshape(groups, length, RV, DH)
    queries = low(jnp.einsum('glhr,glrd->glhd', q_heads, q_basis, precision=highest) / RQ)
    key_rows = low(jnp.einsum('glhr,glrd->glhd', k_heads, k_basis, precision=highest) / RK)
    value_rows = low(jnp.einsum('glhr,glrd->glhd', v_heads, v_basis, precision=highest) / RV)
    mixed = low_back(low(attend(queries, key_rows, value_rows, row_lens)))
    attn_out = low_back(project(mixed.reshape(groups, length, H * DH), out_project))
    middle = inputs + attn_out
    normed_two = low(middle * rms_scale(middle) * ffn_gain)
    gate_act = low_back(project(normed_two, gate_weight))
    up_act = low_back(project(normed_two, up_weight))
    hidden = low(jax.nn.silu(gate_act) * up_act)
    return middle + project(hidden, down_weight)

def reference(block_input, seq_lengths, attn_gain, query_heads, query_basis, key_heads, key_basis, value_heads, value_basis, out_project, ffn_gain, gate_weight, up_weight, down_weight, out_cotangent):
    params = tuple((tensor.astype(jnp.float32) for tensor in (attn_gain, query_heads, query_basis, key_heads, key_basis, value_heads, value_basis, out_project, ffn_gain, gate_weight, up_weight, down_weight)))
    group_size = math.gcd(ROWS, max(1, 4096 // SEQ_LEN))
    step_count = ROWS // group_size
    stacked_in = block_input.astype(jnp.float32).reshape(step_count, group_size, SEQ_LEN, D)
    stacked_len = seq_lengths.reshape(step_count, group_size)

    def forward(inputs, weights):

        def advance(carry, item_pair):
            return (carry, block_forward(weights, item_pair[0], item_pair[1]))
        unused, outputs = lax.scan(advance, jnp.zeros((), jnp.float32), (inputs, stacked_len))
        return outputs
    outputs, pullback = jax.vjp(forward, stacked_in, params)
    cotangent = out_cotangent.astype(jnp.float32).reshape(step_count, group_size, SEQ_LEN, D)
    input_grad, grads = pullback(cotangent)
    return (outputs.reshape(ROWS, SEQ_LEN, D).astype(jnp.bfloat16), input_grad.reshape(ROWS, SEQ_LEN, D), grads[0], grads[1], grads[2], grads[3], grads[4], grads[5], grads[6], grads[7], grads[8], grads[9], grads[10], grads[11])
```

```python
import functools
import math

import jax
import jax.numpy as jnp
from jax import lax
from jax.experimental import pallas as pl
from jax.experimental.pallas import tpu as pltpu
from jax.sharding import PartitionSpec as P

DH = 64
RQ = 6
RK = 2
RV = 2
LANES = 128
EPS = 1e-06
KEY_BLOCK = 256
F32 = jnp.float32
BF16 = jnp.bfloat16


def dot(a, b):
    return lax.dot_general(a, b, (((1,), (0,)), ((), ())), preferred_element_type=F32)


def dot_nt(a, b):
    return lax.dot_general(a, b, (((1,), (1,)), ((), ())), preferred_element_type=F32)


def dot_tn(a, b):
    return lax.dot_general(a, b, (((0,), (0,)), ((), ())), preferred_element_type=F32)


def lane_of(shape):
    return lax.broadcasted_iota(jnp.int32, shape, len(shape) - 1)


def both_halves(pair):
    swapped = pltpu.roll(pair, DH, 1)
    low = lane_of(pair.shape) < DH
    return jnp.where(low, pair, swapped), jnp.where(low, swapped, pair)


def turn(pair, cos, sin):
    half = DH // 2
    first = lane_of(pair.shape) % DH < half
    other = jnp.where(first, pltpu.roll(pair, LANES - half, 1), pltpu.roll(pair, half, 1))
    return pair * cos + other * sin


def split_heads(rows, head_rows, tokens):
    group = lane_of(rows.shape) // DH
    return jnp.concatenate([jnp.where(group == h, rows, jnp.zeros_like(rows)) for h in range(head_rows)], axis=0)


def join_heads(block, head_rows, tokens):
    out = block[:tokens]
    group = lane_of(out.shape) // DH
    for h in range(1, head_rows):
        out = jnp.where(group == h, block[h * tokens : (h + 1) * tokens], out)
    return out


def factor_kernel(width, x_ref, gain_ref, wqh_ref, wqb_ref, wkb_ref, wvb_ref, wh_ref, cos_ref, sin_ref, eq_ref,
                  xn_ref, aq_ref, bq_ref, q_ref, kv_ref, hd_ref):
    rows, tokens, model = x_ref.shape
    hd = q_ref.shape[2]
    count = rows * tokens
    x = x_ref[...].astype(F32).reshape(count, model)
    scale = lax.rsqrt(jnp.mean(x * x, axis=-1, keepdims=True) + EPS)
    xn = (x * scale * gain_ref[...]).astype(BF16)
    xn_ref[...] = xn.reshape(rows, tokens, model)
    cos = jnp.concatenate([cos_ref[...]] * rows, axis=0)
    sin = jnp.concatenate([sin_ref[...]] * rows, axis=0)
    keys = turn(dot(xn, wkb_ref[...]), cos, sin).astype(BF16)
    values = dot(xn, wvb_ref[...]).astype(BF16)
    heads = dot(xn, wh_ref[...])
    lanes = lane_of((tokens, LANES)) // width
    pack = heads[:tokens]
    for r in range(rows):
        part = slice(r * tokens, (r + 1) * tokens)
        kv_ref[2 * r] = keys[part]
        kv_ref[2 * r + 1] = values[part]
        if r:
            pack = jnp.where(lanes == r, heads[part], pack)
    hd_ref[0] = pack.astype(BF16)
    aq = dot(xn, wqh_ref[...])
    aq_ref[...] = aq.reshape(rows, tokens, aq.shape[1])
    aq_high = aq.astype(BF16)
    aq_low = (aq - aq_high.astype(F32)).astype(BF16)
    basis = dot(xn, wqb_ref[...])
    total = [jnp.zeros((count, LANES), F32) for _ in range(hd // LANES)]
    for p in range(RQ // 2):
        pair = turn(basis[:, p * LANES : (p + 1) * LANES], cos, sin)
        bq_ref[:, :, p * LANES : (p + 1) * LANES] = pair.reshape(rows, tokens, LANES)
        for half, vec in enumerate(both_halves(pair)):
            spread = eq_ref[:, (2 * p + half) * hd : (2 * p + half + 1) * hd]
            coef = dot(aq_high, spread) + dot(aq_low, spread)
            for c in range(hd // LANES):
                total[c] = total[c] + coef[:, c * LANES : (c + 1) * LANES] * vec
    for c in range(hd // LANES):
        low = (total[c] / RQ).astype(BF16).astype(F32) * (1.0 / math.sqrt(DH))
        q_ref[:, :, c * LANES : (c + 1) * LANES] = low.astype(BF16).reshape(rows, tokens, LANES)


def whole(*shape):
    return pl.BlockSpec(shape, lambda *_: (0,) * len(shape))


def factors(x, gain, wqh, wqb, wkb, wvb, wh, cos, sin, eq, pack_rows, width):
    rows, tokens, model = x.shape
    hd = eq.shape[1] // RQ
    packs = rows // pack_rows
    nq = wqh.shape[1]

    def row_block(last):
        return pl.BlockSpec((pack_rows, tokens, last), lambda g: (g, 0, 0))

    return pl.pallas_call(
        functools.partial(factor_kernel, width),
        grid=(packs,),
        in_specs=[row_block(model), whole(1, model), whole(*wqh.shape), whole(*wqb.shape), whole(*wkb.shape),
                  whole(*wvb.shape), whole(*wh.shape), whole(*cos.shape), whole(*sin.shape), whole(*eq.shape)],
        out_specs=[row_block(model), row_block(nq), row_block(RQ * DH), row_block(hd),
                   pl.BlockSpec((2 * pack_rows, tokens, LANES), lambda g: (g, 0, 0)),
                   pl.BlockSpec((1, tokens, LANES), lambda g: (g, 0, 0))],
        out_shape=[
            jax.ShapeDtypeStruct((rows, tokens, model), BF16),
            jax.ShapeDtypeStruct((rows, tokens, nq), F32),
            jax.ShapeDtypeStruct((rows, tokens, RQ * DH), F32),
            jax.ShapeDtypeStruct((rows, tokens, hd), BF16),
            jax.ShapeDtypeStruct((2 * rows, tokens, LANES), BF16),
            jax.ShapeDtypeStruct((packs, tokens, LANES), BF16),
        ],
        compiler_params=pltpu.CompilerParams(vmem_limit_bytes=56 * 2**20),
        name="factors",
    )(x, gain.reshape(1, model), wqh, wqb, wkb, wvb, wh, cos, sin, eq)


def query_grad_kernel(dq_ref, aq_ref, bq_ref, eq_ref, cos_ref, sin_ref, da_ref, db_ref):
    rows, tokens, hd = dq_ref.shape
    count = rows * tokens
    dq = dq_ref[...].reshape(count, hd)
    aq = aq_ref[...].reshape(count, aq_ref.shape[2])
    aq_high = aq.astype(BF16)
    aq_low = (aq - aq_high.astype(F32)).astype(BF16)
    cos = jnp.concatenate([cos_ref[...]] * rows, axis=0)
    sin = jnp.concatenate([sin_ref[...]] * rows, axis=0)
    da = jnp.zeros(aq.shape, F32)
    low = lane_of((count, LANES)) < DH
    for p in range(RQ // 2):
        pair = bq_ref[:, :, p * LANES : (p + 1) * LANES].reshape(count, LANES)
        sums = []
        for half, vec in enumerate(both_halves(pair)):
            spread = eq_ref[:, (2 * p + half) * hd : (2 * p + half + 1) * hd]
            coef = dot(aq_high, spread) + dot(aq_low, spread)
            acc = jnp.zeros((count, LANES), F32)
            prods = []
            for c in range(hd // LANES):
                part = dq[:, c * LANES : (c + 1) * LANES]
                acc = acc + coef[:, c * LANES : (c + 1) * LANES] * part
                prods.append(part * vec)
            prod = jnp.concatenate(prods, axis=1)
            high = prod.astype(BF16)
            rest = (prod - high.astype(F32)).astype(BF16)
            da = da + dot_nt(high, spread) + dot_nt(rest, spread)
            sums.append(acc + pltpu.roll(acc, DH, 1))
        turned = turn(jnp.where(low, sums[0], sums[1]), cos, -sin) * (1.0 / RQ)
        db_ref[:, :, p * LANES : (p + 1) * LANES] = turned.astype(BF16).reshape(rows, tokens, LANES)
    da_ref[...] = (da * (1.0 / RQ)).astype(BF16).reshape(da_ref.shape)


def query_grads(dq, aq, bq, eq, cos, sin, pack_rows):
    rows, tokens, hd = dq.shape
    nq = aq.shape[2]

    def row_block(last):
        return pl.BlockSpec((pack_rows, tokens, last), lambda g: (g, 0, 0))

    return pl.pallas_call(
        query_grad_kernel,
        grid=(rows // pack_rows,),
        in_specs=[row_block(hd), row_block(nq), row_block(RQ * DH), whole(*eq.shape), whole(*cos.shape), whole(*sin.shape)],
        out_specs=[row_block(nq), row_block(RQ * DH)],
        out_shape=[jax.ShapeDtypeStruct((rows, tokens, nq), BF16), jax.ShapeDtypeStruct((rows, tokens, RQ * DH), BF16)],
        compiler_params=pltpu.CompilerParams(vmem_limit_bytes=56 * 2**20),
        name="query_grads",
    )(dq, aq, bq, eq, cos, sin)


def build_rows(basis, coefs, spread, hd):
    first, second = both_halves(basis.astype(F32))
    coef = dot(coefs, spread)
    one, two = coef[:, :hd], coef[:, hd:]
    cols = [one[:, c : c + LANES] * first + two[:, c : c + LANES] * second for c in range(0, hd, LANES)]
    return jnp.concatenate(cols, axis=1).astype(BF16), one, two, first, second


def row_limits(info_ref, row, tokens, block):
    first = info_ref[info_ref.shape[0] - 1]
    length = info_ref[row]
    used = jnp.minimum(length, first + tokens)
    return first, length, (used + block - 1) // block


def limit_lanes(first, length, tokens, lanes):
    slot = lax.broadcasted_iota(jnp.int32, (1, lanes), 1) % tokens
    return jnp.minimum(first + slot, length - 1)


def attend_kernel(pack_rows, group, block, info_ref, q_ref, kv_ref, hd_ref, spread_ref, o_ref, ob_ref, lse_ref, s_ref, v_ref):
    row = pl.program_id(0)
    _, tokens, hd = q_ref.shape
    lanes = group * tokens
    wide = group * DH
    groups = hd // wide
    first, length, blocks = row_limits(info_ref, row, tokens, block)
    limit = limit_lanes(first, length, tokens, lanes)
    queries = [split_heads(q_ref[0, :, g * wide : (g + 1) * wide], group, tokens) for g in range(groups)]
    place = row % pack_rows

    def scores(b, peaks):
        at = pl.ds(pl.multiple_of(b * block, block), block)
        coefs = hd_ref[0, at, :]
        keys, *_ = build_rows(kv_ref[0, at, :], coefs, spread_ref[place, :, : 2 * hd], hd)
        values, *_ = build_rows(kv_ref[1, at, :], coefs, spread_ref[place, :, 2 * hd :], hd)
        position = b * block + lax.broadcasted_iota(jnp.int32, (block, 1), 0)
        live = position < first + tokens
        v_ref[at, :] = jnp.where(live, values.astype(F32), 0.0).astype(BF16)
        out = []
        for g in range(groups):
            raw = dot_nt(keys[:, g * wide : (g + 1) * wide], queries[g])
            raw = jnp.where(position <= limit, raw, -1e30)
            s_ref[at, g * lanes : (g + 1) * lanes] = raw
            out.append(jnp.maximum(peaks[g], jnp.max(raw, axis=0, keepdims=True)))
        return tuple(out)

    peaks = lax.fori_loop(0, blocks, scores, tuple(jnp.full((1, lanes), -1e30, F32) for _ in range(groups)))

    def exps(b, totals):
        at = pl.ds(pl.multiple_of(b * block, block), block)
        out = []
        for g in range(groups):
            part = slice(g * lanes, (g + 1) * lanes)
            e = jnp.exp(s_ref[at, part] - peaks[g])
            s_ref[at, part] = e
            out.append(totals[g] + jnp.sum(e, axis=0, keepdims=True))
        return tuple(out)

    totals = lax.fori_loop(0, blocks, exps, tuple(jnp.zeros((1, lanes), F32) for _ in range(groups)))
    shares = [1.0 / t for t in totals]

    def mix(b, outs):
        at = pl.ds(pl.multiple_of(b * block, block), block)
        res = []
        for g in range(groups):
            p = (s_ref[at, g * lanes : (g + 1) * lanes] * shares[g]).astype(BF16)
            res.append(outs[g] + dot_tn(p, v_ref[at, g * wide : (g + 1) * wide]))
        return tuple(res)

    outs = lax.fori_loop(0, blocks, mix, tuple(jnp.zeros((lanes, wide), F32) for _ in range(groups)))
    for g in range(groups):
        mixed = join_heads(outs[g], group, tokens)
        o_ref[0, :, g * wide : (g + 1) * wide] = mixed
        ob_ref[0, :, g * wide : (g + 1) * wide] = mixed.astype(BF16)
        lse_ref[0, :, g * lanes : (g + 1) * lanes] = peaks[g] + jnp.log(totals[g])


def attend(info, q, kv, shift, spread, pack_rows, group, block):
    rows, tokens, hd = q.shape
    length = kv.shape[1]
    n_lanes = hd // DH * tokens
    grid_spec = pltpu.PrefetchScalarGridSpec(
        num_scalar_prefetch=1,
        grid=(rows,),
        in_specs=[
            pl.BlockSpec((1, tokens, hd), lambda r, i: (r, 0, 0)),
            pl.BlockSpec((2, length, LANES), lambda r, i: (lax.rem(r + i[rows], rows), 0, 0)),
            pl.BlockSpec((1, length, LANES), lambda r, i: (2 * rows + r // pack_rows, 0, 0)),
            pl.BlockSpec(spread.shape, lambda r, i: (0, 0, 0)),
        ],
        out_specs=[
            pl.BlockSpec((1, tokens, hd), lambda r, i: (r, 0, 0)),
            pl.BlockSpec((1, tokens, hd), lambda r, i: (r, 0, 0)),
            pl.BlockSpec((1, 1, n_lanes), lambda r, i: (r, 0, 0)),
        ],
        scratch_shapes=[pltpu.VMEM((length, n_lanes), F32), pltpu.VMEM((length, hd), BF16)],
    )
    return pl.pallas_call(
        functools.partial(attend_kernel, pack_rows, group, block),
        grid_spec=grid_spec,
        out_shape=[
            jax.ShapeDtypeStruct((rows, tokens, hd), F32),
            jax.ShapeDtypeStruct((rows, tokens, hd), BF16),
            jax.ShapeDtypeStruct((rows, 1, n_lanes), F32),
        ],
        compiler_params=pltpu.CompilerParams(vmem_limit_bytes=56 * 2**20),
        name="attend",
    )(info, q, kv, kv, spread)


def attend_back_kernel(pack_rows, group, block, info_ref, q_ref, kv_ref, hd_ref, spread_ref, o_ref, do_ref, lse_ref,
                       dq_ref, dkv_ref, dhd_ref, dq_acc):
    row = pl.program_id(0)
    _, tokens, hd = q_ref.shape
    lanes = group * tokens
    wide = group * DH
    groups = hd // wide
    first, length, blocks = row_limits(info_ref, row, tokens, block)
    limit = limit_lanes(first, length, tokens, lanes)
    place = row % pack_rows
    queries, grads, deltas, peaks = [], [], [], []
    for g in range(groups):
        part = slice(g * wide, (g + 1) * wide)
        do = do_ref[0, :, part]
        queries.append(split_heads(q_ref[0, :, part], group, tokens))
        grads.append(split_heads(do, group, tokens))
        weighed = split_heads(do.astype(F32) * o_ref[0, :, part], group, tokens)
        high = weighed.astype(BF16)
        low = (weighed - high.astype(F32)).astype(BF16)
        ones = jnp.ones((16, wide), BF16)
        deltas.append((dot_nt(ones, high) + dot_nt(ones, low))[:1])
        peaks.append(lse_ref[0, :, g * lanes : (g + 1) * lanes])
    dq_acc[...] = jnp.zeros_like(dq_acc)
    dkv_ref[...] = jnp.zeros_like(dkv_ref)

    @pl.when(place == 0)
    def _():
        dhd_ref[...] = jnp.zeros_like(dhd_ref)

    def fold(coef, grad):
        acc = coef[:, :LANES] * grad[:, :LANES]
        for c in range(LANES, hd, LANES):
            acc = acc + coef[:, c : c + LANES] * grad[:, c : c + LANES]
        return acc + pltpu.roll(acc, DH, 1)

    def times(grad, vec):
        return jnp.concatenate([grad[:, c : c + LANES] * vec for c in range(0, hd, LANES)], axis=1).astype(BF16)

    def one(b, carry):
        at = pl.ds(pl.multiple_of(b * block, block), block)
        position = b * block + lax.broadcasted_iota(jnp.int32, (block, 1), 0)
        live = position < first + tokens
        coefs = jnp.where(live, hd_ref[0, at, :].astype(F32), 0.0).astype(BF16)
        kbasis = jnp.where(live, kv_ref[0, at, :].astype(F32), 0.0)
        vbasis = jnp.where(live, kv_ref[1, at, :].astype(F32), 0.0)
        keys, ka, kb, k0, k1 = build_rows(kbasis, coefs, spread_ref[place, :, : 2 * hd], hd)
        values, va, vb, v0, v1 = build_rows(vbasis, coefs, spread_ref[place, :, 2 * hd :], hd)
        dks, dvs = [], []
        for g in range(groups):
            part = slice(g * wide, (g + 1) * wide)
            raw = dot_nt(keys[:, part], queries[g])
            p = jnp.where(position <= limit, jnp.exp(raw - peaks[g]), 0.0)
            dp = dot_nt(values[:, part], grads[g])
            ds = (p * (dp - deltas[g])).astype(BF16)
            dvs.append(dot(p.astype(BF16), grads[g]))
            dks.append(dot(ds, queries[g]))
            dq_acc[g] += dot_tn(ds, keys[:, part])
        dk = jnp.concatenate(dks, axis=1)
        dv = jnp.concatenate(dvs, axis=1)
        low = lane_of((block, LANES)) < DH
        dkv_ref[0, at, :] = jnp.where(low, fold(ka, dk), fold(kb, dk)).astype(BF16)
        dkv_ref[1, at, :] = jnp.where(low, fold(va, dv), fold(vb, dv)).astype(BF16)
        prods = jnp.concatenate([times(dk, k0), times(dk, k1), times(dv, v0), times(dv, v1)], axis=1)
        dcoef = dot_nt(prods, spread_ref[place])
        dhd_ref[0, at, :] = (dhd_ref[0, at, :].astype(F32) + dcoef).astype(BF16)
        return carry

    lax.fori_loop(0, blocks, one, 0)
    for g in range(groups):
        dq_ref[0, :, g * wide : (g + 1) * wide] = join_heads(dq_acc[g], group, tokens) * (1.0 / math.sqrt(DH))


def attend_back(info, q, kv, spread, o, do, lse, pack_rows, group, block):
    rows, tokens, hd = q.shape
    length = kv.shape[1]
    n_lanes = hd // DH * tokens
    packs = rows // pack_rows

    def place(r, i):
        return (lax.rem(r + i[rows], rows), 0, 0)

    def own(r, i):
        return (r, 0, 0)

    grid_spec = pltpu.PrefetchScalarGridSpec(
        num_scalar_prefetch=1,
        grid=(rows,),
        in_specs=[
            pl.BlockSpec((1, tokens, hd), own),
            pl.BlockSpec((2, length, LANES), place),
            pl.BlockSpec((1, length, LANES), lambda r, i: (2 * rows + r // pack_rows, 0, 0)),
            pl.BlockSpec(spread.shape, lambda r, i: (0, 0, 0)),
            pl.BlockSpec((1, tokens, hd), own),
            pl.BlockSpec((1, tokens, hd), own),
            pl.BlockSpec((1, 1, n_lanes), own),
        ],
        out_specs=[
            pl.BlockSpec((1, tokens, hd), own),
            pl.BlockSpec((2, length, LANES), place),
            pl.BlockSpec((1, length, LANES), lambda r, i: (r // pack_rows, 0, 0)),
        ],
        scratch_shapes=[pltpu.VMEM((hd // (group * DH), group * tokens, group * DH), F32)],
    )
    return pl.pallas_call(
        functools.partial(attend_back_kernel, pack_rows, group, block),
        grid_spec=grid_spec,
        out_shape=[
            jax.ShapeDtypeStruct((rows, tokens, hd), F32),
            jax.ShapeDtypeStruct((2 * rows, length, LANES), BF16),
            jax.ShapeDtypeStruct((packs, length, LANES), BF16),
        ],
        compiler_params=pltpu.CompilerParams(vmem_limit_bytes=56 * 2**20),
        name="attend_back",
    )(info, q, kv, kv, spread, o, do, lse)


def norm_back(inputs, row_scale, gain_vec, grad_rows):
    weighted = grad_rows * gain_vec
    cubed = row_scale * row_scale * row_scale
    input_part = row_scale * weighted - inputs * cubed * jnp.mean(inputs * weighted, axis=-1, keepdims=True)
    gain_part = jnp.sum(grad_rows * inputs * row_scale, axis=(0, 1))
    return (input_part, gain_part)


def project(activations, weight):
    return jnp.einsum("rsd,de->rse", activations, weight, preferred_element_type=F32)


def back_project(grad_rows, weight):
    return jnp.einsum("rse,de->rsd", grad_rows, weight, preferred_element_type=F32)


def weight_grad(normed, grad_rows):
    return jnp.einsum("rsd,rse->de", normed, grad_rows, preferred_element_type=F32)


def head_sum(partial):
    return lax.psum(partial.astype(BF16), "head").astype(F32)


def rms_scale(tensor):
    return lax.rsqrt(jnp.mean(tensor * tensor, axis=-1, keepdims=True) + EPS)


def spread_tables(head_count, width, pack_rows):
    hd = head_count * DH
    lane = jnp.arange(LANES, dtype=jnp.int32)[None, :, None]
    row = jnp.arange(pack_rows, dtype=jnp.int32)[:, None, None]
    col = jnp.arange(4 * hd, dtype=jnp.int32)[None, None, :]
    kind, head = col // hd, col % hd // DH
    source = row * width + (kind // 2) * (head_count * RK) + head * RK + kind % 2
    spread = jnp.where(lane == source, 0.5, 0.0).astype(BF16)
    factor = jnp.arange(head_count * RQ, dtype=jnp.int32)[:, None]
    col = jnp.arange(RQ * hd, dtype=jnp.int32)[None, :]
    query = jnp.where(factor == col % hd // DH * RQ + col // hd, 1.0, 0.0).astype(BF16)
    return spread, query


def rope_tables(position):
    half = DH // 2
    frequency = jnp.exp(jnp.arange(half).astype(F32) * (-2.0 * math.log(10000.0) / DH))
    angles = position[:, None] * frequency[None, :]
    cos, sin = jnp.cos(angles), jnp.sin(angles)
    return jnp.concatenate([cos] * 4, axis=1), jnp.concatenate([-sin, sin, -sin, sin], axis=1)


def shards(
    block_input,
    seq_lengths,
    attn_gain,
    query_heads,
    query_basis,
    key_heads,
    key_basis,
    value_heads,
    value_basis,
    out_project,
    ffn_gain,
    gate_weight,
    up_weight,
    down_weight,
    out_cotangent,
):
    row_count, slot_count, model_dim = block_input.shape
    head_count = query_heads.shape[1] // RQ
    hd = head_count * DH
    length = slot_count * lax.axis_size("seq")
    first_slot = lax.axis_index("seq") * slot_count
    width = head_count * (RK + RV)
    pack_rows = max(n for n in range(1, row_count + 1) if row_count % n == 0 and n * width <= LANES)
    group = min(4, head_count)
    block = math.gcd(length, KEY_BLOCK)
    spread, query_spread = spread_tables(head_count, width, pack_rows)
    cos, sin = rope_tables((first_slot + jnp.arange(slot_count, dtype=jnp.int32)).astype(F32))
    both = jnp.concatenate([key_heads, value_heads], axis=1)
    packed = jnp.concatenate([both] * pack_rows + [jnp.zeros((model_dim, LANES - width * pack_rows), BF16)], axis=1)
    normed, aq, bq, queries, own_kv, own_heads = factors(
        block_input, attn_gain, query_heads, query_basis, key_basis, value_basis, packed, cos, sin, query_spread,
        pack_rows, width)
    inputs = block_input.astype(F32)
    scale_one = rms_scale(inputs)
    kv = lax.all_gather(jnp.concatenate([own_kv, own_heads], axis=0), "seq", axis=1, tiled=True)
    shift = jnp.zeros((), jnp.int32)
    info = jnp.stack([*[seq_lengths[r] for r in range(row_count)], shift, first_slot]).astype(jnp.int32)
    attended, mixed_flat, lse = attend(info, queries, kv, shift, spread, pack_rows, group, block)
    attn_out = head_sum(project(mixed_flat, out_project))
    middle = inputs + attn_out
    scale_two = rms_scale(middle)
    normed_two = (middle * scale_two * ffn_gain).astype(BF16)
    gate_act = project(normed_two, gate_weight)
    up_act = project(normed_two, up_weight)
    sigmoid_gate = jax.nn.sigmoid(gate_act)
    silu_gate = gate_act * sigmoid_gate
    hidden = (silu_gate * up_act).astype(BF16)
    ffn_out = head_sum(project(hidden, down_weight))
    block_output = (middle + ffn_out).astype(BF16)
    cotangent = out_cotangent.astype(F32)
    down_grad = jnp.einsum("rsf,rsd->fd", hidden, out_cotangent, preferred_element_type=F32)
    d_hidden = jnp.einsum("rsd,fd->rsf", out_cotangent, down_weight, preferred_element_type=F32)
    d_gate = (d_hidden * up_act * (sigmoid_gate * (1.0 + gate_act * (1.0 - sigmoid_gate)))).astype(BF16)
    d_up = (d_hidden * silu_gate).astype(BF16)
    gate_grad = weight_grad(normed_two, d_gate)
    up_grad = weight_grad(normed_two, d_up)
    d_normed_two = head_sum(back_project(d_gate, gate_weight) + back_project(d_up, up_weight))
    d_middle_norm, ffn_gain_part = norm_back(middle, scale_two, ffn_gain, d_normed_two)
    d_middle = cotangent + d_middle_norm
    d_branch = d_middle.astype(BF16)
    out_project_grad = jnp.einsum("rsf,rsd->fd", mixed_flat, d_branch, preferred_element_type=F32)
    d_mixed = back_project(d_branch, out_project).astype(BF16)
    d_queries, d_kv, d_heads = attend_back(info, queries, kv, spread, attended, d_mixed, lse, pack_rows, group, block)
    dq_heads, dq_basis = query_grads(d_queries, aq, bq, query_spread, cos, sin, pack_rows)
    key_grads = lax.psum_scatter(
        jnp.concatenate([d_kv, d_heads], axis=0), "seq", scatter_dimension=1, tiled=True)
    d_kv_own = key_grads[: 2 * row_count].reshape(row_count, 2, slot_count, LANES).astype(F32)
    half = DH // 2
    pairs = d_kv_own[:, 0].reshape(row_count, slot_count, 2, 2, half)
    u, w = pairs[:, :, :, 0], pairs[:, :, :, 1]
    c, s = cos[None, :, None, :half], sin[None, :, None, half:DH]
    dk_basis = jnp.stack([u * c + w * s, w * c - u * s], axis=3).reshape(row_count, slot_count, LANES).astype(BF16)
    dv_basis = d_kv_own[:, 1].astype(BF16)
    packs = row_count // pack_rows
    d_heads_own = key_grads[2 * row_count :, :, : width * pack_rows].reshape(packs, slot_count, pack_rows, width)
    d_heads_own = jnp.transpose(d_heads_own, (0, 2, 1, 3)).reshape(row_count, slot_count, width).astype(BF16)
    dk_heads, dv_heads = d_heads_own[..., : head_count * RK], d_heads_own[..., head_count * RK :]
    d_normed = head_sum(
        back_project(dq_heads, query_heads) + back_project(dq_basis, query_basis)
        + back_project(dk_heads, key_heads) + back_project(dk_basis, key_basis)
        + back_project(dv_heads, value_heads) + back_project(dv_basis, value_basis))
    d_input_norm, attn_gain_part = norm_back(inputs, scale_one, attn_gain, d_normed)
    input_grad = d_middle + d_input_norm
    head_grads = weight_grad(normed, jnp.concatenate([dq_heads, dk_heads, dv_heads], axis=-1))
    basis_grads = weight_grad(normed, jnp.concatenate([dq_basis, dk_basis, dv_basis], axis=-1))

    def seq_sum(*parts):
        return tuple(t.astype(F32) for t in lax.psum(tuple(t.astype(BF16) for t in parts), "seq"))

    gate_grad, up_grad, down_grad = seq_sum(gate_grad, up_grad, down_grad)
    out_project_grad, head_grads, attn_gain_part, ffn_gain_part = seq_sum(
        out_project_grad, head_grads, attn_gain_part, ffn_gain_part)
    basis_grads = lax.psum(basis_grads, ("seq", "head"))
    nq, nk = head_count * RQ, head_count * RK
    return (
        block_output,
        input_grad,
        attn_gain_part,
        head_grads[:, :nq],
        basis_grads[:, : RQ * DH],
        head_grads[:, nq : nq + nk],
        basis_grads[:, RQ * DH : (RQ + RK) * DH],
        head_grads[:, nq + nk :],
        basis_grads[:, (RQ + RK) * DH :],
        out_project_grad,
        ffn_gain_part,
        gate_grad,
        up_grad,
        down_grad,
    )


def solution(mesh):
    rows = P(None, "seq", None)
    columns, features = P(None, "head"), P("head", None)
    in_specs = (rows, P(), P(), columns, P(), columns, P(), columns, P(), features, P(), columns, columns, features, rows)
    out_specs = (rows, rows, P(), columns, P(), columns, P(), columns, P(), features, P(), columns, columns, features)
    return jax.shard_map(shards, mesh=mesh, in_specs=in_specs, out_specs=out_specs, check_vma=False)
```

```python
import functools
import math

import jax
import jax.numpy as jnp
from jax import lax
from jax.experimental import pallas as pl
from jax.experimental.pallas import tpu as pltpu
from jax.sharding import PartitionSpec as P

DH = 64
RQ = 6
RK = 2
RV = 2
LANES = 128
EPS = 1e-06
KEY_BLOCK = 256
F32 = jnp.float32
BF16 = jnp.bfloat16


def dot(a, b):
    return lax.dot_general(a, b, (((1,), (0,)), ((), ())), preferred_element_type=F32)


def dot_nt(a, b):
    return lax.dot_general(a, b, (((1,), (1,)), ((), ())), preferred_element_type=F32)


def dot_tn(a, b):
    return lax.dot_general(a, b, (((0,), (0,)), ((), ())), preferred_element_type=F32)


def lane_of(shape):
    return lax.broadcasted_iota(jnp.int32, shape, len(shape) - 1)


def both_halves(pair):
    swapped = pltpu.roll(pair, DH, 1)
    low = lane_of(pair.shape) < DH
    return jnp.where(low, pair, swapped), jnp.where(low, swapped, pair)


def turn(pair, cos, sin):
    half = DH // 2
    first = lane_of(pair.shape) % DH < half
    other = jnp.where(first, pltpu.roll(pair, LANES - half, 1), pltpu.roll(pair, half, 1))
    return pair * cos + other * sin


def split_heads(rows, head_rows, tokens):
    group = lane_of(rows.shape) // DH
    return jnp.concatenate([jnp.where(group == h, rows, jnp.zeros_like(rows)) for h in range(head_rows)], axis=0)


def join_heads(block, head_rows, tokens):
    out = block[:tokens]
    group = lane_of(out.shape) // DH
    for h in range(1, head_rows):
        out = jnp.where(group == h, block[h * tokens : (h + 1) * tokens], out)
    return out


def factor_kernel(width, x_ref, gain_ref, wqh_ref, wqb_ref, wkb_ref, wvb_ref, wh_ref, cos_ref, sin_ref, eq_ref,
                  xn_ref, aq_ref, bq_ref, q_ref, kv_ref, hd_ref):
    rows, tokens, model = x_ref.shape
    hd = q_ref.shape[2]
    count = rows * tokens
    x = x_ref[...].astype(F32).reshape(count, model)
    scale = lax.rsqrt(jnp.mean(x * x, axis=-1, keepdims=True) + EPS)
    xn = (x * scale * gain_ref[...]).astype(BF16)
    xn_ref[...] = xn.reshape(rows, tokens, model)
    cos = jnp.concatenate([cos_ref[...]] * rows, axis=0)
    sin = jnp.concatenate([sin_ref[...]] * rows, axis=0)
    keys = turn(dot(xn, wkb_ref[...]), cos, sin).astype(BF16)
    values = dot(xn, wvb_ref[...]).astype(BF16)
    heads = dot(xn, wh_ref[...])
    lanes = lane_of((tokens, LANES)) // width
    pack = heads[:tokens]
    for r in range(rows):
        part = slice(r * tokens, (r + 1) * tokens)
        kv_ref[2 * r] = keys[part]
        kv_ref[2 * r + 1] = values[part]
        if r:
            pack = jnp.where(lanes == r, heads[part], pack)
    hd_ref[0] = pack.astype(BF16)
    aq = dot(xn, wqh_ref[...])
    aq_ref[...] = aq.reshape(rows, tokens, aq.shape[1])
    aq_high = aq.astype(BF16)
    aq_low = (aq - aq_high.astype(F32)).astype(BF16)
    basis = dot(xn, wqb_ref[...])
    total = [jnp.zeros((count, LANES), F32) for _ in range(hd // LANES)]
    for p in range(RQ // 2):
        pair = turn(basis[:, p * LANES : (p + 1) * LANES], cos, sin)
        bq_ref[:, :, p * LANES : (p + 1) * LANES] = pair.reshape(rows, tokens, LANES)
        for half, vec in enumerate(both_halves(pair)):
            spread = eq_ref[:, (2 * p + half) * hd : (2 * p + half + 1) * hd]
            coef = dot(aq_high, spread) + dot(aq_low, spread)
            for c in range(hd // LANES):
                total[c] = total[c] + coef[:, c * LANES : (c + 1) * LANES] * vec
    for c in range(hd // LANES):
        low = (total[c] / RQ).astype(BF16).astype(F32) * (1.0 / math.sqrt(DH))
        q_ref[:, :, c * LANES : (c + 1) * LANES] = low.astype(BF16).reshape(rows, tokens, LANES)


def whole(*shape):
    return pl.BlockSpec(shape, lambda *_: (0,) * len(shape))


def factors(x, gain, wqh, wqb, wkb, wvb, wh, cos, sin, eq, pack_rows, width):
    rows, tokens, model = x.shape
    hd = eq.shape[1] // RQ
    packs = rows // pack_rows
    nq = wqh.shape[1]

    def row_block(last):
        return pl.BlockSpec((pack_rows, tokens, last), lambda g: (g, 0, 0))

    return pl.pallas_call(
        functools.partial(factor_kernel, width),
        grid=(packs,),
        in_specs=[row_block(model), whole(1, model), whole(*wqh.shape), whole(*wqb.shape), whole(*wkb.shape),
                  whole(*wvb.shape), whole(*wh.shape), whole(*cos.shape), whole(*sin.shape), whole(*eq.shape)],
        out_specs=[row_block(model), row_block(nq), row_block(RQ * DH), row_block(hd),
                   pl.BlockSpec((2 * pack_rows, tokens, LANES), lambda g: (g, 0, 0)),
                   pl.BlockSpec((1, tokens, LANES), lambda g: (g, 0, 0))],
        out_shape=[
            jax.ShapeDtypeStruct((rows, tokens, model), BF16),
            jax.ShapeDtypeStruct((rows, tokens, nq), F32),
            jax.ShapeDtypeStruct((rows, tokens, RQ * DH), F32),
            jax.ShapeDtypeStruct((rows, tokens, hd), BF16),
            jax.ShapeDtypeStruct((2 * rows, tokens, LANES), BF16),
            jax.ShapeDtypeStruct((packs, tokens, LANES), BF16),
        ],
        compiler_params=pltpu.CompilerParams(vmem_limit_bytes=56 * 2**20),
        name="factors",
    )(x, gain.reshape(1, model), wqh, wqb, wkb, wvb, wh, cos, sin, eq)


def query_grad_kernel(dq_ref, aq_ref, bq_ref, eq_ref, cos_ref, sin_ref, da_ref, db_ref):
    rows, tokens, hd = dq_ref.shape
    count = rows * tokens
    dq = dq_ref[...].reshape(count, hd)
    aq = aq_ref[...].reshape(count, aq_ref.shape[2])
    aq_high = aq.astype(BF16)
    aq_low = (aq - aq_high.astype(F32)).astype(BF16)
    cos = jnp.concatenate([cos_ref[...]] * rows, axis=0)
    sin = jnp.concatenate([sin_ref[...]] * rows, axis=0)
    da = jnp.zeros(aq.shape, F32)
    low = lane_of((count, LANES)) < DH
    for p in range(RQ // 2):
        pair = bq_ref[:, :, p * LANES : (p + 1) * LANES].reshape(count, LANES)
        sums = []
        for half, vec in enumerate(both_halves(pair)):
            spread = eq_ref[:, (2 * p + half) * hd : (2 * p + half + 1) * hd]
            coef = dot(aq_high, spread) + dot(aq_low, spread)
            acc = jnp.zeros((count, LANES), F32)
            prods = []
            for c in range(hd // LANES):
                part = dq[:, c * LANES : (c + 1) * LANES]
                acc = acc + coef[:, c * LANES : (c + 1) * LANES] * part
                prods.append(part * vec)
            prod = jnp.concatenate(prods, axis=1)
            high = prod.astype(BF16)
            rest = (prod - high.astype(F32)).astype(BF16)
            da = da + dot_nt(high, spread) + dot_nt(rest, spread)
            sums.append(acc + pltpu.roll(acc, DH, 1))
        turned = turn(jnp.where(low, sums[0], sums[1]), cos, -sin) * (1.0 / RQ)
        db_ref[:, :, p * LANES : (p + 1) * LANES] = turned.astype(BF16).reshape(rows, tokens, LANES)
    da_ref[...] = (da * (1.0 / RQ)).astype(BF16).reshape(da_ref.shape)


def query_grads(dq, aq, bq, eq, cos, sin, pack_rows):
    rows, tokens, hd = dq.shape
    nq = aq.shape[2]

    def row_block(last):
        return pl.BlockSpec((pack_rows, tokens, last), lambda g: (g, 0, 0))

    return pl.pallas_call(
        query_grad_kernel,
        grid=(rows // pack_rows,),
        in_specs=[row_block(hd), row_block(nq), row_block(RQ * DH), whole(*eq.shape), whole(*cos.shape), whole(*sin.shape)],
        out_specs=[row_block(nq), row_block(RQ * DH)],
        out_shape=[jax.ShapeDtypeStruct((rows, tokens, nq), BF16), jax.ShapeDtypeStruct((rows, tokens, RQ * DH), BF16)],
        compiler_params=pltpu.CompilerParams(vmem_limit_bytes=56 * 2**20),
        name="query_grads",
    )(dq, aq, bq, eq, cos, sin)


def build_rows(basis, coefs, spread, hd):
    first, second = both_halves(basis.astype(F32))
    coef = dot(coefs, spread)
    one, two = coef[:, :hd], coef[:, hd:]
    cols = [one[:, c : c + LANES] * first + two[:, c : c + LANES] * second for c in range(0, hd, LANES)]
    return jnp.concatenate(cols, axis=1).astype(BF16), one, two, first, second


def row_limits(info_ref, row, tokens, block):
    first = info_ref[info_ref.shape[0] - 1]
    length = info_ref[row]
    used = jnp.minimum(length, first + tokens)
    return first, length, (used + block - 1) // block


def limit_lanes(first, length, tokens, lanes):
    slot = lax.broadcasted_iota(jnp.int32, (1, lanes), 1) % tokens
    return jnp.minimum(first + slot, length - 1)


def attend_kernel(pack_rows, group, block, info_ref, q_ref, kv_ref, hd_ref, spread_ref, o_ref, ob_ref, lse_ref, s_ref, v_ref):
    row = pl.program_id(0)
    _, tokens, hd = q_ref.shape
    lanes = group * tokens
    wide = group * DH
    groups = hd // wide
    first, length, blocks = row_limits(info_ref, row, tokens, block)
    limit = limit_lanes(first, length, tokens, lanes)
    queries = [split_heads(q_ref[0, :, g * wide : (g + 1) * wide], group, tokens) for g in range(groups)]
    place = row % pack_rows

    def scores(b, peaks):
        at = pl.ds(pl.multiple_of(b * block, block), block)
        coefs = hd_ref[0, at, :]
        keys, *_ = build_rows(kv_ref[0, at, :], coefs, spread_ref[place, :, : 2 * hd], hd)
        values, *_ = build_rows(kv_ref[1, at, :], coefs, spread_ref[place, :, 2 * hd :], hd)
        position = b * block + lax.broadcasted_iota(jnp.int32, (block, 1), 0)
        live = position < first + tokens
        v_ref[at, :] = jnp.where(live, values.astype(F32), 0.0).astype(BF16)
        out = []
        for g in range(groups):
            raw = dot_nt(keys[:, g * wide : (g + 1) * wide], queries[g])
            raw = jnp.where(position <= limit, raw, -1e30)
            s_ref[at, g * lanes : (g + 1) * lanes] = raw
            out.append(jnp.maximum(peaks[g], jnp.max(raw, axis=0, keepdims=True)))
        return tuple(out)

    peaks = lax.fori_loop(0, blocks, scores, tuple(jnp.full((1, lanes), -1e30, F32) for _ in range(groups)))

    def exps(b, totals):
        at = pl.ds(pl.multiple_of(b * block, block), block)
        out = []
        for g in range(groups):
            part = slice(g * lanes, (g + 1) * lanes)
            e = jnp.exp(s_ref[at, part] - peaks[g])
            s_ref[at, part] = e
            out.append(totals[g] + jnp.sum(e, axis=0, keepdims=True))
        return tuple(out)

    totals = lax.fori_loop(0, blocks, exps, tuple(jnp.zeros((1, lanes), F32) for _ in range(groups)))
    shares = [1.0 / t for t in totals]

    def mix(b, outs):
        at = pl.ds(pl.multiple_of(b * block, block), block)
        res = []
        for g in range(groups):
            p = (s_ref[at, g * lanes : (g + 1) * lanes] * shares[g]).astype(BF16)
            res.append(outs[g] + dot_tn(p, v_ref[at, g * wide : (g + 1) * wide]))
        return tuple(res)

    outs = lax.fori_loop(0, blocks, mix, tuple(jnp.zeros((lanes, wide), F32) for _ in range(groups)))
    for g in range(groups):
        mixed = join_heads(outs[g], group, tokens)
        o_ref[0, :, g * wide : (g + 1) * wide] = mixed
        ob_ref[0, :, g * wide : (g + 1) * wide] = mixed.astype(BF16)
        lse_ref[0, :, g * lanes : (g + 1) * lanes] = peaks[g] + jnp.log(totals[g])


def attend(info, q, kv, shift, spread, pack_rows, group, block):
    rows, tokens, hd = q.shape
    length = kv.shape[1]
    n_lanes = hd // DH * tokens
    grid_spec = pltpu.PrefetchScalarGridSpec(
        num_scalar_prefetch=1,
        grid=(rows,),
        in_specs=[
            pl.BlockSpec((1, tokens, hd), lambda r, i: (r, 0, 0)),
            pl.BlockSpec((2, length, LANES), lambda r, i: (lax.rem(r + i[rows], rows), 0, 0)),
            pl.BlockSpec((1, length, LANES), lambda r, i: (2 * rows + r // pack_rows, 0, 0)),
            pl.BlockSpec(spread.shape, lambda r, i: (0, 0, 0)),
        ],
        out_specs=[
            pl.BlockSpec((1, tokens, hd), lambda r, i: (r, 0, 0)),
            pl.BlockSpec((1, tokens, hd), lambda r, i: (r, 0, 0)),
            pl.BlockSpec((1, 1, n_lanes), lambda r, i: (r, 0, 0)),
        ],
        scratch_shapes=[pltpu.VMEM((length, n_lanes), F32), pltpu.VMEM((length, hd), BF16)],
    )
    return pl.pallas_call(
        functools.partial(attend_kernel, pack_rows, group, block),
        grid_spec=grid_spec,
        out_shape=[
            jax.ShapeDtypeStruct((rows, tokens, hd), F32),
            jax.ShapeDtypeStruct((rows, tokens, hd), BF16),
            jax.ShapeDtypeStruct((rows, 1, n_lanes), F32),
        ],
        compiler_params=pltpu.CompilerParams(vmem_limit_bytes=56 * 2**20),
        name="attend",
    )(info, q, kv, kv, spread)


def attend_back_kernel(pack_rows, group, block, info_ref, q_ref, kv_ref, hd_ref, spread_ref, o_ref, do_ref, lse_ref,
                       dq_ref, dkv_ref, dhd_ref, dq_acc):
    row = pl.program_id(0)
    _, tokens, hd = q_ref.shape
    lanes = group * tokens
    wide = group * DH
    groups = hd // wide
    first, length, blocks = row_limits(info_ref, row, tokens, block)
    limit = limit_lanes(first, length, tokens, lanes)
    place = row % pack_rows
    queries, grads, deltas, peaks = [], [], [], []
    for g in range(groups):
        part = slice(g * wide, (g + 1) * wide)
        do = do_ref[0, :, part]
        queries.append(split_heads(q_ref[0, :, part], group, tokens))
        grads.append(split_heads(do, group, tokens))
        weighed = split_heads(do.astype(F32) * o_ref[0, :, part], group, tokens)
        high = weighed.astype(BF16)
        low = (weighed - high.astype(F32)).astype(BF16)
        ones = jnp.ones((16, wide), BF16)
        deltas.append((dot_nt(ones, high) + dot_nt(ones, low))[:1])
        peaks.append(lse_ref[0, :, g * lanes : (g + 1) * lanes])
    dq_acc[...] = jnp.zeros_like(dq_acc)
    dkv_ref[...] = jnp.zeros_like(dkv_ref)

    @pl.when(place == 0)
    def _():
        dhd_ref[...] = jnp.zeros_like(dhd_ref)

    def fold(coef, grad):
        acc = coef[:, :LANES] * grad[:, :LANES]
        for c in range(LANES, hd, LANES):
            acc = acc + coef[:, c : c + LANES] * grad[:, c : c + LANES]
        return acc + pltpu.roll(acc, DH, 1)

    def times(grad, vec):
        return jnp.concatenate([grad[:, c : c + LANES] * vec for c in range(0, hd, LANES)], axis=1).astype(BF16)

    def one(b, carry):
        at = pl.ds(pl.multiple_of(b * block, block), block)
        position = b * block + lax.broadcasted_iota(jnp.int32, (block, 1), 0)
        live = position < first + tokens
        coefs = jnp.where(live, hd_ref[0, at, :].astype(F32), 0.0).astype(BF16)
        kbasis = jnp.where(live, kv_ref[0, at, :].astype(F32), 0.0)
        vbasis = jnp.where(live, kv_ref[1, at, :].astype(F32), 0.0)
        keys, ka, kb, k0, k1 = build_rows(kbasis, coefs, spread_ref[place, :, : 2 * hd], hd)
        values, va, vb, v0, v1 = build_rows(vbasis, coefs, spread_ref[place, :, 2 * hd :], hd)
        dks, dvs = [], []
        for g in range(groups):
            part = slice(g * wide, (g + 1) * wide)
            raw = dot_nt(keys[:, part], queries[g])
            p = jnp.where(position <= limit, jnp.exp(raw - peaks[g]), 0.0)
            dp = dot_nt(values[:, part], grads[g])
            ds = (p * (dp - deltas[g])).astype(BF16)
            dvs.append(dot(p.astype(BF16), grads[g]))
            dks.append(dot(ds, queries[g]))
            dq_acc[g] += dot_tn(ds, keys[:, part])
        dk = jnp.concatenate(dks, axis=1)
        dv = jnp.concatenate(dvs, axis=1)
        low = lane_of((block, LANES)) < DH
        dkv_ref[0, at, :] = jnp.where(low, fold(ka, dk), fold(kb, dk)).astype(BF16)
        dkv_ref[1, at, :] = jnp.where(low, fold(va, dv), fold(vb, dv)).astype(BF16)
        prods = jnp.concatenate([times(dk, k0), times(dk, k1), times(dv, v0), times(dv, v1)], axis=1)
        dcoef = dot_nt(prods, spread_ref[place])
        dhd_ref[0, at, :] = (dhd_ref[0, at, :].astype(F32) + dcoef).astype(BF16)
        return carry

    lax.fori_loop(0, blocks, one, 0)
    for g in range(groups):
        dq_ref[0, :, g * wide : (g + 1) * wide] = join_heads(dq_acc[g], group, tokens) * (1.0 / math.sqrt(DH))


def attend_back(info, q, kv, spread, o, do, lse, pack_rows, group, block):
    rows, tokens, hd = q.shape
    length = kv.shape[1]
    n_lanes = hd // DH * tokens
    packs = rows // pack_rows

    def place(r, i):
        return (lax.rem(r + i[rows], rows), 0, 0)

    def own(r, i):
        return (r, 0, 0)

    grid_spec = pltpu.PrefetchScalarGridSpec(
        num_scalar_prefetch=1,
        grid=(rows,),
        in_specs=[
            pl.BlockSpec((1, tokens, hd), own),
            pl.BlockSpec((2, length, LANES), place),
            pl.BlockSpec((1, length, LANES), lambda r, i: (2 * rows + r // pack_rows, 0, 0)),
            pl.BlockSpec(spread.shape, lambda r, i: (0, 0, 0)),
            pl.BlockSpec((1, tokens, hd), own),
            pl.BlockSpec((1, tokens, hd), own),
            pl.BlockSpec((1, 1, n_lanes), own),
        ],
        out_specs=[
            pl.BlockSpec((1, tokens, hd), own),
            pl.BlockSpec((2, length, LANES), place),
            pl.BlockSpec((1, length, LANES), lambda r, i: (r // pack_rows, 0, 0)),
        ],
        scratch_shapes=[pltpu.VMEM((hd // (group * DH), group * tokens, group * DH), F32)],
    )
    return pl.pallas_call(
        functools.partial(attend_back_kernel, pack_rows, group, block),
        grid_spec=grid_spec,
        out_shape=[
            jax.ShapeDtypeStruct((rows, tokens, hd), F32),
            jax.ShapeDtypeStruct((2 * rows, length, LANES), BF16),
            jax.ShapeDtypeStruct((packs, length, LANES), BF16),
        ],
        compiler_params=pltpu.CompilerParams(vmem_limit_bytes=56 * 2**20),
        name="attend_back",
    )(info, q, kv, kv, spread, o, do, lse)


MESH = pl.DeviceIdType.MESH
SIZES = {"z": 4, "y": 2, "x": 2}
STRIDES = {"z": 4, "y": 2, "x": 1}
CORES = 2


def on_known_slice():
    return lax.axis_size("seq") == math.prod(SIZES.values()) and lax.axis_size("head") == CORES


class Links:
    def __init__(self, send_sems, recv_sems):
        self.seq = lax.axis_index("seq")
        self.core = lax.axis_index("head")
        self.at = {d: lax.rem(self.seq // STRIDES[d], SIZES[d]) for d in SIZES}
        self.send_sems, self.recv_sems = send_sems, recv_sems
        self.count = 0
        self.started = []

    def along(self, d, offset):
        there = lax.rem(self.at[d] + offset, SIZES[d])
        return there, (self.seq + (there - self.at[d]) * STRIDES[d], self.core)

    def other_core(self):
        return (self.seq, 1 - self.core)

    def greet(self, core, chips=True):
        barrier = pltpu.get_barrier_semaphore()
        devices = [self.other_core()] if core else []
        if chips:
            devices += [self.along(d, o)[1] for d in SIZES for o in range(1, SIZES[d])]
        for device in devices:
            pl.semaphore_signal(barrier, inc=1, device_id=device, device_id_type=MESH)
        pl.semaphore_wait(barrier, len(devices))

    def send(self, src, dst, device):
        copy = pltpu.make_async_remote_copy(
            src_ref=src, dst_ref=dst, send_sem=self.send_sems.at[self.count], recv_sem=self.recv_sems.at[self.count],
            device_id=device, device_id_type=MESH)
        self.count += 1
        copy.start()
        self.started.append(copy)
        return copy

    def finish(self):
        for copy in self.started:
            copy.wait_send()


def accumulate(acc, slots):
    lead = acc.shape[:-2]

    def body(i, carry):
        at = []
        for size in reversed(lead):
            at.insert(0, lax.rem(i, size))
            i = i // size
        value = acc[(*at, slice(None), slice(None))].astype(F32)
        for o in range(slots.shape[0]):
            value = value + slots[(o, *at, slice(None), slice(None))].astype(F32)
        acc[(*at, slice(None), slice(None))] = value.astype(BF16)
        return carry

    lax.fori_loop(0, math.prod(lead), body, 0)


def scatter_steps(links, order, source, acc, slots, ready):
    fixed = {}
    for k, d in enumerate(order):
        copies = []
        for o in range(1, SIZES[d]):
            there, device = links.along(d, o)
            view = source if k == 0 else acc
            copies.append(links.send(view({**fixed, d: there}), slots[k].at[o - 1], device))
        yield
        if k == 0:
            ready()
        for copy in copies:
            copy.wait_recv()
        fixed[d] = links.at[d]
        accumulate(acc(fixed), slots[k])


def gather_steps(links, order, out, first):
    for k in reversed(range(len(order))):
        fixed = {d: links.at[d] for d in order[: k + 1]}
        copies = []
        for o in range(1, SIZES[order[k]]):
            _, device = links.along(order[k], o)
            src = first if first is not None and k == len(order) - 1 else out(fixed)
            copies.append(links.send(src, out(fixed), device))
        yield
        for copy in copies:
            copy.wait_recv()


def run_waves(groups):
    live, waiting = [], list(groups)
    while live or waiting:
        if waiting:
            live.append(list(waiting.pop(0)))
        for group in live:
            group[:] = [job for job in group if next(job, "end") != "end"]
        live = [group for group in live if group]


def slot_shapes(order, units, tail):
    shapes, open_dims = [], list(SIZES)
    for d in order:
        open_dims.remove(d)
        shapes.append((SIZES[d] - 1, *units, *[SIZES[e] for e in open_dims], *tail))
    return shapes


def pick(ref, lead, sel, axes, tail=()):
    return ref.at[(*lead, *[sel.get(d, slice(None)) for d in axes], *tail)]


ZYX = ("z", "y", "x")


def collect_jobs(rows, packs):
    step = 4
    own = [(rows + u, min(step, rows - u)) for u in range(0, rows, step)]
    jobs = own + [(2 * rows, packs)]
    half = (len(jobs) + 1) // 2
    return [(first, n, ("y", "x", "z") if i < half else ("x", "y", "z")) for i, (first, n) in enumerate(jobs)]


def collect_kernel(rows, packs, kv_ref, hd_ref, out_ref, local_sems, send_sems, recv_sems):
    links = Links(send_sems, recv_sems)
    links.greet(core=True)
    own = tuple(links.at[d] for d in ZYX)
    locals_ = []
    jobs = collect_jobs(rows, packs)
    for i, (first, n, _) in enumerate(jobs):
        src = hd_ref if first == 2 * rows else kv_ref.at[pl.ds(links.core * rows + first - rows, n)]
        copy = pltpu.make_async_copy(src, out_ref.at[(pl.ds(first, n), *own)], local_sems.at[i])
        copy.start()
        locals_.append(copy)

    def job(i, first, n, order):
        locals_[i].wait()
        yield from gather_steps(links, order, lambda sel: pick(out_ref, [pl.ds(first, n)], sel, ZYX), None)
        if first < 2 * rows:
            copy = links.send(out_ref.at[pl.ds(first, n)], out_ref.at[pl.ds(first - rows, n)], links.other_core())
            yield
            copy.wait_recv()

    made = [job(i, *j) for i, j in enumerate(jobs)]
    half = (len(made) + 1) // 2
    run_waves(list(zip(made[:half], made[half:])))
    links.finish()


def collect(kv, hd):
    units, tokens, _ = kv.shape
    packs = hd.shape[0]
    rows = units // 2
    copies = 8 * len(collect_jobs(rows, packs))
    out = pl.pallas_call(
        functools.partial(collect_kernel, rows, packs),
        out_shape=jax.ShapeDtypeStruct((units + packs, *[SIZES[d] for d in ZYX], tokens, LANES), BF16),
        in_specs=[pl.BlockSpec(memory_space=pl.ANY)] * 2,
        out_specs=pl.BlockSpec(memory_space=pl.ANY),
        scratch_shapes=[pltpu.SemaphoreType.DMA((8,)), pltpu.SemaphoreType.DMA((copies,)), pltpu.SemaphoreType.DMA((copies,))],
        compiler_params=pltpu.CompilerParams(collective_id=1, has_side_effects=True),
        name="collect",
    )(kv, hd)
    return out.reshape(units + packs, -1, LANES)


def return_kernel(rows, packs, dkv_ref, dhd_ref, out_ref, acc_ref, core_ref, *rest):
    jobs = collect_jobs(rows, packs)
    slot_refs, (local_sems, send_sems, recv_sems) = rest[: 3 * len(jobs)], rest[3 * len(jobs) :]
    links = Links(send_sems, recv_sems)
    links.greet(core=True)
    own = tuple(links.at[d] for d in ZYX)
    loads, swaps = [], []
    for i, (first, n, _) in enumerate(jobs):
        heads = first == 2 * rows
        part = pl.ds(first - rows, n)
        if not heads:
            swaps.append(links.send(dkv_ref.at[part], core_ref.at[part], links.other_core()))
        load = pltpu.make_async_copy(dhd_ref if heads else dkv_ref.at[pl.ds(first, n)], acc_ref.at[part], local_sems.at[i])
        load.start()
        loads.append(load)
    out_ref[...] = jnp.zeros_like(out_ref)

    def job(i, first, n, order):
        heads = first == 2 * rows
        part = pl.ds(first - rows, n)
        loads[i].wait()
        if not heads:
            swaps[i].wait_recv()

            def add(j, carry):
                u = first - rows + j // SIZES["z"]
                z = lax.rem(j, SIZES["z"])
                acc_ref[u, z] = (acc_ref[u, z].astype(F32) + core_ref[u, z].astype(F32)).astype(BF16)
                return carry

            lax.fori_loop(0, n * SIZES["z"], add, 0)

        def view(sel):
            return pick(acc_ref, [part], sel, ZYX)

        yield from scatter_steps(links, order, view, view, slot_refs[3 * i : 3 * i + 3], lambda: None)
        for u in range(n):
            at = 2 * rows + u if heads else links.core * rows + first - rows + u
            out_ref[at] = acc_ref[(first - rows + u, *own)]

    made = [job(i, *j) for i, j in enumerate(jobs)]
    half = (len(made) + 1) // 2
    run_waves(list(zip(made[:half], made[half:])))
    links.finish()


def give_back(dkv, dhd):
    units, length, _ = dkv.shape
    packs = dhd.shape[0]
    rows = units // 2
    tokens = length // math.prod(SIZES.values())
    dims = tuple(SIZES[d] for d in ZYX)
    jobs = collect_jobs(rows, packs)
    slots = [pltpu.VMEM(shape, BF16) for _, n, order in jobs for shape in slot_shapes(order, (n,), (tokens, LANES))]
    copies = 8 * len(jobs)
    return pl.pallas_call(
        functools.partial(return_kernel, rows, packs),
        out_shape=jax.ShapeDtypeStruct((units + packs, tokens, LANES), BF16),
        in_specs=[pl.BlockSpec(memory_space=pl.ANY)] * 2,
        out_specs=pl.BlockSpec(memory_space=pltpu.VMEM),
        scratch_shapes=[pltpu.VMEM((rows + packs, *dims, tokens, LANES), BF16), pltpu.VMEM((rows, *dims, tokens, LANES), BF16),
                        *slots, pltpu.SemaphoreType.DMA((8,)), pltpu.SemaphoreType.DMA((copies,)), pltpu.SemaphoreType.DMA((copies,))],
        compiler_params=pltpu.CompilerParams(collective_id=2, has_side_effects=True, vmem_limit_bytes=48 * 2**20),
        name="give_back",
    )(dkv.reshape(units, *dims, tokens, LANES), dhd.reshape(packs, *dims, tokens, LANES))


def pair_kernel(x_ref, out_ref, got_ref, send_sems, recv_sems):
    links = Links(send_sems, recv_sems)
    links.greet(core=True, chips=False)
    copies = [links.send(x_ref.at[r], got_ref.at[r], links.other_core()) for r in range(x_ref.shape[0])]
    for r, copy in enumerate(copies):
        copy.wait_recv()
        out_ref[r] = (x_ref[r].astype(F32) + got_ref[r].astype(F32)).astype(out_ref.dtype)
    links.finish()


def pair_sum(x, ident):
    parts = 4
    rows, tokens, model = x.shape
    flat = x.reshape(parts, rows * tokens // parts, model)
    return pl.pallas_call(
        pair_kernel,
        out_shape=jax.ShapeDtypeStruct(flat.shape, BF16),
        in_specs=[pl.BlockSpec(memory_space=pltpu.VMEM)],
        out_specs=pl.BlockSpec(memory_space=pltpu.VMEM),
        scratch_shapes=[pltpu.VMEM(flat.shape, BF16), pltpu.SemaphoreType.DMA((parts,)), pltpu.SemaphoreType.DMA((parts,))],
        compiler_params=pltpu.CompilerParams(collective_id=ident, has_side_effects=True, vmem_limit_bytes=32 * 2**20),
        name="pair_sum_%d" % ident,
    )(flat).reshape(x.shape)


class Cut:
    def __init__(self, array, axes, rows, cols, order, lane_dim=None, shared=False):
        self.array, self.axes, self.rows, self.cols = array, axes, rows, cols
        self.order, self.lane_dim, self.shared = order, lane_dim, shared

    def tail(self):
        return (self.rows[1], self.cols[1])

    def view(self, ref, sel, core):
        cols = pl.ds(self.cols[0], self.cols[1])
        if self.lane_dim is not None:
            cols = pl.ds(pl.multiple_of(self.cols[0] + sel[self.lane_dim] * self.cols[1], LANES), self.cols[1])
        lead = [core] if self.shared else []
        return pick(ref, lead, sel, self.axes, (pl.ds(self.rows[0], self.rows[1]), cols))

    def inner(self):
        return tuple(d for d in self.axes if d != self.order[0])

    def acc_shape(self):
        return (*[SIZES[d] for d in self.inner()], *self.tail())

    def slots(self):
        shapes, open_dims = [], list(self.inner())
        for d in self.order:
            if d in open_dims:
                open_dims.remove(d)
            shapes.append((SIZES[d] - 1, *[SIZES[e] for e in open_dims], *self.tail()))
        return shapes


def weight_cuts(shapes):
    a, b, c, d = ("x", "y", "z"), ("y", "x", "z"), ("x", "z", "y"), ("y", "z", "x")
    groups = []
    gate_rows, gate_cols = shapes[0][3:]
    parts = 2
    for i in range(parts):
        rows = (i * gate_rows // parts, gate_rows // parts)
        groups.append([Cut(0, ("x", "y", "z"), rows, (0, gate_cols), a), Cut(1, ("x", "y", "z"), rows, (0, gate_cols), b)])
    down_rows, down_cols = shapes[2][2:]
    groups.append([Cut(2, ("y", "z"), (0, down_rows), (0, down_cols // 4), c, lane_dim="x"),
                   Cut(2, ("x", "z"), (0, down_rows), (down_cols // 2, down_cols // 4), d, lane_dim="y")])
    out_rows, out_cols = shapes[3][3:]
    basis_rows, basis_cols = shapes[4][4:]
    head_rows, head_cols = shapes[5][3:]
    axes = ("x", "y", "z")
    cut = basis_cols // LANES // 2 * LANES
    groups.append([Cut(3, axes, (0, out_rows), (0, out_cols // 2), a),
                   Cut(3, axes, (0, out_rows), (out_cols // 2, out_cols // 2), b),
                   Cut(4, axes, (0, basis_rows), (0, cut), a, shared=True),
                   Cut(4, axes, (0, basis_rows), (cut, basis_cols - cut), b, shared=True),
                   Cut(5, axes, (0, head_rows), (0, head_cols), a)])
    return groups


def weight_kernel(groups, count, *refs):
    jobs = [cut for group in groups for cut in group]
    ins, outs = refs[:count], refs[count : 2 * count]
    at = 2 * count
    accs = refs[at : at + len(jobs)]
    at += len(jobs)
    slots = refs[at : at + 3 * len(jobs)]
    at += 3 * len(jobs)
    shared_own, shared_got, local_sems, send_sems, recv_sems = refs[at:]
    links = Links(send_sems, recv_sems)
    links.greet(core=True)
    loads = []
    for i, cut in enumerate(jobs):
        if cut.shared:
            loads.append(None)
            continue
        load = pltpu.make_async_copy(cut.view(ins[cut.array], {cut.order[0]: links.at[cut.order[0]]}, links.core), accs[i],
                                     local_sems.at[i])
        load.start()
        loads.append(load)
    basis = next(cut.array for cut in jobs if cut.shared)
    own = pltpu.make_async_copy(ins[basis].at[links.core], shared_own, local_sems.at[len(jobs)])
    own.start()
    swap = links.send(ins[basis].at[1 - links.core], shared_got, links.other_core())
    stores = []

    def job(i, cut):
        def acc(sel):
            return pick(accs[i], [], sel, cut.inner())

        def source(sel):
            return cut.view(ins[cut.array], sel, links.core)

        ready = loads[i].wait if loads[i] is not None else lambda: None
        if cut.shared:
            summed = pick(shared_own, [], {cut.order[0]: links.at[cut.order[0]]}, cut.axes,
                          (slice(None), pl.ds(cut.cols[0], cut.cols[1])))

            def keep(j, carry):
                p, q = j // accs[i].shape[1], lax.rem(j, accs[i].shape[1])
                accs[i][p, q] = summed[p, q]
                return carry

            lax.fori_loop(0, accs[i].shape[0] * accs[i].shape[1], keep, 0)

            def source(sel):
                return pick(shared_own, [], sel, cut.axes, (slice(None), pl.ds(cut.cols[0], cut.cols[1])))

        yield from scatter_steps(links, cut.order, source, acc, slots[3 * i : 3 * i + 3], ready)
        piece = acc({d: links.at[d] for d in cut.inner()})

        def out(sel):
            return cut.view(outs[cut.array], sel, links.core)

        store = pltpu.make_async_copy(piece, out(links.at), local_sems.at[len(jobs) + 1 + i])
        store.start()
        steps = gather_steps(links, cut.order, out, piece)
        next(steps)
        yield
        store.wait()
        yield from steps

    def first_shared():
        own.wait()
        swap.wait_recv()

        def add(j, carry):
            shape = shared_own.shape
            p, q, r = j // (shape[1] * shape[2]), lax.rem(j // shape[2], shape[1]), lax.rem(j, shape[2])
            shared_own[p, q, r] = (shared_own[p, q, r].astype(F32) + shared_got[p, q, r].astype(F32)).astype(BF16)
            return carry

        lax.fori_loop(0, math.prod(shared_own.shape[:3]), add, 0)
        return
        yield

    made, i = [], 0
    for group in groups:
        lot = []
        if any(cut.shared for cut in group):
            lot.append(first_shared())
        for cut in group:
            lot.append(job(i, cut))
            i += 1
        made.append(lot)
    run_waves(made)
    last = links.send(outs[basis].at[links.core], outs[basis].at[links.core], links.other_core())
    last.wait_recv()
    links.finish()


def weight_sums(gate, up, down, out_proj, basis, heads):
    dims = tuple(SIZES[d] for d in ("x", "y", "z"))

    def pieces(w):
        return w.reshape(*dims, w.shape[0] // math.prod(dims), w.shape[1])

    half = basis.reshape(CORES, *dims, basis.shape[0] // CORES // math.prod(dims), basis.shape[1])
    arrays = [pieces(gate), pieces(up), down.reshape(2, SIZES["z"], -1, down.shape[1]), pieces(out_proj), half, pieces(heads)]
    groups = weight_cuts([w.shape for w in arrays])
    jobs = [cut for group in groups for cut in group]
    accs = [pltpu.VMEM(cut.acc_shape(), BF16) for cut in jobs]
    slots = [pltpu.VMEM(shape, BF16) for cut in jobs for shape in cut.slots()]
    copies = 10 * len(jobs) + 4
    any_space = pl.BlockSpec(memory_space=pl.ANY)
    outs = pl.pallas_call(
        functools.partial(weight_kernel, groups, len(arrays)),
        out_shape=[jax.ShapeDtypeStruct(w.shape, BF16) for w in arrays],
        in_specs=[any_space] * len(arrays),
        out_specs=[any_space] * len(arrays),
        scratch_shapes=[*accs, *slots, pltpu.VMEM(half.shape[1:], BF16), pltpu.VMEM(half.shape[1:], BF16),
                        pltpu.SemaphoreType.DMA((2 * len(jobs) + 1,)), pltpu.SemaphoreType.DMA((copies,)),
                        pltpu.SemaphoreType.DMA((copies,))],
        compiler_params=pltpu.CompilerParams(collective_id=3, has_side_effects=True, vmem_limit_bytes=48 * 2**20),
        name="weight_sums",
    )(*arrays)
    return [o.reshape(w.shape) for o, w in zip(outs, (gate, up, down, out_proj, basis, heads))]


def norm_back(inputs, row_scale, gain_vec, grad_rows):
    weighted = grad_rows * gain_vec
    cubed = row_scale * row_scale * row_scale
    input_part = row_scale * weighted - inputs * cubed * jnp.mean(inputs * weighted, axis=-1, keepdims=True)
    gain_part = jnp.sum(grad_rows * inputs * row_scale, axis=(0, 1))
    return (input_part, gain_part)


def project(activations, weight):
    return jnp.einsum("rsd,de->rse", activations, weight, preferred_element_type=F32)


def back_project(grad_rows, weight):
    return jnp.einsum("rse,de->rsd", grad_rows, weight, preferred_element_type=F32)


def weight_grad(normed, grad_rows):
    return jnp.einsum("rsd,rse->de", normed, grad_rows, preferred_element_type=F32)


def head_sum(partial, ident):
    if on_known_slice():
        return pair_sum(partial.astype(BF16), ident).astype(F32)
    return lax.psum(partial.astype(BF16), "head").astype(F32)


def rms_scale(tensor):
    return lax.rsqrt(jnp.mean(tensor * tensor, axis=-1, keepdims=True) + EPS)


def spread_tables(head_count, width, pack_rows):
    hd = head_count * DH
    lane = jnp.arange(LANES, dtype=jnp.int32)[None, :, None]
    row = jnp.arange(pack_rows, dtype=jnp.int32)[:, None, None]
    col = jnp.arange(4 * hd, dtype=jnp.int32)[None, None, :]
    kind, head = col // hd, col % hd // DH
    source = row * width + (kind // 2) * (head_count * RK) + head * RK + kind % 2
    spread = jnp.where(lane == source, 0.5, 0.0).astype(BF16)
    factor = jnp.arange(head_count * RQ, dtype=jnp.int32)[:, None]
    col = jnp.arange(RQ * hd, dtype=jnp.int32)[None, :]
    query = jnp.where(factor == col % hd // DH * RQ + col // hd, 1.0, 0.0).astype(BF16)
    return spread, query


def rope_tables(position):
    half = DH // 2
    frequency = jnp.exp(jnp.arange(half).astype(F32) * (-2.0 * math.log(10000.0) / DH))
    angles = position[:, None] * frequency[None, :]
    cos, sin = jnp.cos(angles), jnp.sin(angles)
    return jnp.concatenate([cos] * 4, axis=1), jnp.concatenate([-sin, sin, -sin, sin], axis=1)


def shards(
    block_input,
    seq_lengths,
    attn_gain,
    query_heads,
    query_basis,
    key_heads,
    key_basis,
    value_heads,
    value_basis,
    out_project,
    ffn_gain,
    gate_weight,
    up_weight,
    down_weight,
    out_cotangent,
):
    row_count, slot_count, model_dim = block_input.shape
    head_count = query_heads.shape[1] // RQ
    hd = head_count * DH
    length = slot_count * lax.axis_size("seq")
    first_slot = lax.axis_index("seq") * slot_count
    width = head_count * (RK + RV)
    pack_rows = max(n for n in range(1, row_count + 1) if row_count % n == 0 and n * width <= LANES)
    group = min(4, head_count)
    block = math.gcd(length, KEY_BLOCK)
    spread, query_spread = spread_tables(head_count, width, pack_rows)
    cos, sin = rope_tables((first_slot + jnp.arange(slot_count, dtype=jnp.int32)).astype(F32))
    both = jnp.concatenate([key_heads, value_heads], axis=1)
    packed = jnp.concatenate([both] * pack_rows + [jnp.zeros((model_dim, LANES - width * pack_rows), BF16)], axis=1)
    normed, aq, bq, queries, own_kv, own_heads = factors(
        block_input, attn_gain, query_heads, query_basis, key_basis, value_basis, packed, cos, sin, query_spread,
        pack_rows, width)
    inputs = block_input.astype(F32)
    scale_one = rms_scale(inputs)
    if on_known_slice():
        kv = collect(own_kv, own_heads)
        shift = (1 - lax.axis_index("head")) * (row_count // CORES)
    else:
        kv = lax.all_gather(jnp.concatenate([own_kv, own_heads], axis=0), "seq", axis=1, tiled=True)
        shift = jnp.zeros((), jnp.int32)
    info = jnp.stack([*[seq_lengths[r] for r in range(row_count)], shift, first_slot]).astype(jnp.int32)
    attended, mixed_flat, lse = attend(info, queries, kv, shift, spread, pack_rows, group, block)
    attn_out = head_sum(project(mixed_flat, out_project), 4)
    middle = inputs + attn_out
    scale_two = rms_scale(middle)
    normed_two = (middle * scale_two * ffn_gain).astype(BF16)
    gate_act = project(normed_two, gate_weight)
    up_act = project(normed_two, up_weight)
    sigmoid_gate = jax.nn.sigmoid(gate_act)
    silu_gate = gate_act * sigmoid_gate
    hidden = (silu_gate * up_act).astype(BF16)
    ffn_out = head_sum(project(hidden, down_weight), 5)
    block_output = (middle + ffn_out).astype(BF16)
    cotangent = out_cotangent.astype(F32)
    down_grad = jnp.einsum("rsf,rsd->fd", hidden, out_cotangent, preferred_element_type=F32)
    d_hidden = jnp.einsum("rsd,fd->rsf", out_cotangent, down_weight, preferred_element_type=F32)
    d_gate = (d_hidden * up_act * (sigmoid_gate * (1.0 + gate_act * (1.0 - sigmoid_gate)))).astype(BF16)
    d_up = (d_hidden * silu_gate).astype(BF16)
    gate_grad = weight_grad(normed_two, d_gate)
    up_grad = weight_grad(normed_two, d_up)
    d_normed_two = head_sum(back_project(d_gate, gate_weight) + back_project(d_up, up_weight), 6)
    d_middle_norm, ffn_gain_part = norm_back(middle, scale_two, ffn_gain, d_normed_two)
    d_middle = cotangent + d_middle_norm
    d_branch = d_middle.astype(BF16)
    out_project_grad = jnp.einsum("rsf,rsd->fd", mixed_flat, d_branch, preferred_element_type=F32)
    d_mixed = back_project(d_branch, out_project).astype(BF16)
    d_queries, d_kv, d_heads = attend_back(info, queries, kv, spread, attended, d_mixed, lse, pack_rows, group, block)
    dq_heads, dq_basis = query_grads(d_queries, aq, bq, query_spread, cos, sin, pack_rows)
    if on_known_slice():
        key_grads = give_back(d_kv, d_heads)
    else:
        key_grads = lax.psum_scatter(
            jnp.concatenate([d_kv, d_heads], axis=0), "seq", scatter_dimension=1, tiled=True)
    d_kv_own = key_grads[: 2 * row_count].reshape(row_count, 2, slot_count, LANES).astype(F32)
    half = DH // 2
    pairs = d_kv_own[:, 0].reshape(row_count, slot_count, 2, 2, half)
    u, w = pairs[:, :, :, 0], pairs[:, :, :, 1]
    c, s = cos[None, :, None, :half], sin[None, :, None, half:DH]
    dk_basis = jnp.stack([u * c + w * s, w * c - u * s], axis=3).reshape(row_count, slot_count, LANES).astype(BF16)
    dv_basis = d_kv_own[:, 1].astype(BF16)
    packs = row_count // pack_rows
    d_heads_own = key_grads[2 * row_count :, :, : width * pack_rows].reshape(packs, slot_count, pack_rows, width)
    d_heads_own = jnp.transpose(d_heads_own, (0, 2, 1, 3)).reshape(row_count, slot_count, width).astype(BF16)
    dk_heads, dv_heads = d_heads_own[..., : head_count * RK], d_heads_own[..., head_count * RK :]
    d_normed = head_sum(
        back_project(dq_heads, query_heads) + back_project(dq_basis, query_basis)
        + back_project(dk_heads, key_heads) + back_project(dk_basis, key_basis)
        + back_project(dv_heads, value_heads) + back_project(dv_basis, value_basis), 7)
    d_input_norm, attn_gain_part = norm_back(inputs, scale_one, attn_gain, d_normed)
    input_grad = d_middle + d_input_norm
    head_grads = weight_grad(normed, jnp.concatenate([dq_heads, dk_heads, dv_heads], axis=-1))
    basis_grads = weight_grad(normed, jnp.concatenate([dq_basis, dk_basis, dv_basis], axis=-1))

    gains = jnp.stack([attn_gain_part, ffn_gain_part], axis=1)
    small = jnp.concatenate([head_grads, gains], axis=1)
    if on_known_slice():
        small = jnp.pad(small, ((0, 0), (0, -small.shape[1] % LANES)))
        sums = weight_sums(*[t.astype(BF16) for t in (gate_grad, up_grad, down_grad, out_project_grad, basis_grads, small)])
        gate_grad, up_grad, down_grad, out_project_grad, basis_grads, small = [t.astype(F32) for t in sums]
    else:
        sums = lax.psum(tuple(t.astype(BF16) for t in (gate_grad, up_grad, down_grad, out_project_grad, small)), "seq")
        gate_grad, up_grad, down_grad, out_project_grad, small = [t.astype(F32) for t in sums]
        basis_grads = lax.psum(basis_grads, ("seq", "head"))
    head_grads = small
    gain_at = head_count * (RQ + RK + RV)
    attn_gain_part, ffn_gain_part = small[:, gain_at], small[:, gain_at + 1]
    nq, nk = head_count * RQ, head_count * RK
    return (
        block_output,
        input_grad,
        attn_gain_part,
        head_grads[:, :nq],
        basis_grads[:, : RQ * DH],
        head_grads[:, nq : nq + nk],
        basis_grads[:, RQ * DH : (RQ + RK) * DH],
        head_grads[:, nq + nk : gain_at],
        basis_grads[:, (RQ + RK) * DH :],
        out_project_grad,
        ffn_gain_part,
        gate_grad,
        up_grad,
        down_grad,
    )


def solution(mesh):
    rows = P(None, "seq", None)
    columns, features = P(None, "head"), P("head", None)
    in_specs = (rows, P(), P(), columns, P(), columns, P(), columns, P(), features, P(), columns, columns, features, rows)
    out_specs = (rows, rows, P(), columns, P(), columns, P(), columns, P(), features, P(), columns, columns, features)
    return jax.shard_map(shards, mesh=mesh, in_specs=in_specs, out_specs=out_specs, check_vma=False)
```

```python
import functools
import math

import jax
import jax.numpy as jnp
from jax import lax
from jax.experimental import pallas as pl
from jax.experimental.pallas import tpu as pltpu
from jax.sharding import PartitionSpec as P

DH = 64
RQ = 6
RK = 2
RV = 2
LANES = 128
EPS = 1e-06
KEY_BLOCK = 256
F32 = jnp.float32
BF16 = jnp.bfloat16


def dot(a, b):
    return lax.dot_general(a, b, (((1,), (0,)), ((), ())), preferred_element_type=F32)


def dot_nt(a, b):
    return lax.dot_general(a, b, (((1,), (1,)), ((), ())), preferred_element_type=F32)


def dot_tn(a, b):
    return lax.dot_general(a, b, (((0,), (0,)), ((), ())), preferred_element_type=F32)


def lane_of(shape):
    return lax.broadcasted_iota(jnp.int32, shape, len(shape) - 1)


def both_halves(pair):
    swapped = pltpu.roll(pair, DH, 1)
    low = lane_of(pair.shape) < DH
    return jnp.where(low, pair, swapped), jnp.where(low, swapped, pair)


def turn(pair, cos, sin):
    half = DH // 2
    first = lane_of(pair.shape) % DH < half
    other = jnp.where(first, pltpu.roll(pair, LANES - half, 1), pltpu.roll(pair, half, 1))
    return pair * cos + other * sin


def split_heads(rows, head_rows, tokens):
    group = lane_of(rows.shape) // DH
    return jnp.concatenate([jnp.where(group == h, rows, jnp.zeros_like(rows)) for h in range(head_rows)], axis=0)


def join_heads(block, head_rows, tokens):
    out = block[:tokens]
    group = lane_of(out.shape) // DH
    for h in range(1, head_rows):
        out = jnp.where(group == h, block[h * tokens : (h + 1) * tokens], out)
    return out


def factor_kernel(width, x_ref, gain_ref, wqh_ref, wqb_ref, wkb_ref, wvb_ref, wh_ref, cos_ref, sin_ref, eq_ref,
                  xn_ref, aq_ref, bq_ref, q_ref, kv_ref, hd_ref):
    rows, tokens, model = x_ref.shape
    hd = q_ref.shape[2]
    count = rows * tokens
    x = x_ref[...].astype(F32).reshape(count, model)
    scale = lax.rsqrt(jnp.mean(x * x, axis=-1, keepdims=True) + EPS)
    xn = (x * scale * gain_ref[...]).astype(BF16)
    xn_ref[...] = xn.reshape(rows, tokens, model)
    cos = jnp.concatenate([cos_ref[...]] * rows, axis=0)
    sin = jnp.concatenate([sin_ref[...]] * rows, axis=0)
    keys = turn(dot(xn, wkb_ref[...]), cos, sin).astype(BF16)
    values = dot(xn, wvb_ref[...]).astype(BF16)
    heads = dot(xn, wh_ref[...])
    lanes = lane_of((tokens, LANES)) // width
    pack = heads[:tokens]
    for r in range(rows):
        part = slice(r * tokens, (r + 1) * tokens)
        kv_ref[2 * r] = keys[part]
        kv_ref[2 * r + 1] = values[part]
        if r:
            pack = jnp.where(lanes == r, heads[part], pack)
    hd_ref[0] = pack.astype(BF16)
    aq = dot(xn, wqh_ref[...])
    aq_ref[...] = aq.reshape(rows, tokens, aq.shape[1])
    aq_high = aq.astype(BF16)
    aq_low = (aq - aq_high.astype(F32)).astype(BF16)
    basis = dot(xn, wqb_ref[...])
    total = [jnp.zeros((count, LANES), F32) for _ in range(hd // LANES)]
    for p in range(RQ // 2):
        pair = turn(basis[:, p * LANES : (p + 1) * LANES], cos, sin)
        bq_ref[:, :, p * LANES : (p + 1) * LANES] = pair.reshape(rows, tokens, LANES)
        for half, vec in enumerate(both_halves(pair)):
            spread = eq_ref[:, (2 * p + half) * hd : (2 * p + half + 1) * hd]
            coef = dot(aq_high, spread) + dot(aq_low, spread)
            for c in range(hd // LANES):
                total[c] = total[c] + coef[:, c * LANES : (c + 1) * LANES] * vec
    for c in range(hd // LANES):
        low = (total[c] / RQ).astype(BF16).astype(F32) * (1.0 / math.sqrt(DH))
        q_ref[:, :, c * LANES : (c + 1) * LANES] = low.astype(BF16).reshape(rows, tokens, LANES)


def whole(*shape):
    return pl.BlockSpec(shape, lambda *_: (0,) * len(shape))


def factors(x, gain, wqh, wqb, wkb, wvb, wh, cos, sin, eq, pack_rows, width):
    rows, tokens, model = x.shape
    hd = eq.shape[1] // RQ
    packs = rows // pack_rows
    nq = wqh.shape[1]

    def row_block(last):
        return pl.BlockSpec((pack_rows, tokens, last), lambda g: (g, 0, 0))

    return pl.pallas_call(
        functools.partial(factor_kernel, width),
        grid=(packs,),
        in_specs=[row_block(model), whole(1, model), whole(*wqh.shape), whole(*wqb.shape), whole(*wkb.shape),
                  whole(*wvb.shape), whole(*wh.shape), whole(*cos.shape), whole(*sin.shape), whole(*eq.shape)],
        out_specs=[row_block(model), row_block(nq), row_block(RQ * DH), row_block(hd),
                   pl.BlockSpec((2 * pack_rows, tokens, LANES), lambda g: (g, 0, 0)),
                   pl.BlockSpec((1, tokens, LANES), lambda g: (g, 0, 0))],
        out_shape=[
            jax.ShapeDtypeStruct((rows, tokens, model), BF16),
            jax.ShapeDtypeStruct((rows, tokens, nq), F32),
            jax.ShapeDtypeStruct((rows, tokens, RQ * DH), F32),
            jax.ShapeDtypeStruct((rows, tokens, hd), BF16),
            jax.ShapeDtypeStruct((2 * rows, tokens, LANES), BF16),
            jax.ShapeDtypeStruct((packs, tokens, LANES), BF16),
        ],
        compiler_params=pltpu.CompilerParams(vmem_limit_bytes=56 * 2**20),
        name="factors",
    )(x, gain.reshape(1, model), wqh, wqb, wkb, wvb, wh, cos, sin, eq)


def query_grad_rows(dq, aq, bq, eq_ref, cos, sin):
    hd = dq.shape[1]
    aq_high = aq.astype(BF16)
    aq_low = (aq - aq_high.astype(F32)).astype(BF16)
    da = jnp.zeros(aq.shape, F32)
    low = lane_of((dq.shape[0], LANES)) < DH
    turned = []
    for p in range(RQ // 2):
        sums = []
        for half, vec in enumerate(both_halves(bq[:, p * LANES : (p + 1) * LANES])):
            spread = eq_ref[:, (2 * p + half) * hd : (2 * p + half + 1) * hd]
            coef = dot(aq_high, spread) + dot(aq_low, spread)
            acc = None
            prods = []
            for c in range(hd // LANES):
                part = dq[:, c * LANES : (c + 1) * LANES]
                term = coef[:, c * LANES : (c + 1) * LANES] * part
                acc = term if acc is None else acc + term
                prods.append(part * vec)
            prod = jnp.concatenate(prods, axis=1)
            high = prod.astype(BF16)
            rest = (prod - high.astype(F32)).astype(BF16)
            da = da + dot_nt(high, spread) + dot_nt(rest, spread)
            sums.append(acc + pltpu.roll(acc, DH, 1))
        turned.append(turn(jnp.where(low, sums[0], sums[1]), cos, -sin) * (1.0 / RQ))
    return (da * (1.0 / RQ)).astype(BF16), jnp.concatenate(turned, axis=1).astype(BF16)


def query_grad_kernel(dq_ref, aq_ref, bq_ref, eq_ref, cos_ref, sin_ref, da_ref, db_ref):
    rows, tokens, hd = dq_ref.shape
    count = rows * tokens
    da, db = query_grad_rows(
        dq_ref[...].reshape(count, hd), aq_ref[...].reshape(count, -1), bq_ref[...].reshape(count, -1), eq_ref,
        jnp.concatenate([cos_ref[...]] * rows, axis=0), jnp.concatenate([sin_ref[...]] * rows, axis=0))
    da_ref[...] = da.reshape(da_ref.shape)
    db_ref[...] = db.reshape(db_ref.shape)


def query_grads(dq, aq, bq, eq, cos, sin, pack_rows):
    rows, tokens, hd = dq.shape
    nq = aq.shape[2]

    def row_block(last):
        return pl.BlockSpec((pack_rows, tokens, last), lambda g: (g, 0, 0))

    return pl.pallas_call(
        query_grad_kernel,
        grid=(rows // pack_rows,),
        in_specs=[row_block(hd), row_block(nq), row_block(RQ * DH), whole(*eq.shape), whole(*cos.shape), whole(*sin.shape)],
        out_specs=[row_block(nq), row_block(RQ * DH)],
        out_shape=[jax.ShapeDtypeStruct((rows, tokens, nq), BF16), jax.ShapeDtypeStruct((rows, tokens, RQ * DH), BF16)],
        compiler_params=pltpu.CompilerParams(vmem_limit_bytes=56 * 2**20),
        name="query_grads",
    )(dq, aq, bq, eq, cos, sin)


def key_rows(basis):
    turned = basis.astype(F32).T * 0.5
    return turned[:DH], turned[DH:]


def build_heads(coefs, first, second, head_count):
    return jnp.concatenate(
        [coefs[2 * h : 2 * h + 1] * first + coefs[2 * h + 1 : 2 * h + 2] * second for h in range(head_count)], axis=0
    ).astype(BF16)


def row_limits(info_ref, row, tokens, block, lanes):
    first = info_ref[info_ref.shape[0] - 1]
    length = info_ref[row]
    used = jnp.minimum(length, first + tokens)
    slot = lax.broadcasted_iota(jnp.int32, (lanes, 1), 0) % tokens
    return jnp.minimum(first + slot, length - 1), (used + block - 1) // block


def attend_kernel(pack_rows, group, block, width, info_ref, q_ref, kv_ref, hd_ref, o_ref, ob_ref, lse_ref, ct_ref):
    row = pl.program_id(0)
    _, tokens, hd = q_ref.shape
    head_count = hd // DH
    lanes = group * tokens
    wide = group * DH
    groups = hd // wide
    limit, blocks = row_limits(info_ref, row, tokens, block, lanes)
    queries = [split_heads(q_ref[0, :, g * wide : (g + 1) * wide], group, tokens) for g in range(groups)]
    place = pl.multiple_of(row % pack_rows * width, 8)

    def one(b, carry):
        at = pl.ds(pl.multiple_of(b * block, block), block)
        ct_ref[...] = hd_ref[0, at, :].astype(F32).T
        coefs = ct_ref[pl.ds(place, width), :]
        keys = build_heads(coefs[: RK * head_count], *key_rows(kv_ref[0, at, :]), head_count)
        values = build_heads(coefs[RK * head_count :], *key_rows(kv_ref[1, at, :]), head_count)
        live = b * block + lax.broadcasted_iota(jnp.int32, (1, block), 1) <= limit
        out = []
        for g in range(groups):
            peak, total, mixed = carry[g]
            raw = jnp.where(live, dot(queries[g], keys[g * wide : (g + 1) * wide]), -1e30)
            top = jnp.maximum(peak, jnp.max(raw, axis=1, keepdims=True))
            e = jnp.exp(raw - top)
            keep = jnp.exp(peak - top)
            total = total * keep + jnp.sum(e, axis=1, keepdims=True)
            mixed = mixed * keep + dot_nt(e.astype(BF16), values[g * wide : (g + 1) * wide])
            out.append((top, total, mixed))
        return tuple(out)

    start = (jnp.full((lanes, 1), -1e30, F32), jnp.zeros((lanes, 1), F32), jnp.zeros((lanes, wide), F32))
    done = lax.fori_loop(0, blocks, one, (start,) * groups)
    lane = lane_of((tokens, LANES))
    lse = jnp.zeros((tokens, LANES), F32)
    for g in range(groups):
        peak, total, mixed = done[g]
        mixed = join_heads(mixed / total, group, tokens)
        o_ref[0, :, g * wide : (g + 1) * wide] = mixed
        ob_ref[0, :, g * wide : (g + 1) * wide] = mixed.astype(BF16)
        level = peak + jnp.log(total)
        for h in range(group):
            lse = jnp.where(lane == g * group + h, level[h * tokens : (h + 1) * tokens], lse)
    lse_ref[0] = lse


def attend(info, q, kv, pack_rows, group, block, width):
    rows, tokens, hd = q.shape
    length = kv.shape[1]

    def own(r, i):
        return (r, 0, 0)

    grid_spec = pltpu.PrefetchScalarGridSpec(
        num_scalar_prefetch=1,
        grid=(rows,),
        in_specs=[
            pl.BlockSpec((1, tokens, hd), own),
            pl.BlockSpec((2, length, LANES), lambda r, i: (lax.rem(r + i[rows], rows), 0, 0)),
            pl.BlockSpec((1, length, LANES), lambda r, i: (2 * rows + r // pack_rows, 0, 0)),
        ],
        out_specs=[pl.BlockSpec((1, tokens, hd), own), pl.BlockSpec((1, tokens, hd), own), pl.BlockSpec((1, tokens, LANES), own)],
        scratch_shapes=[pltpu.VMEM((LANES, block), F32)],
    )
    return pl.pallas_call(
        functools.partial(attend_kernel, pack_rows, group, block, width),
        grid_spec=grid_spec,
        out_shape=[
            jax.ShapeDtypeStruct((rows, tokens, hd), F32),
            jax.ShapeDtypeStruct((rows, tokens, hd), BF16),
            jax.ShapeDtypeStruct((rows, tokens, LANES), F32),
        ],
        compiler_params=pltpu.CompilerParams(vmem_limit_bytes=32 * 2**20),
        name="attend",
    )(info, q, kv, kv)


def attend_back_kernel(pack_rows, group, block, width, info_ref, q_ref, kv_ref, hd_ref, o_ref, do_ref, lse_ref,
                       dq_ref, dkv_ref, dhd_ref, dq_acc, ct_ref, dct_ref):
    row = pl.program_id(0)
    _, tokens, hd = q_ref.shape
    head_count = hd // DH
    lanes = group * tokens
    wide = group * DH
    groups = hd // wide
    limit, blocks = row_limits(info_ref, row, tokens, block, lanes)
    place = pl.multiple_of(row % pack_rows * width, 8)
    queries, grads, deltas, levels = [], [], [], []
    for g in range(groups):
        part = slice(g * wide, (g + 1) * wide)
        do = do_ref[0, :, part]
        queries.append(split_heads(q_ref[0, :, part], group, tokens))
        grads.append(split_heads(do, group, tokens))
        weighed = split_heads(do.astype(F32) * o_ref[0, :, part], group, tokens)
        deltas.append(jnp.sum(weighed, axis=1, keepdims=True))
        levels.append(jnp.concatenate([lse_ref[0, :, h : h + 1] for h in range(g * group, (g + 1) * group)], axis=0))
    queries_t = [q.astype(F32).T.astype(BF16) for q in queries]
    grads_t = [g.astype(F32).T.astype(BF16) for g in grads]
    dq_acc[...] = jnp.zeros_like(dq_acc)
    dkv_ref[...] = jnp.zeros_like(dkv_ref)
    dct_ref[...] = jnp.zeros_like(dct_ref)

    @pl.when(row % pack_rows == 0)
    def _():
        dhd_ref[...] = jnp.zeros_like(dhd_ref)

    def factor_grads(grad, coefs, vectors):
        sums, rows = [None, None], []
        for h in range(head_count):
            part = grad[h * DH : (h + 1) * DH]
            for r in range(2):
                term = coefs[2 * h + r : 2 * h + r + 1] * part
                sums[r] = term if h == 0 else sums[r] + term
                rows.append(jnp.sum(part * vectors[r], axis=0, keepdims=True))
        return (jnp.concatenate(sums, axis=0) * 0.5).T.astype(BF16), rows

    def one(b, carry):
        at = pl.ds(pl.multiple_of(b * block, block), block)
        ct_ref[...] = hd_ref[0, at, :].astype(F32).T
        coefs = ct_ref[pl.ds(place, width), :]
        key_coefs, value_coefs = coefs[: RK * head_count], coefs[RK * head_count :]
        key_vectors, value_vectors = key_rows(kv_ref[0, at, :]), key_rows(kv_ref[1, at, :])
        keys = build_heads(key_coefs, *key_vectors, head_count)
        values = build_heads(value_coefs, *value_vectors, head_count)
        live = b * block + lax.broadcasted_iota(jnp.int32, (1, block), 1) <= limit
        dks, dvs = [], []
        for g in range(groups):
            part = slice(g * wide, (g + 1) * wide)
            p = jnp.where(live, jnp.exp(dot(queries[g], keys[part]) - levels[g]), 0.0)
            dp = dot(grads[g], values[part])
            ds = (p * (dp - deltas[g])).astype(BF16)
            dvs.append(dot(grads_t[g], p.astype(BF16)))
            dks.append(dot(queries_t[g], ds))
            dq_acc[g] += dot_nt(ds, keys[part])
        dkv_ref[0, at, :], key_grads = factor_grads(jnp.concatenate(dks, axis=0), key_coefs, key_vectors)
        dkv_ref[1, at, :], value_grads = factor_grads(jnp.concatenate(dvs, axis=0), value_coefs, value_vectors)
        dct_ref[pl.ds(place, width), :] = jnp.concatenate(key_grads + value_grads, axis=0)
        dhd_ref[0, at, :] = (dhd_ref[0, at, :].astype(F32) + dct_ref[...].T).astype(BF16)
        return carry

    lax.fori_loop(0, blocks, one, 0)
    for g in range(groups):
        dq_ref[0, :, g * wide : (g + 1) * wide] = join_heads(dq_acc[g], group, tokens) * (1.0 / math.sqrt(DH))


def attend_back(info, q, kv, o, do, lse, pack_rows, group, block, width):
    rows, tokens, hd = q.shape
    length = kv.shape[1]
    packs = rows // pack_rows

    def place(r, i):
        return (lax.rem(r + i[rows], rows), 0, 0)

    def own(r, i):
        return (r, 0, 0)

    grid_spec = pltpu.PrefetchScalarGridSpec(
        num_scalar_prefetch=1,
        grid=(rows,),
        in_specs=[
            pl.BlockSpec((1, tokens, hd), own),
            pl.BlockSpec((2, length, LANES), place),
            pl.BlockSpec((1, length, LANES), lambda r, i: (2 * rows + r // pack_rows, 0, 0)),
            pl.BlockSpec((1, tokens, hd), own),
            pl.BlockSpec((1, tokens, hd), own),
            pl.BlockSpec((1, tokens, LANES), own),
        ],
        out_specs=[
            pl.BlockSpec((1, tokens, hd), own),
            pl.BlockSpec((2, length, LANES), place),
            pl.BlockSpec((1, length, LANES), lambda r, i: (r // pack_rows, 0, 0)),
        ],
        scratch_shapes=[pltpu.VMEM((hd // (group * DH), group * tokens, group * DH), F32),
                        pltpu.VMEM((LANES, block), F32), pltpu.VMEM((LANES, block), F32)],
    )
    return pl.pallas_call(
        functools.partial(attend_back_kernel, pack_rows, group, block, width),
        grid_spec=grid_spec,
        out_shape=[
            jax.ShapeDtypeStruct((rows, tokens, hd), F32),
            jax.ShapeDtypeStruct((2 * rows, length, LANES), BF16),
            jax.ShapeDtypeStruct((packs, length, LANES), BF16),
        ],
        compiler_params=pltpu.CompilerParams(vmem_limit_bytes=32 * 2**20),
        name="attend_back",
    )(info, q, kv, kv, o, do, lse)


MESH = pl.DeviceIdType.MESH
SIZES = {"z": 4, "y": 2, "x": 2}
STRIDES = {"z": 4, "y": 2, "x": 1}
CORES = 2


def on_known_slice():
    return lax.axis_size("seq") == math.prod(SIZES.values()) and lax.axis_size("head") == CORES


class Links:
    def __init__(self, send_sems, recv_sems):
        self.seq = lax.axis_index("seq")
        self.core = lax.axis_index("head")
        self.at = {d: lax.rem(self.seq // STRIDES[d], SIZES[d]) for d in SIZES}
        self.send_sems, self.recv_sems = send_sems, recv_sems
        self.count = 0
        self.started = []

    def along(self, d, offset):
        there = lax.rem(self.at[d] + offset, SIZES[d])
        return there, (self.seq + (there - self.at[d]) * STRIDES[d], self.core)

    def other_core(self):
        return (self.seq, 1 - self.core)

    def greet(self, core, chips=True):
        barrier = pltpu.get_barrier_semaphore()
        devices = [self.other_core()] if core else []
        if chips:
            devices += [self.along(d, o)[1] for d in SIZES for o in range(1, SIZES[d])]
        for device in devices:
            pl.semaphore_signal(barrier, inc=1, device_id=device, device_id_type=MESH)
        pl.semaphore_wait(barrier, len(devices))

    def send(self, src, dst, device):
        copy = pltpu.make_async_remote_copy(
            src_ref=src, dst_ref=dst, send_sem=self.send_sems.at[self.count], recv_sem=self.recv_sems.at[self.count],
            device_id=device, device_id_type=MESH)
        self.count += 1
        copy.start()
        self.started.append(copy)
        return copy

    def finish(self):
        for copy in self.started:
            copy.wait_send()


def accumulate(acc, slots):
    lead = acc.shape[:-2]

    def body(i, carry):
        at = []
        for size in reversed(lead):
            at.insert(0, lax.rem(i, size))
            i = i // size
        value = acc[(*at, slice(None), slice(None))].astype(F32)
        for o in range(slots.shape[0]):
            value = value + slots[(o, *at, slice(None), slice(None))].astype(F32)
        acc[(*at, slice(None), slice(None))] = value.astype(BF16)
        return carry

    lax.fori_loop(0, math.prod(lead), body, 0)


def scatter_steps(links, order, source, acc, slots, ready):
    fixed = {}
    for k, d in enumerate(order):
        copies = []
        for o in range(1, SIZES[d]):
            there, device = links.along(d, o)
            view = source if k == 0 else acc
            copies.append(links.send(view({**fixed, d: there}), slots[k].at[o - 1], device))
        yield
        if k == 0:
            ready()
        for copy in copies:
            copy.wait_recv()
        fixed[d] = links.at[d]
        accumulate(acc(fixed), slots[k])


def gather_steps(links, order, out, first):
    for k in reversed(range(len(order))):
        fixed = {d: links.at[d] for d in order[: k + 1]}
        copies = []
        for o in range(1, SIZES[order[k]]):
            _, device = links.along(order[k], o)
            src = first if first is not None and k == len(order) - 1 else out(fixed)
            copies.append(links.send(src, out(fixed), device))
        yield
        for copy in copies:
            copy.wait_recv()


def run_waves(groups):
    live, waiting = [], list(groups)
    while live or waiting:
        if waiting:
            live.append(list(waiting.pop(0)))
        for group in live:
            group[:] = [job for job in group if next(job, "end") != "end"]
        live = [group for group in live if group]


def in_pairs(jobs):
    half = (len(jobs) + 1) // 2
    return [jobs[i : i + 1] + jobs[half + i : half + i + 1] for i in range(half)]


def slot_shapes(order, units, tail):
    shapes, open_dims = [], list(SIZES)
    for d in order:
        open_dims.remove(d)
        shapes.append((SIZES[d] - 1, *units, *[SIZES[e] for e in open_dims], *tail))
    return shapes


def pick(ref, lead, sel, axes, tail=()):
    return ref.at[(*lead, *[sel.get(d, slice(None)) for d in axes], *tail)]


ZYX = ("z", "y", "x")


def collect_jobs(rows, packs):
    step = 2
    own = [(rows + u, min(step, rows - u)) for u in range(0, rows, step)]
    jobs = own + [(2 * rows, packs)]
    half = (len(jobs) + 1) // 2
    return [(first, n, ("y", "x", "z") if i < half else ("x", "y", "z")) for i, (first, n) in enumerate(jobs)]


def collect_kernel(rows, packs, kv_ref, hd_ref, out_ref, local_sems, send_sems, recv_sems):
    links = Links(send_sems, recv_sems)
    links.greet(core=True)
    own = tuple(links.at[d] for d in ZYX)
    locals_ = []
    jobs = collect_jobs(rows, packs)
    for i, (first, n, _) in enumerate(jobs):
        src = hd_ref if first == 2 * rows else kv_ref.at[pl.ds(links.core * rows + first - rows, n)]
        copy = pltpu.make_async_copy(src, out_ref.at[(pl.ds(first, n), *own)], local_sems.at[i])
        copy.start()
        locals_.append(copy)

    def job(i, first, n, order):
        locals_[i].wait()
        yield from gather_steps(links, order, lambda sel: pick(out_ref, [pl.ds(first, n)], sel, ZYX), None)
        if first < 2 * rows:
            copy = links.send(out_ref.at[pl.ds(first, n)], out_ref.at[pl.ds(first - rows, n)], links.other_core())
            yield
            copy.wait_recv()

    run_waves(in_pairs([job(i, *j) for i, j in enumerate(jobs)]))
    links.finish()


def collect(kv, hd):
    units, tokens, _ = kv.shape
    packs = hd.shape[0]
    rows = units // 2
    copies = 8 * len(collect_jobs(rows, packs))
    out = pl.pallas_call(
        functools.partial(collect_kernel, rows, packs),
        out_shape=jax.ShapeDtypeStruct((units + packs, *[SIZES[d] for d in ZYX], tokens, LANES), BF16),
        in_specs=[pl.BlockSpec(memory_space=pl.ANY)] * 2,
        out_specs=pl.BlockSpec(memory_space=pl.ANY),
        scratch_shapes=[pltpu.SemaphoreType.DMA((8,)), pltpu.SemaphoreType.DMA((copies,)), pltpu.SemaphoreType.DMA((copies,))],
        compiler_params=pltpu.CompilerParams(collective_id=1, has_side_effects=True),
        name="collect",
    )(kv, hd)
    return out.reshape(units + packs, -1, LANES)


def return_kernel(rows, packs, chunk, groups, count, dkv_ref, dhd_ref, cos_ref, sin_ref, dq_ref, aq_ref, bq_ref, eq_ref, *refs):
    ins, refs = refs[:count], refs[count:]
    (dk_ref, dv_ref, dh_ref, da_ref, db_ref), refs = refs[:5], refs[5:]
    outs, refs = refs[:count], refs[count:]
    acc_ref, core_ref, refs = refs[0], refs[1], refs[2:]
    jobs = collect_jobs(rows, packs)
    slot_refs, refs = refs[: 3 * len(jobs)], refs[3 * len(jobs) :]
    cuts = [cut for group in groups for cut in group]
    cut_accs, cut_slots, refs = refs[: len(cuts)], refs[len(cuts) : 4 * len(cuts)], refs[4 * len(cuts) :]
    local_sems, cut_sems, send_sems, recv_sems = refs
    links = Links(send_sems, recv_sems)
    links.greet(core=True)
    own = tuple(links.at[d] for d in ZYX)
    loads, swaps = [], []
    for i, (first, n, _) in enumerate(jobs):
        heads = first == 2 * rows
        part = pl.ds(first - rows, n)
        if not heads:
            swaps.append(links.send(dkv_ref.at[part], core_ref.at[part], links.other_core()))
        load = pltpu.make_async_copy(dhd_ref if heads else dkv_ref.at[pl.ds(first, n)], acc_ref.at[part], local_sems.at[i])
        load.start()
        loads.append(load)
    cut_loads = [start_load(links, cut, ins[cut.array], cut_accs[i], cut_sems.at[2 * i]) for i, cut in enumerate(cuts)]
    dk_ref[...] = jnp.zeros_like(dk_ref)
    dv_ref[...] = jnp.zeros_like(dv_ref)

    def job(i, first, n, order):
        heads = first == 2 * rows
        part = pl.ds(first - rows, n)
        loads[i].wait()
        if not heads:
            swaps[i].wait_recv()

            def add(j, carry):
                u = first - rows + j // SIZES["z"]
                z = lax.rem(j, SIZES["z"])
                acc_ref[u, z] = (acc_ref[u, z].astype(F32) + core_ref[u, z].astype(F32)).astype(BF16)
                return carry

            lax.fori_loop(0, n * SIZES["z"], add, 0)

        def view(sel):
            return pick(acc_ref, [part], sel, ZYX)

        yield from scatter_steps(links, order, view, view, slot_refs[3 * i : 3 * i + 3], lambda: None)
        for u in range(n):
            piece = acc_ref[(first - rows + u, *own)]
            row = links.core * (rows // 2) + (first - rows + u) // 2
            if heads:
                dh_ref[u] = piece
            elif u % 2 == 0:
                dk_ref[row] = turn(piece.astype(F32), cos_ref[...], -sin_ref[...]).astype(BF16)
            else:
                dv_ref[row] = piece

    def query_part(first):
        part = pl.ds(first, chunk)
        tokens = dq_ref.shape[1]
        cos = jnp.concatenate([cos_ref[...]] * chunk, axis=0)
        sin = jnp.concatenate([sin_ref[...]] * chunk, axis=0)
        da, db = query_grad_rows(dq_ref[part].reshape(chunk * tokens, -1), aq_ref[part].reshape(chunk * tokens, -1),
                                 bq_ref[part].reshape(chunk * tokens, -1), eq_ref, cos, sin)
        da_ref[part] = da.reshape(chunk, tokens, -1)
        db_ref[part] = db.reshape(chunk, tokens, -1)
        yield

    waves = in_pairs([job(i, *j) for i, j in enumerate(jobs)])
    at = 0
    for wave, group in zip(waves, groups):
        for cut in group:
            wave.insert(0, cut_job(links, cut, ins[cut.array], outs[cut.array], cut_accs[at], cut_slots[3 * at : 3 * at + 3],
                                   cut_loads[at], cut_sems.at[2 * at + 1]))
            at += 1
    for i, first in enumerate(range(0, dq_ref.shape[0], chunk)):
        waves[min(i, len(waves) - 1)].append(query_part(first))
    run_waves(waves)
    links.finish()


def give_back(dkv, dhd, cos, sin, dq, aq, bq, eq, chunk, named):
    units, length, _ = dkv.shape
    packs = dhd.shape[0]
    rows = units // 2
    tokens = length // math.prod(SIZES.values())
    dims = tuple(SIZES[d] for d in ZYX)
    jobs = collect_jobs(rows, packs)
    slots = [pltpu.VMEM(shape, BF16) for _, n, order in jobs for shape in slot_shapes(order, (n,), (tokens, LANES))]
    arrays = {name: pieces(name, w) for name, w in named.items()}
    groups = weight_cuts({name: w.shape for name, w in arrays.items()})
    cuts = [cut for group in groups for cut in group]
    copies = 8 * len(jobs) + 10 * len(cuts)
    vmem, any_space = pl.BlockSpec(memory_space=pltpu.VMEM), pl.BlockSpec(memory_space=pl.ANY)
    outs = pl.pallas_call(
        functools.partial(return_kernel, rows, packs, chunk, groups, len(arrays)),
        out_shape=[
            jax.ShapeDtypeStruct((rows, tokens, LANES), BF16),
            jax.ShapeDtypeStruct((rows, tokens, LANES), BF16),
            jax.ShapeDtypeStruct((packs, tokens, LANES), BF16),
            jax.ShapeDtypeStruct(aq.shape, BF16),
            jax.ShapeDtypeStruct(bq.shape, BF16),
            *[jax.ShapeDtypeStruct(w.shape, BF16) for w in arrays.values()],
        ],
        in_specs=[any_space] * 2 + [vmem] * 6 + [any_space] * len(arrays),
        out_specs=[vmem] * 5 + [any_space] * len(arrays),
        scratch_shapes=[pltpu.VMEM((rows + packs, *dims, tokens, LANES), BF16), pltpu.VMEM((rows, *dims, tokens, LANES), BF16),
                        *slots, *[pltpu.VMEM(cut.acc_shape(), BF16) for cut in cuts],
                        *[pltpu.VMEM(shape, BF16) for cut in cuts for shape in cut.slots()],
                        pltpu.SemaphoreType.DMA((8,)), pltpu.SemaphoreType.DMA((2 * len(cuts),)),
                        pltpu.SemaphoreType.DMA((copies,)), pltpu.SemaphoreType.DMA((copies,))],
        compiler_params=pltpu.CompilerParams(collective_id=2, has_side_effects=True, vmem_limit_bytes=48 * 2**20),
        name="give_back",
    )(dkv.reshape(units, *dims, tokens, LANES), dhd.reshape(packs, *dims, tokens, LANES), cos, sin, dq, aq, bq, eq,
      *arrays.values())
    return outs[:5], [o.reshape(w.shape) for o, w in zip(outs[5:], named.values())]


def pair_kernel(x_ref, out_ref, got_ref, send_sems, recv_sems):
    links = Links(send_sems, recv_sems)
    links.greet(core=True, chips=False)
    copies = [links.send(x_ref.at[r], got_ref.at[r], links.other_core()) for r in range(x_ref.shape[0])]
    for r, copy in enumerate(copies):
        copy.wait_recv()
        out_ref[r] = (x_ref[r].astype(F32) + got_ref[r].astype(F32)).astype(out_ref.dtype)
    links.finish()


def pair_sum(x, ident):
    parts = 4
    rows, tokens, model = x.shape
    flat = x.reshape(parts, rows * tokens // parts, model)
    return pl.pallas_call(
        pair_kernel,
        out_shape=jax.ShapeDtypeStruct(flat.shape, BF16),
        in_specs=[pl.BlockSpec(memory_space=pltpu.VMEM)],
        out_specs=pl.BlockSpec(memory_space=pltpu.VMEM),
        scratch_shapes=[pltpu.VMEM(flat.shape, BF16), pltpu.SemaphoreType.DMA((parts,)), pltpu.SemaphoreType.DMA((parts,))],
        compiler_params=pltpu.CompilerParams(collective_id=ident, has_side_effects=True, vmem_limit_bytes=32 * 2**20),
        name="pair_sum_%d" % ident,
    )(flat).reshape(x.shape)


class Cut:
    def __init__(self, array, axes, rows, cols, order, lane_dim=None, shared=False):
        self.array, self.axes, self.rows, self.cols = array, axes, rows, cols
        self.order, self.lane_dim, self.shared = order, lane_dim, shared

    def tail(self):
        return (self.rows[1], self.cols[1])

    def view(self, ref, sel, core):
        cols = pl.ds(self.cols[0], self.cols[1])
        if self.lane_dim is not None:
            cols = pl.ds(pl.multiple_of(self.cols[0] + sel[self.lane_dim] * self.cols[1], LANES), self.cols[1])
        lead = [core] if self.shared else []
        return pick(ref, lead, sel, self.axes, (pl.ds(self.rows[0], self.rows[1]), cols))

    def inner(self):
        return tuple(d for d in self.axes if d != self.order[0])

    def acc_shape(self):
        return (*[SIZES[d] for d in self.inner()], *self.tail())

    def slots(self):
        shapes, open_dims = [], list(self.inner())
        for d in self.order:
            if d in open_dims:
                open_dims.remove(d)
            shapes.append((SIZES[d] - 1, *[SIZES[e] for e in open_dims], *self.tail()))
        return shapes


def weight_cuts(shapes):
    a, b, c, d = ("x", "y", "z"), ("y", "x", "z"), ("x", "z", "y"), ("y", "z", "x")
    groups = []
    index = {name: i for i, name in enumerate(shapes)}
    axes = ("x", "y", "z")
    if "down" in shapes:
        n, cols = shapes["down"][2:]
        groups.append([Cut(index["down"], ("y", "z"), (0, n), (0, cols // 4), c, lane_dim="x"),
                       Cut(index["down"], ("x", "z"), (0, n), (cols // 2, cols // 4), d, lane_dim="y")])
    if "out" in shapes:
        n, cols = shapes["out"][3:]
        groups.append([Cut(index["out"], axes, (0, n), (0, cols // 2), a), Cut(index["out"], axes, (0, n), (cols // 2, cols // 2), b)])
    if "small" in shapes:
        m, wide = shapes["small"][3:]
        groups.append([Cut(index["small"], ("y", "z", "x"), (0, m), (0, wide), a)])
    if "basis" in shapes:
        n, cols = shapes["basis"][4:]
        cut = cols // LANES // 2 * LANES
        groups[-1] += [Cut(index["basis"], axes, (0, n), (0, cut), a, shared=True),
                       Cut(index["basis"], axes, (0, n), (cut, cols - cut), b, shared=True)]
    return groups


def pieces(name, w):
    dims = (2, 2, 4)
    chips = math.prod(SIZES.values())
    if name == "basis":
        return w.reshape(CORES, *dims, w.shape[0] // CORES // chips, w.shape[1])
    if name == "down":
        return w.reshape(2, 4, -1, w.shape[1])
    if name == "small":
        return w.reshape(2, 4, 2, -1, LANES)
    return w.reshape(*dims, w.shape[0] // chips, w.shape[1])


def start_load(links, cut, ref, acc, sem):
    if cut.shared:
        return None
    load = pltpu.make_async_copy(cut.view(ref, {cut.order[0]: links.at[cut.order[0]]}, links.core), acc, sem)
    load.start()
    return load


def cut_job(links, cut, in_ref, out_ref, acc_ref, slots, load, store_sem, shared_ref=None):
    def acc(sel):
        return pick(acc_ref, [], sel, cut.inner())

    def source(sel):
        return cut.view(in_ref, sel, links.core)

    def out(sel):
        return cut.view(out_ref, sel, links.core)

    if cut.shared:
        cols = pl.ds(cut.cols[0], cut.cols[1])
        summed = pick(shared_ref, [], {cut.order[0]: links.at[cut.order[0]]}, cut.axes, (slice(None), cols))

        def keep(j, carry):
            p, q = j // acc_ref.shape[1], lax.rem(j, acc_ref.shape[1])
            acc_ref[p, q] = summed[p, q]
            return carry

        lax.fori_loop(0, acc_ref.shape[0] * acc_ref.shape[1], keep, 0)

        def source(sel):
            return pick(shared_ref, [], sel, cut.axes, (slice(None), cols))

    yield from scatter_steps(links, cut.order, source, acc, slots, load.wait if load is not None else lambda: None)
    piece = acc({d: links.at[d] for d in cut.inner()})
    store = pltpu.make_async_copy(piece, out(links.at), store_sem)
    store.start()
    steps = gather_steps(links, cut.order, out, piece)
    next(steps)
    yield
    store.wait()
    yield from steps


def weight_kernel(groups, count, basis, *refs):
    jobs = [cut for group in groups for cut in group]
    ins, outs = refs[:count], refs[count : 2 * count]
    at = 2 * count
    accs = refs[at : at + len(jobs)]
    at += len(jobs)
    slots = refs[at : at + 3 * len(jobs)]
    at += 3 * len(jobs)
    shared_own, shared_got, local_sems, send_sems, recv_sems = refs[at:]
    links = Links(send_sems, recv_sems)
    links.greet(core=True)
    loads = [start_load(links, cut, ins[cut.array], accs[i], local_sems.at[2 * i]) for i, cut in enumerate(jobs)]
    own = pltpu.make_async_copy(ins[basis].at[links.core], shared_own, local_sems.at[2 * len(jobs)])
    own.start()
    swap = links.send(ins[basis].at[1 - links.core], shared_got, links.other_core())

    def first_shared():
        own.wait()
        swap.wait_recv()

        def add(j, carry):
            shape = shared_own.shape
            p, q, r = j // (shape[1] * shape[2]), lax.rem(j // shape[2], shape[1]), lax.rem(j, shape[2])
            shared_own[p, q, r] = (shared_own[p, q, r].astype(F32) + shared_got[p, q, r].astype(F32)).astype(BF16)
            return carry

        lax.fori_loop(0, math.prod(shared_own.shape[:3]), add, 0)
        return
        yield

    made, i, ready = [], 0, False
    for group in groups:
        lot = []
        for cut in group:
            if cut.shared and not ready:
                lot.append(first_shared())
                ready = True
            lot.append(cut_job(links, cut, ins[cut.array], outs[cut.array], accs[i], slots[3 * i : 3 * i + 3], loads[i],
                               local_sems.at[2 * i + 1], shared_own))
            i += 1
        made.append(lot)
    run_waves(made)
    last = links.send(outs[basis].at[links.core], outs[basis].at[links.core], links.other_core())
    last.wait_recv()
    links.finish()


def weight_sums(named):
    arrays = {name: pieces(name, w) for name, w in named.items()}
    groups = weight_cuts({name: w.shape for name, w in arrays.items()})
    jobs = [cut for group in groups for cut in group]
    accs = [pltpu.VMEM(cut.acc_shape(), BF16) for cut in jobs]
    slots = [pltpu.VMEM(shape, BF16) for cut in jobs for shape in cut.slots()]
    copies = 10 * len(jobs) + 4
    any_space = pl.BlockSpec(memory_space=pl.ANY)
    shared = arrays["basis"].shape[1:]
    outs = pl.pallas_call(
        functools.partial(weight_kernel, groups, len(arrays), list(arrays).index("basis")),
        out_shape=[jax.ShapeDtypeStruct(w.shape, BF16) for w in arrays.values()],
        in_specs=[any_space] * len(arrays),
        out_specs=[any_space] * len(arrays),
        scratch_shapes=[*accs, *slots, pltpu.VMEM(shared, BF16), pltpu.VMEM(shared, BF16),
                        pltpu.SemaphoreType.DMA((2 * len(jobs) + 1,)), pltpu.SemaphoreType.DMA((copies,)),
                        pltpu.SemaphoreType.DMA((copies,))],
        compiler_params=pltpu.CompilerParams(collective_id=3, has_side_effects=True, vmem_limit_bytes=48 * 2**20),
        name="weight_sums",
    )(*arrays.values())
    return [o.reshape(w.shape) for o, w in zip(outs, named.values())]


def norm_back(inputs, row_scale, gain_vec, grad_rows):
    weighted = grad_rows * gain_vec
    cubed = row_scale * row_scale * row_scale
    input_part = row_scale * weighted - inputs * cubed * jnp.mean(inputs * weighted, axis=-1, keepdims=True)
    gain_part = jnp.sum(grad_rows * inputs * row_scale, axis=(0, 1))
    return (input_part, gain_part)


def project(activations, weight):
    return jnp.einsum("rsd,de->rse", activations, weight, preferred_element_type=F32)


def back_project(grad_rows, weight):
    return jnp.einsum("rse,de->rsd", grad_rows, weight, preferred_element_type=F32)


def weight_grad(normed, grad_rows):
    return jnp.einsum("rsd,rse->de", normed, grad_rows, preferred_element_type=F32)


def head_sum(partial, ident):
    if on_known_slice():
        return pair_sum(partial.astype(BF16), ident).astype(F32)
    return lax.psum(partial.astype(BF16), "head").astype(F32)


def rms_scale(tensor):
    return lax.rsqrt(jnp.mean(tensor * tensor, axis=-1, keepdims=True) + EPS)


def query_table(head_count):
    hd = head_count * DH
    factor = jnp.arange(head_count * RQ, dtype=jnp.int32)[:, None]
    col = jnp.arange(RQ * hd, dtype=jnp.int32)[None, :]
    return jnp.where(factor == col % hd // DH * RQ + col // hd, 1.0, 0.0).astype(BF16)


def rope_tables(position):
    half = DH // 2
    frequency = jnp.exp(jnp.arange(half).astype(F32) * (-2.0 * math.log(10000.0) / DH))
    angles = position[:, None] * frequency[None, :]
    cos, sin = jnp.cos(angles), jnp.sin(angles)
    return jnp.concatenate([cos] * 4, axis=1), jnp.concatenate([-sin, sin, -sin, sin], axis=1)


def shards(
    block_input,
    seq_lengths,
    attn_gain,
    query_heads,
    query_basis,
    key_heads,
    key_basis,
    value_heads,
    value_basis,
    out_project,
    ffn_gain,
    gate_weight,
    up_weight,
    down_weight,
    out_cotangent,
):
    row_count, slot_count, model_dim = block_input.shape
    head_count = query_heads.shape[1] // RQ
    hd = head_count * DH
    length = slot_count * lax.axis_size("seq")
    first_slot = lax.axis_index("seq") * slot_count
    width = head_count * (RK + RV)
    pack_rows = max(n for n in range(1, row_count + 1) if row_count % n == 0 and n * width <= LANES)
    group = min(4, head_count)
    block = math.gcd(length, KEY_BLOCK)
    query_spread = query_table(head_count)
    cos, sin = rope_tables((first_slot + jnp.arange(slot_count, dtype=jnp.int32)).astype(F32))
    both = jnp.concatenate([key_heads, value_heads], axis=1)
    packed = jnp.concatenate([both] * pack_rows + [jnp.zeros((model_dim, LANES - width * pack_rows), BF16)], axis=1)
    normed, aq, bq, queries, own_kv, own_heads = factors(
        block_input, attn_gain, query_heads, query_basis, key_basis, value_basis, packed, cos, sin, query_spread,
        pack_rows, width)
    inputs = block_input.astype(F32)
    scale_one = rms_scale(inputs)
    if on_known_slice():
        kv = collect(own_kv, own_heads)
        shift = (1 - lax.axis_index("head")) * (row_count // CORES)
    else:
        kv = lax.all_gather(jnp.concatenate([own_kv, own_heads], axis=0), "seq", axis=1, tiled=True)
        shift = jnp.zeros((), jnp.int32)
    info = jnp.stack([*[seq_lengths[r] for r in range(row_count)], shift, first_slot]).astype(jnp.int32)
    attended, mixed_flat, lse = attend(info, queries, kv, pack_rows, group, block, width)
    attn_out = head_sum(project(mixed_flat, out_project), 4)
    middle = inputs + attn_out
    scale_two = rms_scale(middle)
    normed_two = (middle * scale_two * ffn_gain).astype(BF16)
    gate_act = project(normed_two, gate_weight)
    up_act = project(normed_two, up_weight)
    sigmoid_gate = jax.nn.sigmoid(gate_act)
    silu_gate = gate_act * sigmoid_gate
    hidden = (silu_gate * up_act).astype(BF16)
    ffn_out = head_sum(project(hidden, down_weight), 5)
    block_output = (middle + ffn_out).astype(BF16)
    cotangent = out_cotangent.astype(F32)
    down_grad = jnp.einsum("rsf,rsd->fd", hidden, out_cotangent, preferred_element_type=F32)
    d_hidden = jnp.einsum("rsd,fd->rsf", out_cotangent, down_weight, preferred_element_type=F32)
    d_gate = (d_hidden * up_act * (sigmoid_gate * (1.0 + gate_act * (1.0 - sigmoid_gate)))).astype(BF16)
    d_up = (d_hidden * silu_gate).astype(BF16)
    gate_grad = weight_grad(normed_two, d_gate)
    up_grad = weight_grad(normed_two, d_up)
    d_normed_two = head_sum(back_project(d_gate, gate_weight) + back_project(d_up, up_weight), 6)
    d_middle_norm, ffn_gain_part = norm_back(middle, scale_two, ffn_gain, d_normed_two)
    d_middle = cotangent + d_middle_norm
    d_branch = d_middle.astype(BF16)
    out_project_grad = jnp.einsum("rsf,rsd->fd", mixed_flat, d_branch, preferred_element_type=F32)
    d_mixed = back_project(d_branch, out_project).astype(BF16)
    d_queries, d_kv, d_heads = attend_back(info, queries, kv, attended, d_mixed, lse, pack_rows, group, block, width)
    packs = row_count // pack_rows
    model_cut = model_dim // 2
    if on_known_slice():
        (dk_basis, dv_basis, d_heads_own, dq_heads, dq_basis), (down_right, out_project_grad) = give_back(
            d_kv, d_heads, cos, sin, d_queries, aq, bq, query_spread, pack_rows,
            {"down": down_grad[:, model_cut:].astype(BF16), "out": out_project_grad.astype(BF16)})
    else:
        dq_heads, dq_basis = query_grads(d_queries, aq, bq, query_spread, cos, sin, pack_rows)
        key_grads = lax.psum_scatter(
            jnp.concatenate([d_kv, d_heads], axis=0), "seq", scatter_dimension=1, tiled=True)
        d_kv_own = key_grads[: 2 * row_count].reshape(row_count, 2, slot_count, LANES)
        half = DH // 2
        pairs = d_kv_own[:, 0].astype(F32).reshape(row_count, slot_count, 2, 2, half)
        u, w = pairs[:, :, :, 0], pairs[:, :, :, 1]
        c, s = cos[None, :, None, :half], sin[None, :, None, half:DH]
        dk_basis = jnp.stack([u * c + w * s, w * c - u * s], axis=3).reshape(row_count, slot_count, LANES).astype(BF16)
        dv_basis = d_kv_own[:, 1]
        d_heads_own = key_grads[2 * row_count :]
    d_heads_own = d_heads_own[:, :, : width * pack_rows].reshape(packs, slot_count, pack_rows, width)
    d_heads_own = jnp.transpose(d_heads_own, (0, 2, 1, 3)).reshape(row_count, slot_count, width)
    dk_heads, dv_heads = d_heads_own[..., : head_count * RK], d_heads_own[..., head_count * RK :]
    d_normed = head_sum(
        back_project(dq_heads, query_heads) + back_project(dq_basis, query_basis)
        + back_project(dk_heads, key_heads) + back_project(dk_basis, key_basis)
        + back_project(dv_heads, value_heads) + back_project(dv_basis, value_basis), 7)
    d_input_norm, attn_gain_part = norm_back(inputs, scale_one, attn_gain, d_normed)
    input_grad = d_middle + d_input_norm
    head_grads = weight_grad(jnp.concatenate([dq_heads, dk_heads, dv_heads], axis=-1), normed)
    basis_grads = weight_grad(normed, jnp.concatenate([dq_basis, dk_basis, dv_basis], axis=-1))
    small = jnp.concatenate([head_grads, attn_gain_part[None], ffn_gain_part[None]], axis=0).astype(BF16)
    if on_known_slice():
        gate_grad, up_grad, down_left = [
            t.astype(F32) for t in lax.psum(tuple(t.astype(BF16) for t in (gate_grad, up_grad, down_grad[:, :model_cut])), "seq")]
        down_grad = jnp.concatenate([down_left, down_right.astype(F32)], axis=1)
        height = small.shape[0]
        wide = model_dim // LANES
        small = jnp.pad(small, ((0, -height % 32), (0, 0)))
        full = small.shape[0]
        small = jnp.transpose(small.reshape(full, wide, LANES), (1, 0, 2))
        small, basis_grads = weight_sums({"small": small, "basis": basis_grads.astype(BF16)})
        small = jnp.transpose(small, (1, 0, 2)).reshape(full, model_dim)
    else:
        sums = lax.psum(tuple(t.astype(BF16) for t in (gate_grad, up_grad, down_grad, out_project_grad, small)), "seq")
        gate_grad, up_grad, down_grad, out_project_grad, small = [t.astype(F32) for t in sums]
        basis_grads = lax.psum(basis_grads, ("seq", "head"))
    nq, nk, nv = head_count * RQ, head_count * RK, head_count * RV
    cuts = (0, nq, nq + nk, nq + nk + nv)
    query_heads_grad, key_heads_grad, value_heads_grad = [small[i:j].astype(F32).T for i, j in zip(cuts, cuts[1:])]
    cuts = (0, RQ * DH, (RQ + RK) * DH, (RQ + RK + RV) * DH)
    query_basis_grad, key_basis_grad, value_basis_grad = [basis_grads[:, i:j].astype(F32) for i, j in zip(cuts, cuts[1:])]
    return (
        block_output,
        input_grad,
        small[nq + nk + nv].astype(F32),
        query_heads_grad,
        query_basis_grad,
        key_heads_grad,
        key_basis_grad,
        value_heads_grad,
        value_basis_grad,
        out_project_grad.astype(F32),
        small[nq + nk + nv + 1].astype(F32),
        gate_grad,
        up_grad,
        down_grad,
    )


def solution(mesh):
    rows = P(None, "seq", None)
    columns, features = P(None, "head"), P("head", None)
    in_specs = (rows, P(), P(), columns, P(), columns, P(), columns, P(), features, P(), columns, columns, features, rows)
    out_specs = (rows, rows, P(), columns, P(), columns, P(), columns, P(), features, P(), columns, columns, features)
    return jax.shard_map(shards, mesh=mesh, in_specs=in_specs, out_specs=out_specs, check_vma=False)
```

```python
import functools
import math

import jax
import jax.numpy as jnp
from jax import lax
from jax.experimental import pallas as pl
from jax.experimental.pallas import tpu as pltpu
from jax.sharding import PartitionSpec as P

DH = 64
RQ = 6
RK = 2
RV = 2
LANES = 128
EPS = 1e-06
KEY_BLOCK = 256
F32 = jnp.float32
BF16 = jnp.bfloat16


def dot(a, b):
    return lax.dot_general(a, b, (((1,), (0,)), ((), ())), preferred_element_type=F32)


def dot_nt(a, b):
    return lax.dot_general(a, b, (((1,), (1,)), ((), ())), preferred_element_type=F32)


def dot_tn(a, b):
    return lax.dot_general(a, b, (((0,), (0,)), ((), ())), preferred_element_type=F32)


def lane_of(shape):
    return lax.broadcasted_iota(jnp.int32, shape, len(shape) - 1)


def both_halves(pair):
    swapped = pltpu.roll(pair, DH, 1)
    low = lane_of(pair.shape) < DH
    return jnp.where(low, pair, swapped), jnp.where(low, swapped, pair)


def turn(pair, cos, sin):
    half = DH // 2
    first = lane_of(pair.shape) % DH < half
    other = jnp.where(first, pltpu.roll(pair, LANES - half, 1), pltpu.roll(pair, half, 1))
    return pair * cos + other * sin


def split_heads(rows, head_rows, tokens):
    group = lane_of(rows.shape) // DH
    return jnp.concatenate([jnp.where(group == h, rows, jnp.zeros_like(rows)) for h in range(head_rows)], axis=0)


def join_heads(block, head_rows, tokens):
    out = block[:tokens]
    group = lane_of(out.shape) // DH
    for h in range(1, head_rows):
        out = jnp.where(group == h, block[h * tokens : (h + 1) * tokens], out)
    return out


def query_rows(aq, bq, eq_ref, hd):
    aq_high = aq.astype(BF16)
    aq_low = (aq - aq_high.astype(F32)).astype(BF16)
    total = [None] * (hd // LANES)
    for p in range(RQ // 2):
        for half, vec in enumerate(both_halves(bq[:, p * LANES : (p + 1) * LANES])):
            spread = eq_ref[:, (2 * p + half) * hd : (2 * p + half + 1) * hd]
            coef = dot(aq_high, spread) + dot(aq_low, spread)
            for c in range(hd // LANES):
                term = coef[:, c * LANES : (c + 1) * LANES] * vec
                total[c] = term if total[c] is None else total[c] + term
    return [((t / RQ).astype(BF16).astype(F32) * (1.0 / math.sqrt(DH))).astype(BF16) for t in total]


def factor_kernel(width, with_queries, x_ref, gain_ref, wqh_ref, wqb_ref, wkb_ref, wvb_ref, wkh_ref, wvh_ref, cos_ref, sin_ref,
                  eq_ref, xn_ref, aq_ref, bq_ref, kv_ref, hd_ref, *q_refs):
    rows, tokens, model = x_ref.shape
    count = rows * tokens
    x = x_ref[...].astype(F32).reshape(count, model)
    scale = lax.rsqrt(jnp.mean(x * x, axis=-1, keepdims=True) + EPS)
    xn = (x * scale * gain_ref[...]).astype(BF16)
    xn_ref[...] = xn.reshape(rows, tokens, model)
    cos = jnp.concatenate([cos_ref[...]] * rows, axis=0)
    sin = jnp.concatenate([sin_ref[...]] * rows, axis=0)
    keys = turn(dot(xn, wkb_ref[...]), cos, sin).astype(BF16)
    values = dot(xn, wvb_ref[...]).astype(BF16)
    coefs = [dot_nt(xn, w_ref[...]).astype(BF16) for w_ref in (wkh_ref, wvh_ref)]
    pack = jnp.zeros((tokens, LANES), F32)
    for r in range(rows):
        part = slice(r * tokens, (r + 1) * tokens)
        kv_ref[2 * r] = keys[part]
        kv_ref[2 * r + 1] = values[part]
        at = r * width
        for coef in coefs:
            n = coef.shape[1]
            to = lane_of((n, LANES)) == lax.broadcasted_iota(jnp.int32, (n, LANES), 0) + at
            pack = pack + dot(coef[part], jnp.where(to, 1.0, 0.0).astype(BF16))
            at += n
    hd_ref[0] = pack.astype(BF16)
    aq = dot_nt(xn, wqh_ref[...])
    aq_ref[...] = aq.reshape(rows, tokens, aq.shape[1])
    basis = dot(xn, wqb_ref[...])
    bq = jnp.concatenate([turn(basis[:, p : p + LANES], cos, sin) for p in range(0, RQ * DH, LANES)], axis=1)
    bq_ref[...] = bq.reshape(rows, tokens, RQ * DH)
    if with_queries:
        for c, q in enumerate(query_rows(aq, bq, eq_ref, q_refs[0].shape[2])):
            q_refs[0][:, :, c * LANES : (c + 1) * LANES] = q.reshape(rows, tokens, LANES)


def whole(*shape):
    return pl.BlockSpec(shape, lambda *_: (0,) * len(shape))


def factors(x, gain, wqh, wqb, wkb, wvb, wkh, wvh, cos, sin, eq, pack_rows, width, with_queries):
    rows, tokens, model = x.shape
    hd = eq.shape[1] // RQ
    packs = rows // pack_rows
    nq = wqh.shape[0]

    def row_block(last):
        return pl.BlockSpec((pack_rows, tokens, last), lambda g: (g, 0, 0))

    out_specs = [row_block(model), row_block(nq), row_block(RQ * DH),
                 pl.BlockSpec((2 * pack_rows, tokens, LANES), lambda g: (g, 0, 0)),
                 pl.BlockSpec((1, tokens, LANES), lambda g: (g, 0, 0))]
    out_shape = [
        jax.ShapeDtypeStruct((rows, tokens, model), BF16),
        jax.ShapeDtypeStruct((rows, tokens, nq), F32),
        jax.ShapeDtypeStruct((rows, tokens, RQ * DH), F32),
        jax.ShapeDtypeStruct((2 * rows, tokens, LANES), BF16),
        jax.ShapeDtypeStruct((packs, tokens, LANES), BF16),
    ]
    if with_queries:
        out_specs.append(row_block(hd))
        out_shape.append(jax.ShapeDtypeStruct((rows, tokens, hd), BF16))
    return pl.pallas_call(
        functools.partial(factor_kernel, width, with_queries),
        grid=(packs,),
        in_specs=[row_block(model), whole(1, model), *[whole(*w.shape) for w in (wqh, wqb, wkb, wvb, wkh, wvh, cos, sin, eq)]],
        out_specs=out_specs,
        out_shape=out_shape,
        compiler_params=pltpu.CompilerParams(vmem_limit_bytes=32 * 2**20),
        name="factors",
    )(x, gain.reshape(1, model), wqh, wqb, wkb, wvb, wkh, wvh, cos, sin, eq)


def query_grad_rows(dq, aq, bq, eq_ref, cos, sin):
    hd = dq.shape[1]
    aq_high = aq.astype(BF16)
    aq_low = (aq - aq_high.astype(F32)).astype(BF16)
    da = jnp.zeros(aq.shape, F32)
    low = lane_of((dq.shape[0], LANES)) < DH
    turned = []
    for p in range(RQ // 2):
        sums = []
        for half, vec in enumerate(both_halves(bq[:, p * LANES : (p + 1) * LANES])):
            spread = eq_ref[:, (2 * p + half) * hd : (2 * p + half + 1) * hd]
            coef = dot(aq_high, spread) + dot(aq_low, spread)
            acc = None
            prods = []
            for c in range(hd // LANES):
                part = dq[:, c * LANES : (c + 1) * LANES]
                term = coef[:, c * LANES : (c + 1) * LANES] * part
                acc = term if acc is None else acc + term
                prods.append(part * vec)
            prod = jnp.concatenate(prods, axis=1)
            high = prod.astype(BF16)
            rest = (prod - high.astype(F32)).astype(BF16)
            da = da + dot_nt(high, spread) + dot_nt(rest, spread)
            sums.append(acc + pltpu.roll(acc, DH, 1))
        turned.append(turn(jnp.where(low, sums[0], sums[1]), cos, -sin) * (1.0 / RQ))
    return (da * (1.0 / RQ)).astype(BF16), jnp.concatenate(turned, axis=1).astype(BF16)


def query_grad_kernel(dq_ref, aq_ref, bq_ref, eq_ref, cos_ref, sin_ref, da_ref, db_ref):
    rows, tokens, hd = dq_ref.shape
    count = rows * tokens
    da, db = query_grad_rows(
        dq_ref[...].reshape(count, hd), aq_ref[...].reshape(count, -1), bq_ref[...].reshape(count, -1), eq_ref,
        jnp.concatenate([cos_ref[...]] * rows, axis=0), jnp.concatenate([sin_ref[...]] * rows, axis=0))
    da_ref[...] = da.reshape(da_ref.shape)
    db_ref[...] = db.reshape(db_ref.shape)


def query_grads(dq, aq, bq, eq, cos, sin, pack_rows):
    rows, tokens, hd = dq.shape
    nq = aq.shape[2]

    def row_block(last):
        return pl.BlockSpec((pack_rows, tokens, last), lambda g: (g, 0, 0))

    return pl.pallas_call(
        query_grad_kernel,
        grid=(rows // pack_rows,),
        in_specs=[row_block(hd), row_block(nq), row_block(RQ * DH), whole(*eq.shape), whole(*cos.shape), whole(*sin.shape)],
        out_specs=[row_block(nq), row_block(RQ * DH)],
        out_shape=[jax.ShapeDtypeStruct((rows, tokens, nq), BF16), jax.ShapeDtypeStruct((rows, tokens, RQ * DH), BF16)],
        compiler_params=pltpu.CompilerParams(vmem_limit_bytes=56 * 2**20),
        name="query_grads",
    )(dq, aq, bq, eq, cos, sin)


def key_rows(basis):
    turned = basis.astype(F32).T * 0.5
    return turned[:DH], turned[DH:]


def build_heads(coefs, first, second, head_count):
    return jnp.concatenate(
        [coefs[2 * h : 2 * h + 1] * first + coefs[2 * h + 1 : 2 * h + 2] * second for h in range(head_count)], axis=0
    ).astype(BF16)


def row_limits(info_ref, row, tokens, block, lanes):
    first = info_ref[info_ref.shape[0] - 1]
    length = info_ref[row]
    used = jnp.minimum(length, first + tokens)
    slot = lax.broadcasted_iota(jnp.int32, (lanes, 1), 0) % tokens
    return jnp.minimum(first + slot, length - 1), (used + block - 1) // block


def forward_row(q, read, place, width, limit, blocks, block, group, ct_ref):
    tokens, hd = q.shape
    head_count = hd // DH
    lanes = group * tokens
    wide = group * DH
    groups = hd // wide
    queries = [split_heads(q[:, g * wide : (g + 1) * wide], group, tokens) for g in range(groups)]

    def one(b, carry):
        ct_ref[...] = read(2, b).astype(F32).T
        coefs = ct_ref[pl.ds(place, width), :]
        keys = build_heads(coefs[: RK * head_count], *key_rows(read(0, b)), head_count)
        values = build_heads(coefs[RK * head_count :], *key_rows(read(1, b)), head_count)
        live = b * block + lax.broadcasted_iota(jnp.int32, (1, block), 1) <= limit
        out = []
        for g in range(groups):
            peak, total, mixed = carry[g]
            raw = jnp.where(live, dot(queries[g], keys[g * wide : (g + 1) * wide]), -1e30)
            top = jnp.maximum(peak, jnp.max(raw, axis=1, keepdims=True))
            e = jnp.exp(raw - top)
            keep = jnp.exp(peak - top)
            total = total * keep + jnp.sum(e, axis=1, keepdims=True)
            mixed = mixed * keep + dot_nt(e.astype(BF16), values[g * wide : (g + 1) * wide])
            out.append((top, total, mixed))
        return tuple(out)

    start = (jnp.full((lanes, 1), -1e30, F32), jnp.zeros((lanes, 1), F32), jnp.zeros((lanes, wide), F32))
    done = lax.fori_loop(0, blocks, one, (start,) * groups)
    lane = lane_of((tokens, LANES))
    lse = jnp.zeros((tokens, LANES), F32)
    parts = []
    for g in range(groups):
        peak, total, mixed = done[g]
        parts.append(join_heads(mixed / total, group, tokens))
        level = peak + jnp.log(total)
        for h in range(group):
            lse = jnp.where(lane == g * group + h, level[h * tokens : (h + 1) * tokens], lse)
    return parts, lse


def attend_kernel(pack_rows, group, block, width, info_ref, q_ref, kv_ref, hd_ref, o_ref, ob_ref, lse_ref, ct_ref):
    row = pl.program_id(0)
    _, tokens, hd = q_ref.shape
    wide = group * DH
    limit, blocks = row_limits(info_ref, row, tokens, block, group * tokens)

    def read(i, b):
        at = pl.ds(pl.multiple_of(b * block, block), block)
        return hd_ref[0, at, :] if i == 2 else kv_ref[i, at, :]

    parts, lse_ref[0] = forward_row(
        q_ref[0], read, pl.multiple_of(row % pack_rows * width, 8), width, limit, blocks, block, group, ct_ref)
    for g, mixed in enumerate(parts):
        o_ref[0, :, g * wide : (g + 1) * wide] = mixed
        ob_ref[0, :, g * wide : (g + 1) * wide] = mixed.astype(BF16)


def attend(info, q, kv, pack_rows, group, block, width):
    rows, tokens, hd = q.shape
    length = kv.shape[1]

    def own(r, i):
        return (r, 0, 0)

    grid_spec = pltpu.PrefetchScalarGridSpec(
        num_scalar_prefetch=1,
        grid=(rows,),
        in_specs=[
            pl.BlockSpec((1, tokens, hd), own),
            pl.BlockSpec((2, length, LANES), lambda r, i: (lax.rem(r + i[rows], rows), 0, 0)),
            pl.BlockSpec((1, length, LANES), lambda r, i: (2 * rows + r // pack_rows, 0, 0)),
        ],
        out_specs=[pl.BlockSpec((1, tokens, hd), own), pl.BlockSpec((1, tokens, hd), own), pl.BlockSpec((1, tokens, LANES), own)],
        scratch_shapes=[pltpu.VMEM((LANES, block), F32)],
    )
    return pl.pallas_call(
        functools.partial(attend_kernel, pack_rows, group, block, width),
        grid_spec=grid_spec,
        out_shape=[
            jax.ShapeDtypeStruct((rows, tokens, hd), F32),
            jax.ShapeDtypeStruct((rows, tokens, hd), BF16),
            jax.ShapeDtypeStruct((rows, tokens, LANES), F32),
        ],
        compiler_params=pltpu.CompilerParams(vmem_limit_bytes=32 * 2**20),
        name="attend",
    )(info, q, kv, kv)


def attend_back_kernel(pack_rows, group, block, width, info_ref, q_ref, kv_ref, hd_ref, o_ref, do_ref, lse_ref,
                       dq_ref, dkv_ref, dhd_ref, dq_acc, ct_ref, dct_ref):
    row = pl.program_id(0)
    _, tokens, hd = q_ref.shape
    head_count = hd // DH
    lanes = group * tokens
    wide = group * DH
    groups = hd // wide
    limit, blocks = row_limits(info_ref, row, tokens, block, lanes)
    place = pl.multiple_of(row % pack_rows * width, 8)
    queries, grads, deltas, levels = [], [], [], []
    for g in range(groups):
        part = slice(g * wide, (g + 1) * wide)
        do = do_ref[0, :, part]
        queries.append(split_heads(q_ref[0, :, part], group, tokens))
        grads.append(split_heads(do, group, tokens))
        weighed = split_heads(do.astype(F32) * o_ref[0, :, part], group, tokens)
        deltas.append(jnp.sum(weighed, axis=1, keepdims=True))
        levels.append(jnp.concatenate([lse_ref[0, :, h : h + 1] for h in range(g * group, (g + 1) * group)], axis=0))
    queries_t = [q.astype(F32).T.astype(BF16) for q in queries]
    grads_t = [g.astype(F32).T.astype(BF16) for g in grads]
    dq_acc[...] = jnp.zeros_like(dq_acc)
    dkv_ref[...] = jnp.zeros_like(dkv_ref)
    dct_ref[...] = jnp.zeros_like(dct_ref)

    @pl.when(row % pack_rows == 0)
    def _():
        dhd_ref[...] = jnp.zeros_like(dhd_ref)

    def factor_grads(grad, coefs, vectors):
        sums, rows = [None, None], []
        for h in range(head_count):
            part = grad[h * DH : (h + 1) * DH]
            for r in range(2):
                term = coefs[2 * h + r : 2 * h + r + 1] * part
                sums[r] = term if h == 0 else sums[r] + term
                rows.append(jnp.sum(part * vectors[r], axis=0, keepdims=True))
        return (jnp.concatenate(sums, axis=0) * 0.5).T.astype(BF16), rows

    def one(b, carry):
        at = pl.ds(pl.multiple_of(b * block, block), block)
        ct_ref[...] = hd_ref[0, at, :].astype(F32).T
        coefs = ct_ref[pl.ds(place, width), :]
        key_coefs, value_coefs = coefs[: RK * head_count], coefs[RK * head_count :]
        key_vectors, value_vectors = key_rows(kv_ref[0, at, :]), key_rows(kv_ref[1, at, :])
        keys = build_heads(key_coefs, *key_vectors, head_count)
        values = build_heads(value_coefs, *value_vectors, head_count)
        live = b * block + lax.broadcasted_iota(jnp.int32, (1, block), 1) <= limit
        dks, dvs = [], []
        for g in range(groups):
            part = slice(g * wide, (g + 1) * wide)
            p = jnp.where(live, jnp.exp(dot(queries[g], keys[part]) - levels[g]), 0.0)
            dp = dot(grads[g], values[part])
            ds = (p * (dp - deltas[g])).astype(BF16)
            dvs.append(dot(grads_t[g], p.astype(BF16)))
            dks.append(dot(queries_t[g], ds))
            dq_acc[g] += dot_nt(ds, keys[part])
        dkv_ref[0, at, :], key_grads = factor_grads(jnp.concatenate(dks, axis=0), key_coefs, key_vectors)
        dkv_ref[1, at, :], value_grads = factor_grads(jnp.concatenate(dvs, axis=0), value_coefs, value_vectors)
        dct_ref[pl.ds(place, width), :] = jnp.concatenate(key_grads + value_grads, axis=0)
        dhd_ref[0, at, :] = (dhd_ref[0, at, :].astype(F32) + dct_ref[...].T).astype(BF16)
        return carry

    lax.fori_loop(0, blocks, one, 0)
    for g in range(groups):
        dq_ref[0, :, g * wide : (g + 1) * wide] = join_heads(dq_acc[g], group, tokens) * (1.0 / math.sqrt(DH))


def attend_back(info, q, kv, o, do, lse, pack_rows, group, block, width):
    rows, tokens, hd = q.shape
    length = kv.shape[1]
    packs = rows // pack_rows

    def place(r, i):
        return (lax.rem(r + i[rows], rows), 0, 0)

    def own(r, i):
        return (r, 0, 0)

    grid_spec = pltpu.PrefetchScalarGridSpec(
        num_scalar_prefetch=1,
        grid=(rows,),
        in_specs=[
            pl.BlockSpec((1, tokens, hd), own),
            pl.BlockSpec((2, length, LANES), place),
            pl.BlockSpec((1, length, LANES), lambda r, i: (2 * rows + r // pack_rows, 0, 0)),
            pl.BlockSpec((1, tokens, hd), own),
            pl.BlockSpec((1, tokens, hd), own),
            pl.BlockSpec((1, tokens, LANES), own),
        ],
        out_specs=[
            pl.BlockSpec((1, tokens, hd), own),
            pl.BlockSpec((2, length, LANES), place),
            pl.BlockSpec((1, length, LANES), lambda r, i: (r // pack_rows, 0, 0)),
        ],
        scratch_shapes=[pltpu.VMEM((hd // (group * DH), group * tokens, group * DH), F32),
                        pltpu.VMEM((LANES, block), F32), pltpu.VMEM((LANES, block), F32)],
    )
    return pl.pallas_call(
        functools.partial(attend_back_kernel, pack_rows, group, block, width),
        grid_spec=grid_spec,
        out_shape=[
            jax.ShapeDtypeStruct((rows, tokens, hd), F32),
            jax.ShapeDtypeStruct((2 * rows, length, LANES), BF16),
            jax.ShapeDtypeStruct((packs, length, LANES), BF16),
        ],
        compiler_params=pltpu.CompilerParams(vmem_limit_bytes=32 * 2**20),
        name="attend_back",
    )(info, q, kv, kv, o, do, lse)


MESH = pl.DeviceIdType.MESH
SIZES = {"z": 4, "y": 2, "x": 2}
STRIDES = {"z": 4, "y": 2, "x": 1}
CORES = 2


def on_known_slice():
    return lax.axis_size("seq") == math.prod(SIZES.values()) and lax.axis_size("head") == CORES


class Links:
    def __init__(self, send_sems, recv_sems):
        self.seq = lax.axis_index("seq")
        self.core = lax.axis_index("head")
        self.at = {d: lax.rem(self.seq // STRIDES[d], SIZES[d]) for d in SIZES}
        self.send_sems, self.recv_sems = send_sems, recv_sems
        self.count = 0
        self.started = []

    def along(self, d, offset):
        there = lax.rem(self.at[d] + offset, SIZES[d])
        return there, (self.seq + (there - self.at[d]) * STRIDES[d], self.core)

    def other_core(self):
        return (self.seq, 1 - self.core)

    def greet(self, core, chips=True):
        barrier = pltpu.get_barrier_semaphore()
        devices = [self.other_core()] if core else []
        if chips:
            devices += [self.along(d, o)[1] for d in SIZES for o in range(1, SIZES[d])]
        for device in devices:
            pl.semaphore_signal(barrier, inc=1, device_id=device, device_id_type=MESH)
        pl.semaphore_wait(barrier, len(devices))

    def send(self, src, dst, device):
        copy = pltpu.make_async_remote_copy(
            src_ref=src, dst_ref=dst, send_sem=self.send_sems.at[self.count], recv_sem=self.recv_sems.at[self.count],
            device_id=device, device_id_type=MESH)
        self.count += 1
        copy.start()
        self.started.append(copy)
        return copy

    def finish(self):
        for copy in self.started:
            copy.wait_send()


def accumulate(acc, slots):
    lead = acc.shape[:-2]

    def body(i, carry):
        at = []
        for size in reversed(lead):
            at.insert(0, lax.rem(i, size))
            i = i // size
        value = acc[(*at, slice(None), slice(None))].astype(F32)
        for o in range(slots.shape[0]):
            value = value + slots[(o, *at, slice(None), slice(None))].astype(F32)
        acc[(*at, slice(None), slice(None))] = value.astype(BF16)
        return carry

    lax.fori_loop(0, math.prod(lead), body, 0)


def scatter_steps(links, order, source, acc, slots, ready):
    fixed = {}
    for k, d in enumerate(order):
        copies = []
        for o in range(1, SIZES[d]):
            there, device = links.along(d, o)
            view = source if k == 0 else acc
            copies.append(links.send(view({**fixed, d: there}), slots[k].at[o - 1], device))
        yield
        if k == 0:
            ready()
        for copy in copies:
            copy.wait_recv()
        fixed[d] = links.at[d]
        accumulate(acc(fixed), slots[k])


def gather_steps(links, order, out, first):
    for k in reversed(range(len(order))):
        fixed = {d: links.at[d] for d in order[: k + 1]}
        copies = []
        for o in range(1, SIZES[order[k]]):
            _, device = links.along(order[k], o)
            src = first if first is not None and k == len(order) - 1 else out(fixed)
            copies.append(links.send(src, out(fixed), device))
        yield
        for copy in copies:
            copy.wait_recv()


def run_waves(groups):
    live, waiting = [], list(groups)
    while live or waiting:
        if waiting:
            live.append(list(waiting.pop(0)))
        for group in live:
            group[:] = [job for job in group if next(job, "end") != "end"]
        live = [group for group in live if group]


def in_pairs(jobs):
    half = (len(jobs) + 1) // 2
    return [jobs[i : i + 1] + jobs[half + i : half + i + 1] for i in range(half)]


def slot_shapes(order, units, tail):
    shapes, open_dims = [], list(SIZES)
    for d in order:
        open_dims.remove(d)
        shapes.append((SIZES[d] - 1, *units, *[SIZES[e] for e in open_dims], *tail))
    return shapes


def pick(ref, lead, sel, axes, tail=()):
    return ref.at[(*lead, *[sel.get(d, slice(None)) for d in axes], *tail)]


ZYX = ("z", "y", "x")


def collect_jobs(rows, packs):
    step = 1
    own = [(rows + u, min(step, rows - u)) for u in range(0, rows, step)]
    jobs = own + [(2 * rows, packs)]
    half = (len(jobs) + 1) // 2
    return [(first, n, ("y", "x", "z") if i < half else ("x", "y", "z")) for i, (first, n) in enumerate(jobs)]


def collect_groups(rows, packs):
    half = rows // CORES
    lots = [[0]] + [list(range(j, min(j + 2, half))) for j in range(1, half, 2)]
    return [([(2 * rows, packs)] if i == 0 else []) + [(rows + 2 * j, 2) for j in lot] for i, lot in enumerate(lots)], lots


def collect_kernel(pack_rows, group, block, width, len_ref, kv_ref, hd_ref, aq_ref, bq_ref, eq_ref, out_ref, o_ref, ob_ref, lse_ref,
                   q_ref, all_ref, ct_ref, local_sems, out_sems, send_sems, recv_sems):
    rows, tokens, hd = q_ref.shape
    packs = hd_ref.shape[0]
    half = rows // CORES
    wide = group * DH
    planes = block // (SIZES["y"] * SIZES["x"] * tokens)
    links = Links(send_sems, recv_sems)
    own = tuple(links.at[d] for d in ZYX)
    first_slot = links.seq * tokens
    blocks = (first_slot + tokens + block - 1) // block
    groups, lots = collect_groups(rows, packs)
    jobs = [job for lot in groups for job in lot]
    loads = []
    for i, (first, n) in enumerate(jobs):
        src = hd_ref if first == 2 * rows else kv_ref.at[pl.ds(links.core * rows + first - rows, n)]
        loads.append(pltpu.make_async_copy(src, all_ref.at[(pl.ds(first, n), *own)], local_sems.at[i]))
        loads[-1].start()
    links.greet(core=True)
    stores = []

    def keep(first, n):
        store = pltpu.make_async_copy(all_ref.at[pl.ds(first, n)], out_ref.at[pl.ds(first, n)], out_sems.at[len(stores)])
        store.start()
        stores.append(store)

    def job(i, first, n):
        order = ("x", "y", "z") if i % 2 else ("y", "x", "z")
        loads[i].wait()
        yield from gather_steps(links, order, lambda sel: pick(all_ref, [pl.ds(first, n)], sel, ZYX), None)
        if first < 2 * rows:
            copy = links.send(all_ref.at[pl.ds(first, n)], all_ref.at[pl.ds(first - rows, n)], links.other_core())
        keep(first, n)
        if first < 2 * rows:
            yield
            copy.wait_recv()
            keep(first - rows, n)

    def attend_rows(mine, lot):
        def body(i, carry):
            j = lot[0] + i
            row = j + half * (links.core if mine else 1 - links.core)
            unit = rows * mine + 2 * j
            slot = lax.broadcasted_iota(jnp.int32, (group * tokens, 1), 0) % tokens
            limit = jnp.minimum(first_slot + slot, len_ref[row] - 1)
            pack = row // pack_rows
            place = pl.multiple_of((row - pack * pack_rows) * width, 8)

            def read(k, b):
                at = 2 * rows + pack if k == 2 else unit + k
                return all_ref[at, pl.ds(b * planes, planes)].reshape(block, LANES)

            parts, lse_ref[row] = forward_row(q_ref[row], read, place, width, limit, blocks, block, group, ct_ref)
            for g, mixed in enumerate(parts):
                o_ref[row, :, g * wide : (g + 1) * wide] = mixed
                ob_ref[row, :, g * wide : (g + 1) * wide] = mixed.astype(BF16)
            return carry

        lax.fori_loop(0, len(lot), body, 0)

    live, started, wave, i = [], 0, 0, 0
    steps = 3
    while started < len(groups) or live:
        if started < len(groups):
            for first, n in groups[started]:
                live.append(job(i, first, n))
                i += 1
            started += 1
        live[:] = [made for made in live if next(made, "end") != "end"]
        if 0 <= wave - steps - 1 < len(lots):
            attend_rows(0, lots[wave - steps - 1])
        if 0 <= wave - steps < len(lots):
            attend_rows(1, lots[wave - steps])
        if wave < packs:
            part = pl.ds(wave * pack_rows, pack_rows)
            flat = pack_rows * tokens
            made = query_rows(aq_ref[part].reshape(flat, -1), bq_ref[part].reshape(flat, -1), eq_ref, hd)
            for c, q in enumerate(made):
                q_ref[part, :, c * LANES : (c + 1) * LANES] = q.reshape(pack_rows, tokens, LANES)
        wave += 1
    for store in stores:
        store.wait()
    links.finish()


def collect(lengths, kv, hd, aq, bq, eq, pack_rows, group, width):
    units, tokens, _ = kv.shape
    packs = hd.shape[0]
    rows = units // 2
    hidden = (rows, tokens, eq.shape[1] // RQ)
    length = tokens * math.prod(SIZES.values())
    block = length // 2
    count = sum(len(lot) for lot in collect_groups(rows, packs)[0])
    full = (units + packs, *[SIZES[d] for d in ZYX], tokens, LANES)
    vmem, any_space = pl.BlockSpec(memory_space=pltpu.VMEM), pl.BlockSpec(memory_space=pl.ANY)
    out, o, ob, lse, q = pl.pallas_call(
        functools.partial(collect_kernel, pack_rows, group, block, width),
        out_shape=[jax.ShapeDtypeStruct(full, BF16), jax.ShapeDtypeStruct(hidden, F32), jax.ShapeDtypeStruct(hidden, BF16),
                   jax.ShapeDtypeStruct((rows, tokens, LANES), F32), jax.ShapeDtypeStruct(hidden, BF16)],
        in_specs=[pl.BlockSpec(memory_space=pltpu.SMEM), any_space, any_space, vmem, vmem, vmem],
        out_specs=[any_space, vmem, vmem, vmem, vmem],
        scratch_shapes=[pltpu.VMEM(full, BF16), pltpu.VMEM((LANES, block), F32), pltpu.SemaphoreType.DMA((count,)),
                        pltpu.SemaphoreType.DMA((2 * count,)), pltpu.SemaphoreType.DMA((8 * count,)),
                        pltpu.SemaphoreType.DMA((8 * count,))],
        compiler_params=pltpu.CompilerParams(collective_id=1, has_side_effects=True, vmem_limit_bytes=32 * 2**20),
        name="collect",
    )(lengths, kv, hd, aq, bq, eq)
    return out.reshape(units + packs, length, LANES), o, ob, lse, q


def return_kernel(rows, packs, chunk, groups, count, dkv_ref, dhd_ref, cos_ref, sin_ref, dq_ref, aq_ref, bq_ref, eq_ref, *refs):
    ins, refs = refs[:count], refs[count:]
    (dk_ref, dv_ref, dh_ref, da_ref, db_ref), refs = refs[:5], refs[5:]
    outs, refs = refs[:count], refs[count:]
    acc_ref, core_ref, refs = refs[0], refs[1], refs[2:]
    jobs = collect_jobs(rows, packs)
    slot_refs, refs = refs[: 3 * len(jobs)], refs[3 * len(jobs) :]
    cuts = [cut for group in groups for cut in group]
    cut_accs, cut_slots, refs = refs[: len(cuts)], refs[len(cuts) : 4 * len(cuts)], refs[4 * len(cuts) :]
    local_sems, cut_sems, send_sems, recv_sems = refs
    links = Links(send_sems, recv_sems)
    links.greet(core=True)
    own = tuple(links.at[d] for d in ZYX)
    loads, swaps = [], []
    for i, (first, n, _) in enumerate(jobs):
        heads = first == 2 * rows
        part = pl.ds(first - rows, n)
        if not heads:
            swaps.append(links.send(dkv_ref.at[part], core_ref.at[part], links.other_core()))
        load = pltpu.make_async_copy(dhd_ref if heads else dkv_ref.at[pl.ds(first, n)], acc_ref.at[part], local_sems.at[i])
        load.start()
        loads.append(load)
    cut_loads = [start_load(links, cut, ins[cut.array], cut_accs[i], cut_sems.at[2 * i]) for i, cut in enumerate(cuts)]
    dk_ref[...] = jnp.zeros_like(dk_ref)
    dv_ref[...] = jnp.zeros_like(dv_ref)

    def job(i, first, n, order):
        heads = first == 2 * rows
        part = pl.ds(first - rows, n)
        loads[i].wait()
        if not heads:
            swaps[i].wait_recv()

            def add(j, carry):
                u = first - rows + j // SIZES["z"]
                z = lax.rem(j, SIZES["z"])
                acc_ref[u, z] = (acc_ref[u, z].astype(F32) + core_ref[u, z].astype(F32)).astype(BF16)
                return carry

            lax.fori_loop(0, n * SIZES["z"], add, 0)

        def view(sel):
            return pick(acc_ref, [part], sel, ZYX)

        yield from scatter_steps(links, order, view, view, slot_refs[3 * i : 3 * i + 3], lambda: None)
        for u in range(n):
            piece = acc_ref[(first - rows + u, *own)]
            row = links.core * (rows // 2) + (first - rows + u) // 2
            if heads:
                dh_ref[u] = piece
            elif (first - rows + u) % 2 == 0:
                dk_ref[row] = turn(piece.astype(F32), cos_ref[...], -sin_ref[...]).astype(BF16)
            else:
                dv_ref[row] = piece

    def query_part(first):
        part = pl.ds(first, chunk)
        tokens = dq_ref.shape[1]
        cos = jnp.concatenate([cos_ref[...]] * chunk, axis=0)
        sin = jnp.concatenate([sin_ref[...]] * chunk, axis=0)
        da, db = query_grad_rows(dq_ref[part].reshape(chunk * tokens, -1), aq_ref[part].reshape(chunk * tokens, -1),
                                 bq_ref[part].reshape(chunk * tokens, -1), eq_ref, cos, sin)
        da_ref[part] = da.reshape(chunk, tokens, -1)
        db_ref[part] = db.reshape(chunk, tokens, -1)
        yield

    waves = in_pairs([job(i, *j) for i, j in enumerate(jobs)])
    at = 0
    for wave, group in zip(waves, groups):
        for cut in group:
            wave.insert(0, cut_job(links, cut, ins[cut.array], outs[cut.array], cut_accs[at], cut_slots[3 * at : 3 * at + 3],
                                   cut_loads[at], cut_sems.at[2 * at + 1]))
            at += 1
    for i, first in enumerate(range(0, dq_ref.shape[0], chunk)):
        waves[min(i, len(waves) - 1)].append(query_part(first))
    run_waves(waves)
    links.finish()


def give_back(dkv, dhd, cos, sin, dq, aq, bq, eq, chunk, named):
    units, length, _ = dkv.shape
    packs = dhd.shape[0]
    rows = units // 2
    tokens = length // math.prod(SIZES.values())
    dims = tuple(SIZES[d] for d in ZYX)
    jobs = collect_jobs(rows, packs)
    slots = [pltpu.VMEM(shape, BF16) for _, n, order in jobs for shape in slot_shapes(order, (n,), (tokens, LANES))]
    arrays = {name: pieces(name, w) for name, w in named.items()}
    groups = weight_cuts({name: w.shape for name, w in arrays.items()})
    cuts = [cut for group in groups for cut in group]
    copies = 8 * len(jobs) + 10 * len(cuts)
    vmem, any_space = pl.BlockSpec(memory_space=pltpu.VMEM), pl.BlockSpec(memory_space=pl.ANY)
    outs = pl.pallas_call(
        functools.partial(return_kernel, rows, packs, chunk, groups, len(arrays)),
        out_shape=[
            jax.ShapeDtypeStruct((rows, tokens, LANES), BF16),
            jax.ShapeDtypeStruct((rows, tokens, LANES), BF16),
            jax.ShapeDtypeStruct((packs, tokens, LANES), BF16),
            jax.ShapeDtypeStruct(aq.shape, BF16),
            jax.ShapeDtypeStruct(bq.shape, BF16),
            *[jax.ShapeDtypeStruct(w.shape, BF16) for w in arrays.values()],
        ],
        in_specs=[any_space] * 2 + [vmem] * 6 + [any_space] * len(arrays),
        out_specs=[vmem] * 5 + [any_space] * len(arrays),
        scratch_shapes=[pltpu.VMEM((rows + packs, *dims, tokens, LANES), BF16), pltpu.VMEM((rows, *dims, tokens, LANES), BF16),
                        *slots, *[pltpu.VMEM(cut.acc_shape(), BF16) for cut in cuts],
                        *[pltpu.VMEM(shape, BF16) for cut in cuts for shape in cut.slots()],
                        pltpu.SemaphoreType.DMA((len(jobs),)), pltpu.SemaphoreType.DMA((2 * len(cuts),)),
                        pltpu.SemaphoreType.DMA((copies,)), pltpu.SemaphoreType.DMA((copies,))],
        compiler_params=pltpu.CompilerParams(collective_id=2, has_side_effects=True, vmem_limit_bytes=36 * 2**20),
        name="give_back",
    )(dkv.reshape(units, *dims, tokens, LANES), dhd.reshape(packs, *dims, tokens, LANES), cos, sin, dq, aq, bq, eq,
      *arrays.values())
    return outs[:5], [o.reshape(w.shape) for o, w in zip(outs[5:], named.values())]


def pair_kernel(x_ref, out_ref, got_ref, send_sems, recv_sems):
    links = Links(send_sems, recv_sems)
    links.greet(core=True, chips=False)
    copies = [links.send(x_ref.at[r], got_ref.at[r], links.other_core()) for r in range(x_ref.shape[0])]
    for r, copy in enumerate(copies):
        copy.wait_recv()
        out_ref[r] = (x_ref[r].astype(F32) + got_ref[r].astype(F32)).astype(out_ref.dtype)
    links.finish()


def pair_sum(x, ident):
    parts = 4
    rows, tokens, model = x.shape
    flat = x.reshape(parts, rows * tokens // parts, model)
    return pl.pallas_call(
        pair_kernel,
        out_shape=jax.ShapeDtypeStruct(flat.shape, BF16),
        in_specs=[pl.BlockSpec(memory_space=pltpu.VMEM)],
        out_specs=pl.BlockSpec(memory_space=pltpu.VMEM),
        scratch_shapes=[pltpu.VMEM(flat.shape, BF16), pltpu.SemaphoreType.DMA((parts,)), pltpu.SemaphoreType.DMA((parts,))],
        compiler_params=pltpu.CompilerParams(collective_id=ident, has_side_effects=True, vmem_limit_bytes=32 * 2**20),
        name="pair_sum_%d" % ident,
    )(flat).reshape(x.shape)


class Cut:
    def __init__(self, array, axes, rows, cols, order, lane_dim=None, shared=False):
        self.array, self.axes, self.rows, self.cols = array, axes, rows, cols
        self.order, self.lane_dim, self.shared = order, lane_dim, shared

    def tail(self):
        return (self.rows[1], self.cols[1])

    def view(self, ref, sel, core):
        cols = pl.ds(self.cols[0], self.cols[1])
        if self.lane_dim is not None:
            cols = pl.ds(pl.multiple_of(self.cols[0] + sel[self.lane_dim] * self.cols[1], LANES), self.cols[1])
        lead = [core] if self.shared else []
        return pick(ref, lead, sel, self.axes, (pl.ds(self.rows[0], self.rows[1]), cols))

    def inner(self):
        return tuple(d for d in self.axes if d != self.order[0])

    def acc_shape(self):
        return (*[SIZES[d] for d in self.inner()], *self.tail())

    def slots(self):
        shapes, open_dims = [], list(self.inner())
        for d in self.order:
            if d in open_dims:
                open_dims.remove(d)
            shapes.append((SIZES[d] - 1, *[SIZES[e] for e in open_dims], *self.tail()))
        return shapes


def weight_cuts(shapes):
    a, b, c, d = ("x", "y", "z"), ("y", "x", "z"), ("x", "z", "y"), ("y", "z", "x")
    groups = []
    index = {name: i for i, name in enumerate(shapes)}
    axes = ("x", "y", "z")
    if "down" in shapes:
        n, cols = shapes["down"][2:]
        first = n // 32 * 16
        for rows in ((0, first), (first, n - first)):
            groups.append([Cut(index["down"], ("y", "z"), rows, (0, cols // 4), c, lane_dim="x"),
                           Cut(index["down"], ("x", "z"), rows, (cols // 2, cols // 4), d, lane_dim="y")])
    if "out" in shapes:
        n, cols = shapes["out"][3:]
        for rows in ((0, n // 2), (n // 2, n // 2)):
            groups.append([Cut(index["out"], axes, rows, (0, cols // 2), a), Cut(index["out"], axes, rows, (cols // 2, cols // 2), b)])
    if "small" in shapes:
        m, wide = shapes["small"][3:]
        groups.append([Cut(index["small"], ("y", "z", "x"), (0, m), (0, wide), a)])
    if "basis" in shapes:
        n, cols = shapes["basis"][4:]
        cut = cols // LANES // 2 * LANES
        groups[-1] += [Cut(index["basis"], axes, (0, n), (0, cut), a, shared=True),
                       Cut(index["basis"], axes, (0, n), (cut, cols - cut), b, shared=True)]
    return groups


def pieces(name, w):
    dims = (2, 2, 4)
    chips = math.prod(SIZES.values())
    if name == "basis":
        return w.reshape(CORES, *dims, w.shape[0] // CORES // chips, w.shape[1])
    if name == "down":
        return w.reshape(2, 4, -1, w.shape[1])
    if name == "small":
        return w.reshape(2, 4, 2, -1, LANES)
    return w.reshape(*dims, w.shape[0] // chips, w.shape[1])


def start_load(links, cut, ref, acc, sem):
    if cut.shared:
        return None
    load = pltpu.make_async_copy(cut.view(ref, {cut.order[0]: links.at[cut.order[0]]}, links.core), acc, sem)
    load.start()
    return load


def cut_job(links, cut, in_ref, out_ref, acc_ref, slots, load, store_sem, shared_ref=None):
    def acc(sel):
        return pick(acc_ref, [], sel, cut.inner())

    def source(sel):
        return cut.view(in_ref, sel, links.core)

    def out(sel):
        return cut.view(out_ref, sel, links.core)

    if cut.shared:
        cols = pl.ds(cut.cols[0], cut.cols[1])
        summed = pick(shared_ref, [], {cut.order[0]: links.at[cut.order[0]]}, cut.axes, (slice(None), cols))

        def keep(j, carry):
            p, q = j // acc_ref.shape[1], lax.rem(j, acc_ref.shape[1])
            acc_ref[p, q] = summed[p, q]
            return carry

        lax.fori_loop(0, acc_ref.shape[0] * acc_ref.shape[1], keep, 0)

        def source(sel):
            return pick(shared_ref, [], sel, cut.axes, (slice(None), cols))

    yield from scatter_steps(links, cut.order, source, acc, slots, load.wait if load is not None else lambda: None)
    piece = acc({d: links.at[d] for d in cut.inner()})
    store = pltpu.make_async_copy(piece, out(links.at), store_sem)
    store.start()
    steps = gather_steps(links, cut.order, out, piece)
    next(steps)
    yield
    store.wait()
    yield from steps


def weight_kernel(groups, count, basis, *refs):
    jobs = [cut for group in groups for cut in group]
    ins, outs = refs[:count], refs[count : 2 * count]
    at = 2 * count
    accs = refs[at : at + len(jobs)]
    at += len(jobs)
    slots = refs[at : at + 3 * len(jobs)]
    at += 3 * len(jobs)
    shared_own, shared_got, local_sems, send_sems, recv_sems = refs[at:]
    links = Links(send_sems, recv_sems)
    links.greet(core=True)
    loads = [start_load(links, cut, ins[cut.array], accs[i], local_sems.at[2 * i]) for i, cut in enumerate(jobs)]
    own = pltpu.make_async_copy(ins[basis].at[links.core], shared_own, local_sems.at[2 * len(jobs)])
    own.start()
    swap = links.send(ins[basis].at[1 - links.core], shared_got, links.other_core())

    def first_shared():
        own.wait()
        swap.wait_recv()

        def add(j, carry):
            shape = shared_own.shape
            p, q, r = j // (shape[1] * shape[2]), lax.rem(j // shape[2], shape[1]), lax.rem(j, shape[2])
            shared_own[p, q, r] = (shared_own[p, q, r].astype(F32) + shared_got[p, q, r].astype(F32)).astype(BF16)
            return carry

        lax.fori_loop(0, math.prod(shared_own.shape[:3]), add, 0)
        return
        yield

    made, i, ready = [], 0, False
    for group in groups:
        lot = []
        for cut in group:
            if cut.shared and not ready:
                lot.append(first_shared())
                ready = True
            lot.append(cut_job(links, cut, ins[cut.array], outs[cut.array], accs[i], slots[3 * i : 3 * i + 3], loads[i],
                               local_sems.at[2 * i + 1], shared_own))
            i += 1
        made.append(lot)
    run_waves(made)
    last = links.send(outs[basis].at[links.core], outs[basis].at[links.core], links.other_core())
    last.wait_recv()
    links.finish()


def weight_sums(named):
    arrays = {name: pieces(name, w) for name, w in named.items()}
    groups = weight_cuts({name: w.shape for name, w in arrays.items()})
    jobs = [cut for group in groups for cut in group]
    accs = [pltpu.VMEM(cut.acc_shape(), BF16) for cut in jobs]
    slots = [pltpu.VMEM(shape, BF16) for cut in jobs for shape in cut.slots()]
    copies = 10 * len(jobs) + 4
    any_space = pl.BlockSpec(memory_space=pl.ANY)
    shared = arrays["basis"].shape[1:]
    outs = pl.pallas_call(
        functools.partial(weight_kernel, groups, len(arrays), list(arrays).index("basis")),
        out_shape=[jax.ShapeDtypeStruct(w.shape, BF16) for w in arrays.values()],
        in_specs=[any_space] * len(arrays),
        out_specs=[any_space] * len(arrays),
        scratch_shapes=[*accs, *slots, pltpu.VMEM(shared, BF16), pltpu.VMEM(shared, BF16),
                        pltpu.SemaphoreType.DMA((2 * len(jobs) + 1,)), pltpu.SemaphoreType.DMA((copies,)),
                        pltpu.SemaphoreType.DMA((copies,))],
        compiler_params=pltpu.CompilerParams(collective_id=3, has_side_effects=True, vmem_limit_bytes=48 * 2**20),
        name="weight_sums",
    )(*arrays.values())
    return [o.reshape(w.shape) for o, w in zip(outs, named.values())]


def norm_back(inputs, row_scale, gain_vec, grad_rows):
    weighted = grad_rows * gain_vec
    cubed = row_scale * row_scale * row_scale
    input_part = row_scale * weighted - inputs * cubed * jnp.mean(inputs * weighted, axis=-1, keepdims=True)
    gain_part = jnp.sum(grad_rows * inputs * row_scale, axis=(0, 1))
    return (input_part, gain_part)


def project(activations, weight):
    return jnp.einsum("rsd,de->rse", activations, weight, preferred_element_type=F32)


def back_project(grad_rows, weight):
    return jnp.einsum("rse,de->rsd", grad_rows, weight, preferred_element_type=F32)


def weight_grad(normed, grad_rows):
    return jnp.einsum("rsd,rse->de", normed, grad_rows, preferred_element_type=F32)


def head_sum(partial, ident):
    if on_known_slice():
        return pair_sum(partial.astype(BF16), ident).astype(F32)
    return lax.psum(partial.astype(BF16), "head").astype(F32)


def rms_scale(tensor):
    return lax.rsqrt(jnp.mean(tensor * tensor, axis=-1, keepdims=True) + EPS)


def query_table(head_count):
    hd = head_count * DH
    factor = jnp.arange(head_count * RQ, dtype=jnp.int32)[:, None]
    col = jnp.arange(RQ * hd, dtype=jnp.int32)[None, :]
    return jnp.where(factor == col % hd // DH * RQ + col // hd, 1.0, 0.0).astype(BF16)


def rope_tables(position):
    half = DH // 2
    frequency = jnp.exp(jnp.arange(half).astype(F32) * (-2.0 * math.log(10000.0) / DH))
    angles = position[:, None] * frequency[None, :]
    cos, sin = jnp.cos(angles), jnp.sin(angles)
    return jnp.concatenate([cos] * 4, axis=1), jnp.concatenate([-sin, sin, -sin, sin], axis=1)


def shards(
    block_input,
    seq_lengths,
    attn_gain,
    query_heads,
    query_basis,
    key_heads,
    key_basis,
    value_heads,
    value_basis,
    out_project,
    ffn_gain,
    gate_weight,
    up_weight,
    down_weight,
    out_cotangent,
):
    row_count, slot_count, model_dim = block_input.shape
    head_count = query_heads.shape[1] // RQ
    hd = head_count * DH
    length = slot_count * lax.axis_size("seq")
    first_slot = lax.axis_index("seq") * slot_count
    width = head_count * (RK + RV)
    pack_rows = max(n for n in range(1, row_count + 1) if row_count % n == 0 and n * width <= LANES)
    group = min(4, head_count)
    block = math.gcd(length, KEY_BLOCK)
    query_spread = query_table(head_count)
    cos, sin = rope_tables((first_slot + jnp.arange(slot_count, dtype=jnp.int32)).astype(F32))
    normed, aq, bq, own_kv, own_heads, *queries = factors(
        block_input, attn_gain, query_heads.T, query_basis, key_basis, value_basis, key_heads.T, value_heads.T, cos, sin,
        query_spread, pack_rows, width, not on_known_slice())
    inputs = block_input.astype(F32)
    scale_one = rms_scale(inputs)
    shift = (1 - lax.axis_index("head")) * (row_count // CORES) if on_known_slice() else jnp.zeros((), jnp.int32)
    info = jnp.stack([*[seq_lengths[r] for r in range(row_count)], shift, first_slot]).astype(jnp.int32)
    if on_known_slice():
        kv, attended, mixed_flat, lse, queries = collect(
            seq_lengths, own_kv, own_heads, aq, bq, query_spread, pack_rows, group, width)
    else:
        (queries,) = queries
        kv = lax.all_gather(jnp.concatenate([own_kv, own_heads], axis=0), "seq", axis=1, tiled=True)
        attended, mixed_flat, lse = attend(info, queries, kv, pack_rows, group, block, width)
    attn_out = head_sum(project(mixed_flat, out_project), 4)
    middle = inputs + attn_out
    scale_two = rms_scale(middle)
    normed_two = (middle * scale_two * ffn_gain).astype(BF16)
    gate_act = project(normed_two, gate_weight)
    up_act = project(normed_two, up_weight)
    sigmoid_gate = jax.nn.sigmoid(gate_act)
    silu_gate = gate_act * sigmoid_gate
    hidden = (silu_gate * up_act).astype(BF16)
    ffn_out = head_sum(project(hidden, down_weight), 5)
    block_output = (middle + ffn_out).astype(BF16)
    cotangent = out_cotangent.astype(F32)
    down_grad = jnp.einsum("rsf,rsd->fd", hidden, out_cotangent, preferred_element_type=F32)
    d_hidden = jnp.einsum("rsd,fd->rsf", out_cotangent, down_weight, preferred_element_type=F32)
    d_gate = (d_hidden * up_act * (sigmoid_gate * (1.0 + gate_act * (1.0 - sigmoid_gate)))).astype(BF16)
    d_up = (d_hidden * silu_gate).astype(BF16)
    gate_grad = weight_grad(normed_two, d_gate)
    up_grad = weight_grad(normed_two, d_up)
    d_normed_two = head_sum(back_project(d_gate, gate_weight) + back_project(d_up, up_weight), 6)
    d_middle_norm, ffn_gain_part = norm_back(middle, scale_two, ffn_gain, d_normed_two)
    d_middle = cotangent + d_middle_norm
    d_branch = d_middle.astype(BF16)
    out_project_grad = jnp.einsum("rsf,rsd->fd", mixed_flat, d_branch, preferred_element_type=F32)
    d_mixed = back_project(d_branch, out_project).astype(BF16)
    d_queries, d_kv, d_heads = attend_back(info, queries, kv, attended, d_mixed, lse, pack_rows, group, block, width)
    packs = row_count // pack_rows
    model_cut = model_dim // 2
    if on_known_slice():
        (dk_basis, dv_basis, d_heads_own, dq_heads, dq_basis), (down_right, out_project_grad) = give_back(
            d_kv, d_heads, cos, sin, d_queries, aq, bq, query_spread, pack_rows,
            {"down": down_grad[:, model_cut:].astype(BF16), "out": out_project_grad.astype(BF16)})
    else:
        dq_heads, dq_basis = query_grads(d_queries, aq, bq, query_spread, cos, sin, pack_rows)
        key_grads = lax.psum_scatter(
            jnp.concatenate([d_kv, d_heads], axis=0), "seq", scatter_dimension=1, tiled=True)
        d_kv_own = key_grads[: 2 * row_count].reshape(row_count, 2, slot_count, LANES)
        half = DH // 2
        pairs = d_kv_own[:, 0].astype(F32).reshape(row_count, slot_count, 2, 2, half)
        u, w = pairs[:, :, :, 0], pairs[:, :, :, 1]
        c, s = cos[None, :, None, :half], sin[None, :, None, half:DH]
        dk_basis = jnp.stack([u * c + w * s, w * c - u * s], axis=3).reshape(row_count, slot_count, LANES).astype(BF16)
        dv_basis = d_kv_own[:, 1]
        d_heads_own = key_grads[2 * row_count :]
    d_heads_own = d_heads_own[:, :, : width * pack_rows].reshape(packs, slot_count, pack_rows, width)
    d_heads_own = jnp.transpose(d_heads_own, (0, 2, 1, 3)).reshape(row_count, slot_count, width)
    dk_heads, dv_heads = d_heads_own[..., : head_count * RK], d_heads_own[..., head_count * RK :]
    d_normed = head_sum(
        back_project(dq_heads, query_heads) + back_project(dq_basis, query_basis)
        + back_project(dk_heads, key_heads) + back_project(dk_basis, key_basis)
        + back_project(dv_heads, value_heads) + back_project(dv_basis, value_basis), 7)
    d_input_norm, attn_gain_part = norm_back(inputs, scale_one, attn_gain, d_normed)
    input_grad = d_middle + d_input_norm
    head_grads = weight_grad(jnp.concatenate([dq_heads, dk_heads, dv_heads], axis=-1), normed)
    basis_grads = weight_grad(normed, jnp.concatenate([dq_basis, dk_basis, dv_basis], axis=-1))
    small = jnp.concatenate([head_grads, attn_gain_part[None], ffn_gain_part[None]], axis=0).astype(BF16)
    if on_known_slice():
        gate_grad, up_grad, down_left = [
            t.astype(F32) for t in lax.psum(tuple(t.astype(BF16) for t in (gate_grad, up_grad, down_grad[:, :model_cut])), "seq")]
        down_grad = jnp.concatenate([down_left, down_right.astype(F32)], axis=1)
        height = small.shape[0]
        wide = model_dim // LANES
        small = jnp.pad(small, ((0, -height % 32), (0, 0)))
        full = small.shape[0]
        small = jnp.transpose(small.reshape(full, wide, LANES), (1, 0, 2))
        small, basis_grads = weight_sums({"small": small, "basis": basis_grads.astype(BF16)})
        small = jnp.transpose(small, (1, 0, 2)).reshape(full, model_dim)
    else:
        sums = lax.psum(tuple(t.astype(BF16) for t in (gate_grad, up_grad, down_grad, out_project_grad, small)), "seq")
        gate_grad, up_grad, down_grad, out_project_grad, small = [t.astype(F32) for t in sums]
        basis_grads = lax.psum(basis_grads, ("seq", "head"))
    nq, nk, nv = head_count * RQ, head_count * RK, head_count * RV
    cuts = (0, nq, nq + nk, nq + nk + nv)
    query_heads_grad, key_heads_grad, value_heads_grad = [small[i:j].astype(F32).T for i, j in zip(cuts, cuts[1:])]
    cuts = (0, RQ * DH, (RQ + RK) * DH, (RQ + RK + RV) * DH)
    query_basis_grad, key_basis_grad, value_basis_grad = [basis_grads[:, i:j].astype(F32) for i, j in zip(cuts, cuts[1:])]
    return (
        block_output,
        input_grad,
        small[nq + nk + nv].astype(F32),
        query_heads_grad,
        query_basis_grad,
        key_heads_grad,
        key_basis_grad,
        value_heads_grad,
        value_basis_grad,
        out_project_grad.astype(F32),
        small[nq + nk + nv + 1].astype(F32),
        gate_grad,
        up_grad,
        down_grad,
    )


def solution(mesh):
    rows = P(None, "seq", None)
    columns, features = P(None, "head"), P("head", None)
    in_specs = (rows, P(), P(), columns, P(), columns, P(), columns, P(), features, P(), columns, columns, features, rows)
    out_specs = (rows, rows, P(), columns, P(), columns, P(), columns, P(), features, P(), columns, columns, features)
    return jax.shard_map(shards, mesh=mesh, in_specs=in_specs, out_specs=out_specs, check_vma=False)
```

```python
import functools
import math

import jax
import jax.numpy as jnp
from jax import lax
from jax.experimental import pallas as pl
from jax.experimental.pallas import tpu as pltpu
from jax.sharding import PartitionSpec as P

DH = 64
RQ = 6
RK = 2
RV = 2
LANES = 128
EPS = 1e-06
KEY_BLOCK = 256
F32 = jnp.float32
BF16 = jnp.bfloat16


def dot(a, b):
    return lax.dot_general(a, b, (((1,), (0,)), ((), ())), preferred_element_type=F32)


def dot_nt(a, b):
    return lax.dot_general(a, b, (((1,), (1,)), ((), ())), preferred_element_type=F32)


def dot_tn(a, b):
    return lax.dot_general(a, b, (((0,), (0,)), ((), ())), preferred_element_type=F32)


def lane_of(shape):
    return lax.broadcasted_iota(jnp.int32, shape, len(shape) - 1)


def both_halves(pair):
    swapped = pltpu.roll(pair, DH, 1)
    low = lane_of(pair.shape) < DH
    return jnp.where(low, pair, swapped), jnp.where(low, swapped, pair)


def turn(pair, cos, sin):
    half = DH // 2
    first = lane_of(pair.shape) % DH < half
    other = jnp.where(first, pltpu.roll(pair, LANES - half, 1), pltpu.roll(pair, half, 1))
    return pair * cos + other * sin


def split_heads(rows, head_rows, tokens):
    group = lane_of(rows.shape) // DH
    return jnp.concatenate([jnp.where(group == h, rows, jnp.zeros_like(rows)) for h in range(head_rows)], axis=0)


def join_heads(block, head_rows, tokens):
    out = block[:tokens]
    group = lane_of(out.shape) // DH
    for h in range(1, head_rows):
        out = jnp.where(group == h, block[h * tokens : (h + 1) * tokens], out)
    return out


def query_rows(aq, bq, eq_ref, hd):
    aq_high = aq.astype(BF16)
    aq_low = (aq - aq_high.astype(F32)).astype(BF16)
    total = [None] * (hd // LANES)
    for p in range(RQ // 2):
        for half, vec in enumerate(both_halves(bq[:, p * LANES : (p + 1) * LANES])):
            spread = eq_ref[:, (2 * p + half) * hd : (2 * p + half + 1) * hd]
            coef = dot(aq_high, spread) + dot(aq_low, spread)
            for c in range(hd // LANES):
                term = coef[:, c * LANES : (c + 1) * LANES] * vec
                total[c] = term if total[c] is None else total[c] + term
    return [((t / RQ).astype(BF16).astype(F32) * (1.0 / math.sqrt(DH))).astype(BF16) for t in total]


def factor_kernel(width, with_queries, x_ref, gain_ref, wqh_ref, wqb_ref, wkb_ref, wvb_ref, wkh_ref, wvh_ref, cos_ref, sin_ref,
                  eq_ref, xn_ref, aq_ref, bq_ref, kv_ref, hd_ref, *q_refs):
    rows, tokens, model = x_ref.shape
    count = rows * tokens
    x = x_ref[...].astype(F32).reshape(count, model)
    scale = lax.rsqrt(jnp.mean(x * x, axis=-1, keepdims=True) + EPS)
    xn = (x * scale * gain_ref[...]).astype(BF16)
    xn_ref[...] = xn.reshape(rows, tokens, model)
    cos = jnp.concatenate([cos_ref[...]] * rows, axis=0)
    sin = jnp.concatenate([sin_ref[...]] * rows, axis=0)
    keys = turn(dot(xn, wkb_ref[...]), cos, sin).astype(BF16)
    values = dot(xn, wvb_ref[...]).astype(BF16)
    coefs = [dot_nt(xn, w_ref[...]).astype(BF16) for w_ref in (wkh_ref, wvh_ref)]
    pack = jnp.zeros((tokens, LANES), F32)
    for r in range(rows):
        part = slice(r * tokens, (r + 1) * tokens)
        kv_ref[2 * r] = keys[part]
        kv_ref[2 * r + 1] = values[part]
        at = r * width
        for coef in coefs:
            n = coef.shape[1]
            to = lane_of((n, LANES)) == lax.broadcasted_iota(jnp.int32, (n, LANES), 0) + at
            pack = pack + dot(coef[part], jnp.where(to, 1.0, 0.0).astype(BF16))
            at += n
    hd_ref[0] = pack.astype(BF16)
    aq = dot_nt(xn, wqh_ref[...])
    aq_ref[...] = aq.reshape(rows, tokens, aq.shape[1])
    basis = dot(xn, wqb_ref[...])
    bq = jnp.concatenate([turn(basis[:, p : p + LANES], cos, sin) for p in range(0, RQ * DH, LANES)], axis=1)
    bq_ref[...] = bq.reshape(rows, tokens, RQ * DH)
    if with_queries:
        for c, q in enumerate(query_rows(aq, bq, eq_ref, q_refs[0].shape[2])):
            q_refs[0][:, :, c * LANES : (c + 1) * LANES] = q.reshape(rows, tokens, LANES)


def whole(*shape):
    return pl.BlockSpec(shape, lambda *_: (0,) * len(shape))


def factors(x, gain, wqh, wqb, wkb, wvb, wkh, wvh, cos, sin, eq, pack_rows, width, with_queries):
    rows, tokens, model = x.shape
    hd = eq.shape[1] // RQ
    packs = rows // pack_rows
    nq = wqh.shape[0]

    def row_block(last):
        return pl.BlockSpec((pack_rows, tokens, last), lambda g: (g, 0, 0))

    out_specs = [row_block(model), row_block(nq), row_block(RQ * DH),
                 pl.BlockSpec((2 * pack_rows, tokens, LANES), lambda g: (g, 0, 0)),
                 pl.BlockSpec((1, tokens, LANES), lambda g: (g, 0, 0))]
    out_shape = [
        jax.ShapeDtypeStruct((rows, tokens, model), BF16),
        jax.ShapeDtypeStruct((rows, tokens, nq), F32),
        jax.ShapeDtypeStruct((rows, tokens, RQ * DH), F32),
        jax.ShapeDtypeStruct((2 * rows, tokens, LANES), BF16),
        jax.ShapeDtypeStruct((packs, tokens, LANES), BF16),
    ]
    if with_queries:
        out_specs.append(row_block(hd))
        out_shape.append(jax.ShapeDtypeStruct((rows, tokens, hd), BF16))
    return pl.pallas_call(
        functools.partial(factor_kernel, width, with_queries),
        grid=(packs,),
        in_specs=[row_block(model), whole(1, model), *[whole(*w.shape) for w in (wqh, wqb, wkb, wvb, wkh, wvh, cos, sin, eq)]],
        out_specs=out_specs,
        out_shape=out_shape,
        compiler_params=pltpu.CompilerParams(vmem_limit_bytes=32 * 2**20),
        name="factors",
    )(x, gain.reshape(1, model), wqh, wqb, wkb, wvb, wkh, wvh, cos, sin, eq)


def query_grad_rows(dq, aq, bq, eq_ref, cos, sin):
    hd = dq.shape[1]
    aq_high = aq.astype(BF16)
    aq_low = (aq - aq_high.astype(F32)).astype(BF16)
    da = jnp.zeros(aq.shape, F32)
    low = lane_of((dq.shape[0], LANES)) < DH
    turned = []
    for p in range(RQ // 2):
        sums = []
        for half, vec in enumerate(both_halves(bq[:, p * LANES : (p + 1) * LANES])):
            spread = eq_ref[:, (2 * p + half) * hd : (2 * p + half + 1) * hd]
            coef = dot(aq_high, spread) + dot(aq_low, spread)
            acc = None
            prods = []
            for c in range(hd // LANES):
                part = dq[:, c * LANES : (c + 1) * LANES]
                term = coef[:, c * LANES : (c + 1) * LANES] * part
                acc = term if acc is None else acc + term
                prods.append(part * vec)
            prod = jnp.concatenate(prods, axis=1)
            high = prod.astype(BF16)
            rest = (prod - high.astype(F32)).astype(BF16)
            da = da + dot_nt(high, spread) + dot_nt(rest, spread)
            sums.append(acc + pltpu.roll(acc, DH, 1))
        turned.append(turn(jnp.where(low, sums[0], sums[1]), cos, -sin) * (1.0 / RQ))
    return (da * (1.0 / RQ)).astype(BF16), jnp.concatenate(turned, axis=1).astype(BF16)


def query_grad_kernel(dq_ref, aq_ref, bq_ref, eq_ref, cos_ref, sin_ref, da_ref, db_ref):
    rows, tokens, hd = dq_ref.shape
    count = rows * tokens
    da, db = query_grad_rows(
        dq_ref[...].reshape(count, hd), aq_ref[...].reshape(count, -1), bq_ref[...].reshape(count, -1), eq_ref,
        jnp.concatenate([cos_ref[...]] * rows, axis=0), jnp.concatenate([sin_ref[...]] * rows, axis=0))
    da_ref[...] = da.reshape(da_ref.shape)
    db_ref[...] = db.reshape(db_ref.shape)


def query_grads(dq, aq, bq, eq, cos, sin, pack_rows):
    rows, tokens, hd = dq.shape
    nq = aq.shape[2]

    def row_block(last):
        return pl.BlockSpec((pack_rows, tokens, last), lambda g: (g, 0, 0))

    return pl.pallas_call(
        query_grad_kernel,
        grid=(rows // pack_rows,),
        in_specs=[row_block(hd), row_block(nq), row_block(RQ * DH), whole(*eq.shape), whole(*cos.shape), whole(*sin.shape)],
        out_specs=[row_block(nq), row_block(RQ * DH)],
        out_shape=[jax.ShapeDtypeStruct((rows, tokens, nq), BF16), jax.ShapeDtypeStruct((rows, tokens, RQ * DH), BF16)],
        compiler_params=pltpu.CompilerParams(vmem_limit_bytes=56 * 2**20),
        name="query_grads",
    )(dq, aq, bq, eq, cos, sin)


def key_rows(basis):
    turned = basis.astype(F32).T * 0.5
    return turned[:DH], turned[DH:]


def build_heads(coefs, first, second, head_count):
    return jnp.concatenate(
        [coefs[2 * h : 2 * h + 1] * first + coefs[2 * h + 1 : 2 * h + 2] * second for h in range(head_count)], axis=0
    ).astype(BF16)


def row_limits(info_ref, row, tokens, block, lanes):
    first = info_ref[info_ref.shape[0] - 1]
    length = info_ref[row]
    used = jnp.minimum(length, first + tokens)
    slot = lax.broadcasted_iota(jnp.int32, (lanes, 1), 0) % tokens
    return jnp.minimum(first + slot, length - 1), (used + block - 1) // block


def forward_row(q, read, place, width, limit, blocks, block, group, ct_ref):
    tokens, hd = q.shape
    head_count = hd // DH
    lanes = group * tokens
    wide = group * DH
    groups = hd // wide
    queries = [split_heads(q[:, g * wide : (g + 1) * wide], group, tokens) for g in range(groups)]

    def one(b, carry):
        ct_ref[...] = read(2, b).astype(F32).T
        coefs = ct_ref[pl.ds(place, width), :]
        keys = build_heads(coefs[: RK * head_count], *key_rows(read(0, b)), head_count)
        values = build_heads(coefs[RK * head_count :], *key_rows(read(1, b)), head_count)
        live = b * block + lax.broadcasted_iota(jnp.int32, (1, block), 1) <= limit
        out = []
        for g in range(groups):
            peak, total, mixed = carry[g]
            raw = jnp.where(live, dot(queries[g], keys[g * wide : (g + 1) * wide]), -1e30)
            top = jnp.maximum(peak, jnp.max(raw, axis=1, keepdims=True))
            e = jnp.exp(raw - top)
            keep = jnp.exp(peak - top)
            total = total * keep + jnp.sum(e, axis=1, keepdims=True)
            mixed = mixed * keep + dot_nt(e.astype(BF16), values[g * wide : (g + 1) * wide])
            out.append((top, total, mixed))
        return tuple(out)

    start = (jnp.full((lanes, 1), -1e30, F32), jnp.zeros((lanes, 1), F32), jnp.zeros((lanes, wide), F32))
    done = lax.fori_loop(0, blocks, one, (start,) * groups)
    lane = lane_of((tokens, LANES))
    lse = jnp.zeros((tokens, LANES), F32)
    parts = []
    for g in range(groups):
        peak, total, mixed = done[g]
        parts.append(join_heads(mixed / total, group, tokens))
        level = peak + jnp.log(total)
        for h in range(group):
            lse = jnp.where(lane == g * group + h, level[h * tokens : (h + 1) * tokens], lse)
    return parts, lse


def attend_kernel(pack_rows, group, block, width, info_ref, q_ref, kv_ref, hd_ref, o_ref, ob_ref, lse_ref, ct_ref):
    row = pl.program_id(0)
    _, tokens, hd = q_ref.shape
    wide = group * DH
    limit, blocks = row_limits(info_ref, row, tokens, block, group * tokens)

    def read(i, b):
        at = pl.ds(pl.multiple_of(b * block, block), block)
        return hd_ref[0, at, :] if i == 2 else kv_ref[i, at, :]

    parts, lse_ref[0] = forward_row(
        q_ref[0], read, pl.multiple_of(row % pack_rows * width, 8), width, limit, blocks, block, group, ct_ref)
    for g, mixed in enumerate(parts):
        o_ref[0, :, g * wide : (g + 1) * wide] = mixed
        ob_ref[0, :, g * wide : (g + 1) * wide] = mixed.astype(BF16)


def attend(info, q, kv, pack_rows, group, block, width):
    rows, tokens, hd = q.shape
    length = kv.shape[1]

    def own(r, i):
        return (r, 0, 0)

    grid_spec = pltpu.PrefetchScalarGridSpec(
        num_scalar_prefetch=1,
        grid=(rows,),
        in_specs=[
            pl.BlockSpec((1, tokens, hd), own),
            pl.BlockSpec((2, length, LANES), lambda r, i: (lax.rem(r + i[rows], rows), 0, 0)),
            pl.BlockSpec((1, length, LANES), lambda r, i: (2 * rows + r // pack_rows, 0, 0)),
        ],
        out_specs=[pl.BlockSpec((1, tokens, hd), own), pl.BlockSpec((1, tokens, hd), own), pl.BlockSpec((1, tokens, LANES), own)],
        scratch_shapes=[pltpu.VMEM((LANES, block), F32)],
    )
    return pl.pallas_call(
        functools.partial(attend_kernel, pack_rows, group, block, width),
        grid_spec=grid_spec,
        out_shape=[
            jax.ShapeDtypeStruct((rows, tokens, hd), F32),
            jax.ShapeDtypeStruct((rows, tokens, hd), BF16),
            jax.ShapeDtypeStruct((rows, tokens, LANES), F32),
        ],
        compiler_params=pltpu.CompilerParams(vmem_limit_bytes=32 * 2**20),
        name="attend",
    )(info, q, kv, kv)


def attend_back_kernel(pack_rows, group, block, width, info_ref, q_ref, kv_ref, hd_ref, o_ref, do_ref, lse_ref,
                       dq_ref, dkv_ref, dhd_ref, dq_acc, ct_ref, dct_ref):
    row = pl.program_id(0)
    _, tokens, hd = q_ref.shape
    head_count = hd // DH
    lanes = group * tokens
    wide = group * DH
    groups = hd // wide
    limit, blocks = row_limits(info_ref, row, tokens, block, lanes)
    place = pl.multiple_of(row % pack_rows * width, 8)
    queries, grads, deltas, levels = [], [], [], []
    for g in range(groups):
        part = slice(g * wide, (g + 1) * wide)
        do = do_ref[0, :, part]
        queries.append(split_heads(q_ref[0, :, part], group, tokens))
        grads.append(split_heads(do, group, tokens))
        weighed = split_heads(do.astype(F32) * o_ref[0, :, part], group, tokens)
        deltas.append(jnp.sum(weighed, axis=1, keepdims=True))
        levels.append(jnp.concatenate([lse_ref[0, :, h : h + 1] for h in range(g * group, (g + 1) * group)], axis=0))
    queries_t = [q.astype(F32).T.astype(BF16) for q in queries]
    grads_t = [g.astype(F32).T.astype(BF16) for g in grads]
    dq_acc[...] = jnp.zeros_like(dq_acc)
    dkv_ref[...] = jnp.zeros_like(dkv_ref)
    dct_ref[...] = jnp.zeros_like(dct_ref)

    @pl.when(row % pack_rows == 0)
    def _():
        dhd_ref[...] = jnp.zeros_like(dhd_ref)

    def factor_grads(grad, coefs, vectors):
        sums, rows = [None, None], []
        for h in range(head_count):
            part = grad[h * DH : (h + 1) * DH]
            for r in range(2):
                term = coefs[2 * h + r : 2 * h + r + 1] * part
                sums[r] = term if h == 0 else sums[r] + term
                rows.append(jnp.sum(part * vectors[r], axis=0, keepdims=True))
        return (jnp.concatenate(sums, axis=0) * 0.5).T.astype(BF16), rows

    def one(b, carry):
        at = pl.ds(pl.multiple_of(b * block, block), block)
        ct_ref[...] = hd_ref[0, at, :].astype(F32).T
        coefs = ct_ref[pl.ds(place, width), :]
        key_coefs, value_coefs = coefs[: RK * head_count], coefs[RK * head_count :]
        key_vectors, value_vectors = key_rows(kv_ref[0, at, :]), key_rows(kv_ref[1, at, :])
        keys = build_heads(key_coefs, *key_vectors, head_count)
        values = build_heads(value_coefs, *value_vectors, head_count)
        live = b * block + lax.broadcasted_iota(jnp.int32, (1, block), 1) <= limit
        dks, dvs = [], []
        for g in range(groups):
            part = slice(g * wide, (g + 1) * wide)
            p = jnp.where(live, jnp.exp(dot(queries[g], keys[part]) - levels[g]), 0.0)
            dp = dot(grads[g], values[part])
            ds = (p * (dp - deltas[g])).astype(BF16)
            dvs.append(dot(grads_t[g], p.astype(BF16)))
            dks.append(dot(queries_t[g], ds))
            dq_acc[g] += dot_nt(ds, keys[part])
        dkv_ref[0, at, :], key_grads = factor_grads(jnp.concatenate(dks, axis=0), key_coefs, key_vectors)
        dkv_ref[1, at, :], value_grads = factor_grads(jnp.concatenate(dvs, axis=0), value_coefs, value_vectors)
        dct_ref[pl.ds(place, width), :] = jnp.concatenate(key_grads + value_grads, axis=0)
        dhd_ref[0, at, :] = (dhd_ref[0, at, :].astype(F32) + dct_ref[...].T).astype(BF16)
        return carry

    lax.fori_loop(0, blocks, one, 0)
    for g in range(groups):
        dq_ref[0, :, g * wide : (g + 1) * wide] = join_heads(dq_acc[g], group, tokens) * (1.0 / math.sqrt(DH))


def attend_back(info, q, kv, o, do, lse, pack_rows, group, block, width):
    rows, tokens, hd = q.shape
    length = kv.shape[1]
    packs = rows // pack_rows

    def place(r, i):
        return (lax.rem(r + i[rows], rows), 0, 0)

    def own(r, i):
        return (r, 0, 0)

    grid_spec = pltpu.PrefetchScalarGridSpec(
        num_scalar_prefetch=1,
        grid=(rows,),
        in_specs=[
            pl.BlockSpec((1, tokens, hd), own),
            pl.BlockSpec((2, length, LANES), place),
            pl.BlockSpec((1, length, LANES), lambda r, i: (2 * rows + r // pack_rows, 0, 0)),
            pl.BlockSpec((1, tokens, hd), own),
            pl.BlockSpec((1, tokens, hd), own),
            pl.BlockSpec((1, tokens, LANES), own),
        ],
        out_specs=[
            pl.BlockSpec((1, tokens, hd), own),
            pl.BlockSpec((2, length, LANES), place),
            pl.BlockSpec((1, length, LANES), lambda r, i: (r // pack_rows, 0, 0)),
        ],
        scratch_shapes=[pltpu.VMEM((hd // (group * DH), group * tokens, group * DH), F32),
                        pltpu.VMEM((LANES, block), F32), pltpu.VMEM((LANES, block), F32)],
    )
    return pl.pallas_call(
        functools.partial(attend_back_kernel, pack_rows, group, block, width),
        grid_spec=grid_spec,
        out_shape=[
            jax.ShapeDtypeStruct((rows, tokens, hd), F32),
            jax.ShapeDtypeStruct((2 * rows, length, LANES), BF16),
            jax.ShapeDtypeStruct((packs, length, LANES), BF16),
        ],
        compiler_params=pltpu.CompilerParams(vmem_limit_bytes=32 * 2**20),
        name="attend_back",
    )(info, q, kv, kv, o, do, lse)


MESH = pl.DeviceIdType.MESH
SIZES = {"z": 4, "y": 2, "x": 2}
STRIDES = {"z": 4, "y": 2, "x": 1}
CORES = 2


def on_known_slice():
    return lax.axis_size("seq") == math.prod(SIZES.values()) and lax.axis_size("head") == CORES


class Links:
    def __init__(self, send_sems, recv_sems):
        self.seq = lax.axis_index("seq")
        self.core = lax.axis_index("head")
        self.at = {d: lax.rem(self.seq // STRIDES[d], SIZES[d]) for d in SIZES}
        self.send_sems, self.recv_sems = send_sems, recv_sems
        self.count = 0
        self.started = []

    def along(self, d, offset):
        there = lax.rem(self.at[d] + offset, SIZES[d])
        return there, (self.seq + (there - self.at[d]) * STRIDES[d], self.core)

    def other_core(self):
        return (self.seq, 1 - self.core)

    def greet(self, core, chips=True):
        barrier = pltpu.get_barrier_semaphore()
        devices = [self.other_core()] if core else []
        if chips:
            devices += [self.along(d, o)[1] for d in SIZES for o in range(1, SIZES[d])]
        for device in devices:
            pl.semaphore_signal(barrier, inc=1, device_id=device, device_id_type=MESH)
        pl.semaphore_wait(barrier, len(devices))

    def send(self, src, dst, device):
        copy = pltpu.make_async_remote_copy(
            src_ref=src, dst_ref=dst, send_sem=self.send_sems.at[self.count], recv_sem=self.recv_sems.at[self.count],
            device_id=device, device_id_type=MESH)
        self.count += 1
        copy.start()
        self.started.append(copy)
        return copy

    def finish(self):
        for copy in self.started:
            copy.wait_send()


def accumulate(acc, slots):
    lead = acc.shape[:-2]

    def body(i, carry):
        at = []
        for size in reversed(lead):
            at.insert(0, lax.rem(i, size))
            i = i // size
        value = acc[(*at, slice(None), slice(None))].astype(F32)
        for o in range(slots.shape[0]):
            value = value + slots[(o, *at, slice(None), slice(None))].astype(F32)
        acc[(*at, slice(None), slice(None))] = value.astype(BF16)
        return carry

    lax.fori_loop(0, math.prod(lead), body, 0)


def scatter_steps(links, order, source, acc, slots, ready):
    fixed = {}
    for k, d in enumerate(order):
        copies = []
        for o in range(1, SIZES[d]):
            there, device = links.along(d, o)
            view = source if k == 0 else acc
            copies.append(links.send(view({**fixed, d: there}), slots[k].at[o - 1], device))
        yield
        if k == 0:
            ready()
        for copy in copies:
            copy.wait_recv()
        fixed[d] = links.at[d]
        accumulate(acc(fixed), slots[k])


def gather_steps(links, order, out, first):
    for k in reversed(range(len(order))):
        fixed = {d: links.at[d] for d in order[: k + 1]}
        copies = []
        for o in range(1, SIZES[order[k]]):
            _, device = links.along(order[k], o)
            src = first if first is not None and k == len(order) - 1 else out(fixed)
            copies.append(links.send(src, out(fixed), device))
        yield
        for copy in copies:
            copy.wait_recv()


def run_waves(groups):
    live, waiting = [], list(groups)
    while live or waiting:
        if waiting:
            live.append(list(waiting.pop(0)))
        for group in live:
            group[:] = [job for job in group if next(job, "end") != "end"]
        live = [group for group in live if group]


def in_pairs(jobs):
    half = (len(jobs) + 1) // 2
    return [jobs[i : i + 1] + jobs[half + i : half + i + 1] for i in range(half)]


def slot_shapes(order, units, tail):
    shapes, open_dims = [], list(SIZES)
    for d in order:
        open_dims.remove(d)
        shapes.append((SIZES[d] - 1, *units, *[SIZES[e] for e in open_dims], *tail))
    return shapes


def pick(ref, lead, sel, axes, tail=()):
    return ref.at[(*lead, *[sel.get(d, slice(None)) for d in axes], *tail)]


ZYX = ("z", "y", "x")


def collect_jobs(rows, packs):
    step = 1
    own = [(rows + u, min(step, rows - u)) for u in range(0, rows, step)]
    jobs = own + [(2 * rows, packs)]
    half = (len(jobs) + 1) // 2
    return [(first, n, ("y", "x", "z") if i < half else ("x", "y", "z")) for i, (first, n) in enumerate(jobs)]


def collect_groups(rows, packs):
    half = rows // CORES
    lots = [[0]] + [list(range(j, min(j + 2, half))) for j in range(1, half, 2)]
    return [([(2 * rows, packs)] if i == 0 else []) + [(rows + 2 * j, 2) for j in lot] for i, lot in enumerate(lots)], lots


def collect_kernel(pack_rows, group, block, width, len_ref, kv_ref, hd_ref, aq_ref, bq_ref, eq_ref, out_ref, o_ref, ob_ref, lse_ref,
                   q_ref, all_ref, ct_ref, local_sems, out_sems, send_sems, recv_sems):
    rows, tokens, hd = q_ref.shape
    packs = hd_ref.shape[0]
    half = rows // CORES
    wide = group * DH
    planes = block // (SIZES["y"] * SIZES["x"] * tokens)
    links = Links(send_sems, recv_sems)
    own = tuple(links.at[d] for d in ZYX)
    first_slot = links.seq * tokens
    blocks = (first_slot + tokens + block - 1) // block
    groups, lots = collect_groups(rows, packs)
    jobs = [job for lot in groups for job in lot]
    loads = []
    for i, (first, n) in enumerate(jobs):
        src = hd_ref if first == 2 * rows else kv_ref.at[pl.ds(links.core * rows + first - rows, n)]
        loads.append(pltpu.make_async_copy(src, all_ref.at[(pl.ds(first, n), *own)], local_sems.at[i]))
        loads[-1].start()
    links.greet(core=True)
    stores = []

    def keep(first, n):
        store = pltpu.make_async_copy(all_ref.at[pl.ds(first, n)], out_ref.at[pl.ds(first, n)], out_sems.at[len(stores)])
        store.start()
        stores.append(store)

    def job(i, first, n):
        order = ("x", "y", "z") if i % 2 else ("y", "x", "z")
        loads[i].wait()
        yield from gather_steps(links, order, lambda sel: pick(all_ref, [pl.ds(first, n)], sel, ZYX), None)
        if first < 2 * rows:
            copy = links.send(all_ref.at[pl.ds(first, n)], all_ref.at[pl.ds(first - rows, n)], links.other_core())
        keep(first, n)
        if first < 2 * rows:
            yield
            copy.wait_recv()
            keep(first - rows, n)

    def attend_rows(mine, lot):
        def body(i, carry):
            j = lot[0] + i
            row = j + half * (links.core if mine else 1 - links.core)
            unit = rows * mine + 2 * j
            slot = lax.broadcasted_iota(jnp.int32, (group * tokens, 1), 0) % tokens
            limit = jnp.minimum(first_slot + slot, len_ref[row] - 1)
            pack = row // pack_rows
            place = pl.multiple_of((row - pack * pack_rows) * width, 8)

            def read(k, b):
                at = 2 * rows + pack if k == 2 else unit + k
                return all_ref[at, pl.ds(b * planes, planes)].reshape(block, LANES)

            parts, lse_ref[row] = forward_row(q_ref[row], read, place, width, limit, blocks, block, group, ct_ref)
            for g, mixed in enumerate(parts):
                o_ref[row, :, g * wide : (g + 1) * wide] = mixed
                ob_ref[row, :, g * wide : (g + 1) * wide] = mixed.astype(BF16)
            return carry

        lax.fori_loop(0, len(lot), body, 0)

    live, started, wave, i = [], 0, 0, 0
    steps = 3
    while started < len(groups) or live:
        if started < len(groups):
            for first, n in groups[started]:
                live.append(job(i, first, n))
                i += 1
            started += 1
        live[:] = [made for made in live if next(made, "end") != "end"]
        if 0 <= wave - steps - 1 < len(lots):
            attend_rows(0, lots[wave - steps - 1])
        if 0 <= wave - steps < len(lots):
            attend_rows(1, lots[wave - steps])
        if wave < packs:
            part = pl.ds(wave * pack_rows, pack_rows)
            flat = pack_rows * tokens
            made = query_rows(aq_ref[part].reshape(flat, -1), bq_ref[part].reshape(flat, -1), eq_ref, hd)
            for c, q in enumerate(made):
                q_ref[part, :, c * LANES : (c + 1) * LANES] = q.reshape(pack_rows, tokens, LANES)
        wave += 1
    for store in stores:
        store.wait()
    links.finish()


def collect(lengths, kv, hd, aq, bq, eq, pack_rows, group, width):
    units, tokens, _ = kv.shape
    packs = hd.shape[0]
    rows = units // 2
    hidden = (rows, tokens, eq.shape[1] // RQ)
    length = tokens * math.prod(SIZES.values())
    block = length // 2
    count = sum(len(lot) for lot in collect_groups(rows, packs)[0])
    full = (units + packs, *[SIZES[d] for d in ZYX], tokens, LANES)
    vmem, any_space = pl.BlockSpec(memory_space=pltpu.VMEM), pl.BlockSpec(memory_space=pl.ANY)
    out, o, ob, lse, q = pl.pallas_call(
        functools.partial(collect_kernel, pack_rows, group, block, width),
        out_shape=[jax.ShapeDtypeStruct(full, BF16), jax.ShapeDtypeStruct(hidden, F32), jax.ShapeDtypeStruct(hidden, BF16),
                   jax.ShapeDtypeStruct((rows, tokens, LANES), F32), jax.ShapeDtypeStruct(hidden, BF16)],
        in_specs=[pl.BlockSpec(memory_space=pltpu.SMEM), any_space, any_space, vmem, vmem, vmem],
        out_specs=[any_space, vmem, vmem, vmem, vmem],
        scratch_shapes=[pltpu.VMEM(full, BF16), pltpu.VMEM((LANES, block), F32), pltpu.SemaphoreType.DMA((count,)),
                        pltpu.SemaphoreType.DMA((2 * count,)), pltpu.SemaphoreType.DMA((8 * count,)),
                        pltpu.SemaphoreType.DMA((8 * count,))],
        compiler_params=pltpu.CompilerParams(collective_id=1, has_side_effects=True, vmem_limit_bytes=32 * 2**20),
        name="collect",
    )(lengths, kv, hd, aq, bq, eq)
    return out.reshape(units + packs, length, LANES), o, ob, lse, q


def return_kernel(rows, packs, chunk, groups, count, dkv_ref, dhd_ref, cos_ref, sin_ref, dq_ref, aq_ref, bq_ref, eq_ref, *refs):
    ins, refs = refs[:count], refs[count:]
    (dk_ref, dv_ref, dh_ref, da_ref, db_ref), refs = refs[:5], refs[5:]
    outs, refs = refs[:count], refs[count:]
    acc_ref, core_ref, refs = refs[0], refs[1], refs[2:]
    jobs = collect_jobs(rows, packs)
    slot_refs, refs = refs[: 3 * len(jobs)], refs[3 * len(jobs) :]
    cuts = [cut for group in groups for cut in group]
    cut_accs, cut_slots, refs = refs[: len(cuts)], refs[len(cuts) : 4 * len(cuts)], refs[4 * len(cuts) :]
    local_sems, cut_sems, send_sems, recv_sems = refs
    links = Links(send_sems, recv_sems)
    links.greet(core=True)
    own = tuple(links.at[d] for d in ZYX)
    loads, swaps = [], []
    for i, (first, n, _) in enumerate(jobs):
        heads = first == 2 * rows
        part = pl.ds(first - rows, n)
        if not heads:
            swaps.append(links.send(dkv_ref.at[part], core_ref.at[part], links.other_core()))
        load = pltpu.make_async_copy(dhd_ref if heads else dkv_ref.at[pl.ds(first, n)], acc_ref.at[part], local_sems.at[i])
        load.start()
        loads.append(load)
    cut_loads = [start_load(links, cut, ins[cut.array], cut_accs[i], cut_sems.at[2 * i]) for i, cut in enumerate(cuts)]
    dk_ref[...] = jnp.zeros_like(dk_ref)
    dv_ref[...] = jnp.zeros_like(dv_ref)

    def job(i, first, n, order):
        heads = first == 2 * rows
        part = pl.ds(first - rows, n)
        loads[i].wait()
        if not heads:
            swaps[i].wait_recv()

            def add(j, carry):
                u = first - rows + j // SIZES["z"]
                z = lax.rem(j, SIZES["z"])
                acc_ref[u, z] = (acc_ref[u, z].astype(F32) + core_ref[u, z].astype(F32)).astype(BF16)
                return carry

            lax.fori_loop(0, n * SIZES["z"], add, 0)

        def view(sel):
            return pick(acc_ref, [part], sel, ZYX)

        yield from scatter_steps(links, order, view, view, slot_refs[3 * i : 3 * i + 3], lambda: None)
        for u in range(n):
            piece = acc_ref[(first - rows + u, *own)]
            row = links.core * (rows // 2) + (first - rows + u) // 2
            if heads:
                dh_ref[u] = piece
            elif (first - rows + u) % 2 == 0:
                dk_ref[row] = turn(piece.astype(F32), cos_ref[...], -sin_ref[...]).astype(BF16)
            else:
                dv_ref[row] = piece

    def query_part(first):
        part = pl.ds(first, chunk)
        tokens = dq_ref.shape[1]
        cos = jnp.concatenate([cos_ref[...]] * chunk, axis=0)
        sin = jnp.concatenate([sin_ref[...]] * chunk, axis=0)
        da, db = query_grad_rows(dq_ref[part].reshape(chunk * tokens, -1), aq_ref[part].reshape(chunk * tokens, -1),
                                 bq_ref[part].reshape(chunk * tokens, -1), eq_ref, cos, sin)
        da_ref[part] = da.reshape(chunk, tokens, -1)
        db_ref[part] = db.reshape(chunk, tokens, -1)
        yield

    waves = in_pairs([job(i, *j) for i, j in enumerate(jobs)])
    at = 0
    for wave, group in zip(waves, groups):
        for cut in group:
            wave.insert(0, cut_job(links, cut, ins[cut.array], outs[cut.array], cut_accs[at], cut_slots[3 * at : 3 * at + 3],
                                   cut_loads[at], cut_sems.at[2 * at + 1]))
            at += 1
    for i, first in enumerate(range(0, dq_ref.shape[0], chunk)):
        waves[min(i, len(waves) - 1)].append(query_part(first))
    run_waves(waves)
    links.finish()


def give_back(dkv, dhd, cos, sin, dq, aq, bq, eq, chunk, named):
    units, length, _ = dkv.shape
    packs = dhd.shape[0]
    rows = units // 2
    tokens = length // math.prod(SIZES.values())
    dims = tuple(SIZES[d] for d in ZYX)
    jobs = collect_jobs(rows, packs)
    slots = [pltpu.VMEM(shape, BF16) for _, n, order in jobs for shape in slot_shapes(order, (n,), (tokens, LANES))]
    arrays = {name: pieces(name, w) for name, w in named.items()}
    groups = weight_cuts({name: w.shape for name, w in arrays.items()})
    cuts = [cut for group in groups for cut in group]
    copies = 8 * len(jobs) + 10 * len(cuts)
    vmem, any_space = pl.BlockSpec(memory_space=pltpu.VMEM), pl.BlockSpec(memory_space=pl.ANY)
    outs = pl.pallas_call(
        functools.partial(return_kernel, rows, packs, chunk, groups, len(arrays)),
        out_shape=[
            jax.ShapeDtypeStruct((rows, tokens, LANES), BF16),
            jax.ShapeDtypeStruct((rows, tokens, LANES), BF16),
            jax.ShapeDtypeStruct((packs, tokens, LANES), BF16),
            jax.ShapeDtypeStruct(aq.shape, BF16),
            jax.ShapeDtypeStruct(bq.shape, BF16),
            *[jax.ShapeDtypeStruct(w.shape, BF16) for w in arrays.values()],
        ],
        in_specs=[any_space] * 2 + [vmem] * 6 + [any_space] * len(arrays),
        out_specs=[vmem] * 5 + [any_space] * len(arrays),
        scratch_shapes=[pltpu.VMEM((rows + packs, *dims, tokens, LANES), BF16), pltpu.VMEM((rows, *dims, tokens, LANES), BF16),
                        *slots, *[pltpu.VMEM(cut.acc_shape(), BF16) for cut in cuts],
                        *[pltpu.VMEM(shape, BF16) for cut in cuts for shape in cut.slots()],
                        pltpu.SemaphoreType.DMA((len(jobs),)), pltpu.SemaphoreType.DMA((2 * len(cuts),)),
                        pltpu.SemaphoreType.DMA((copies,)), pltpu.SemaphoreType.DMA((copies,))],
        compiler_params=pltpu.CompilerParams(collective_id=2, has_side_effects=True, vmem_limit_bytes=36 * 2**20),
        name="give_back",
    )(dkv.reshape(units, *dims, tokens, LANES), dhd.reshape(packs, *dims, tokens, LANES), cos, sin, dq, aq, bq, eq,
      *arrays.values())
    return outs[:5], [o.reshape(w.shape) for o, w in zip(outs[5:], named.values())]


def pair_kernel(x_ref, out_ref, got_ref, send_sems, recv_sems):
    links = Links(send_sems, recv_sems)
    links.greet(core=True, chips=False)
    copies = [links.send(x_ref.at[r], got_ref.at[r], links.other_core()) for r in range(x_ref.shape[0])]
    for r, copy in enumerate(copies):
        copy.wait_recv()
        out_ref[r] = (x_ref[r].astype(F32) + got_ref[r].astype(F32)).astype(out_ref.dtype)
    links.finish()


def pair_sum(x, ident):
    parts = 4
    rows, tokens, model = x.shape
    flat = x.reshape(parts, rows * tokens // parts, model)
    return pl.pallas_call(
        pair_kernel,
        out_shape=jax.ShapeDtypeStruct(flat.shape, BF16),
        in_specs=[pl.BlockSpec(memory_space=pltpu.VMEM)],
        out_specs=pl.BlockSpec(memory_space=pltpu.VMEM),
        scratch_shapes=[pltpu.VMEM(flat.shape, BF16), pltpu.SemaphoreType.DMA((parts,)), pltpu.SemaphoreType.DMA((parts,))],
        compiler_params=pltpu.CompilerParams(collective_id=ident, has_side_effects=True, vmem_limit_bytes=32 * 2**20),
        name="pair_sum_%d" % ident,
    )(flat).reshape(x.shape)


class Cut:
    def __init__(self, array, axes, rows, cols, order, lane_dim=None, shared=False):
        self.array, self.axes, self.rows, self.cols = array, axes, rows, cols
        self.order, self.lane_dim, self.shared = order, lane_dim, shared

    def tail(self):
        return (self.rows[1], self.cols[1])

    def view(self, ref, sel, core):
        cols = pl.ds(self.cols[0], self.cols[1])
        if self.lane_dim is not None:
            cols = pl.ds(pl.multiple_of(self.cols[0] + sel[self.lane_dim] * self.cols[1], LANES), self.cols[1])
        lead = [core] if self.shared else []
        return pick(ref, lead, sel, self.axes, (pl.ds(self.rows[0], self.rows[1]), cols))

    def inner(self):
        return tuple(d for d in self.axes if d != self.order[0])

    def acc_shape(self):
        return (*[SIZES[d] for d in self.inner()], *self.tail())

    def slots(self):
        shapes, open_dims = [], list(self.inner())
        for d in self.order:
            if d in open_dims:
                open_dims.remove(d)
            shapes.append((SIZES[d] - 1, *[SIZES[e] for e in open_dims], *self.tail()))
        return shapes


def weight_cuts(shapes):
    a, b, c, d = ("x", "y", "z"), ("y", "x", "z"), ("x", "z", "y"), ("y", "z", "x")
    groups = []
    index = {name: i for i, name in enumerate(shapes)}
    axes = ("x", "y", "z")
    if "down" in shapes:
        n, cols = shapes["down"][2:]
        first = n // 32 * 16
        for rows in ((0, first), (first, n - first)):
            groups.append([Cut(index["down"], ("y", "z"), rows, (0, cols // 4), c, lane_dim="x"),
                           Cut(index["down"], ("x", "z"), rows, (cols // 2, cols // 4), d, lane_dim="y")])
    if "gate" in shapes:
        n, cols = shapes["gate"][3:]
        cut = (cols // LANES + 1) // 2 * LANES
        groups.append([Cut(index["gate"], axes, (0, n), (0, cut), a), Cut(index["gate"], axes, (0, n), (cut, cols - cut), b)])
    if "out" in shapes:
        n, cols = shapes["out"][3:]
        for rows in ((0, n // 2), (n // 2, n // 2)):
            groups.append([Cut(index["out"], axes, rows, (0, cols // 2), a), Cut(index["out"], axes, rows, (cols // 2, cols // 2), b)])
    if "small" in shapes:
        m, wide = shapes["small"][3:]
        groups.append([Cut(index["small"], ("y", "z", "x"), (0, m), (0, wide), a)])
    if "basis" in shapes:
        n, cols = shapes["basis"][4:]
        cut = cols // LANES // 2 * LANES
        groups[-1] += [Cut(index["basis"], axes, (0, n), (0, cut), a, shared=True),
                       Cut(index["basis"], axes, (0, n), (cut, cols - cut), b, shared=True)]
    return groups


def pieces(name, w):
    dims = (2, 2, 4)
    chips = math.prod(SIZES.values())
    if name == "basis":
        return w.reshape(CORES, *dims, w.shape[0] // CORES // chips, w.shape[1])
    if name == "down":
        return w.reshape(2, 4, -1, w.shape[1])
    if name == "small":
        return w.reshape(2, 4, 2, -1, LANES)
    return w.reshape(*dims, w.shape[0] // chips, w.shape[1])


def start_load(links, cut, ref, acc, sem):
    if cut.shared:
        return None
    load = pltpu.make_async_copy(cut.view(ref, {cut.order[0]: links.at[cut.order[0]]}, links.core), acc, sem)
    load.start()
    return load


def cut_job(links, cut, in_ref, out_ref, acc_ref, slots, load, store_sem, shared_ref=None):
    def acc(sel):
        return pick(acc_ref, [], sel, cut.inner())

    def source(sel):
        return cut.view(in_ref, sel, links.core)

    def out(sel):
        return cut.view(out_ref, sel, links.core)

    if cut.shared:
        cols = pl.ds(cut.cols[0], cut.cols[1])
        summed = pick(shared_ref, [], {cut.order[0]: links.at[cut.order[0]]}, cut.axes, (slice(None), cols))

        def keep(j, carry):
            p, q = j // acc_ref.shape[1], lax.rem(j, acc_ref.shape[1])
            acc_ref[p, q] = summed[p, q]
            return carry

        lax.fori_loop(0, acc_ref.shape[0] * acc_ref.shape[1], keep, 0)

        def source(sel):
            return pick(shared_ref, [], sel, cut.axes, (slice(None), cols))

    yield from scatter_steps(links, cut.order, source, acc, slots, load.wait if load is not None else lambda: None)
    piece = acc({d: links.at[d] for d in cut.inner()})
    store = pltpu.make_async_copy(piece, out(links.at), store_sem)
    store.start()
    steps = gather_steps(links, cut.order, out, piece)
    next(steps)
    yield
    store.wait()
    yield from steps


def weight_kernel(groups, count, basis, small, swapped, *refs):
    jobs = [cut for group in groups for cut in group]
    ins, mine, refs = refs[:count], refs[count : count + swapped], refs[count + swapped :]
    outs, theirs, their_small, refs = refs[:count], refs[count : count + swapped], refs[count + swapped], refs[count + swapped + 1 :]
    at = 0
    accs = refs[at : at + len(jobs)]
    at += len(jobs)
    slots = refs[at : at + 3 * len(jobs)]
    at += 3 * len(jobs)
    shared_own, shared_got, local_sems, send_sems, recv_sems = refs[at:]
    links = Links(send_sems, recv_sems)
    links.greet(core=True)
    loads = [start_load(links, cut, ins[cut.array], accs[i], local_sems.at[2 * i]) for i, cut in enumerate(jobs)]
    own = pltpu.make_async_copy(ins[basis].at[links.core], shared_own, local_sems.at[2 * len(jobs)])
    own.start()
    swap = links.send(ins[basis].at[1 - links.core], shared_got, links.other_core())
    swaps = [links.send(src, dst, links.other_core()) for src, dst in zip(mine, theirs)]

    def first_shared():
        own.wait()
        swap.wait_recv()

        def add(j, carry):
            shape = shared_own.shape
            p, q, r = j // (shape[1] * shape[2]), lax.rem(j // shape[2], shape[1]), lax.rem(j, shape[2])
            shared_own[p, q, r] = (shared_own[p, q, r].astype(F32) + shared_got[p, q, r].astype(F32)).astype(BF16)
            return carry

        lax.fori_loop(0, math.prod(shared_own.shape[:3]), add, 0)
        return
        yield

    made, i, ready = [], 0, False
    for group in groups:
        lot = []
        for cut in group:
            if cut.shared and not ready:
                lot.append(first_shared())
                ready = True
            lot.append(cut_job(links, cut, ins[cut.array], outs[cut.array], accs[i], slots[3 * i : 3 * i + 3], loads[i],
                               local_sems.at[2 * i + 1], shared_own))
            i += 1
        made.append(lot)
    run_waves(made)
    swaps.append(links.send(outs[basis].at[links.core], outs[basis].at[links.core], links.other_core()))
    swaps.append(links.send(outs[small], their_small, links.other_core()))
    for copy in swaps:
        copy.wait_recv()
    links.finish()


def weight_sums(named, partials):
    arrays = {name: pieces(name, w) for name, w in named.items()}
    names = list(arrays)
    groups = weight_cuts({name: w.shape for name, w in arrays.items()})
    jobs = [cut for group in groups for cut in group]
    accs = [pltpu.VMEM(cut.acc_shape(), BF16) for cut in jobs]
    slots = [pltpu.VMEM(shape, BF16) for cut in jobs for shape in cut.slots()]
    copies = 10 * len(jobs) + 4 + len(partials)
    any_space = pl.BlockSpec(memory_space=pl.ANY)
    shared = arrays["basis"].shape[1:]
    shapes = [w.shape for w in (*arrays.values(), *partials, arrays["small"])]
    outs = pl.pallas_call(
        functools.partial(weight_kernel, groups, len(arrays), names.index("basis"), names.index("small"), len(partials)),
        out_shape=[jax.ShapeDtypeStruct(shape, BF16) for shape in shapes],
        in_specs=[any_space] * (len(arrays) + len(partials)),
        out_specs=[any_space] * len(shapes),
        scratch_shapes=[*accs, *slots, pltpu.VMEM(shared, BF16), pltpu.VMEM(shared, BF16),
                        pltpu.SemaphoreType.DMA((2 * len(jobs) + 1,)), pltpu.SemaphoreType.DMA((copies,)),
                        pltpu.SemaphoreType.DMA((copies,))],
        compiler_params=pltpu.CompilerParams(collective_id=3, has_side_effects=True, vmem_limit_bytes=24 * 2**20),
        name="weight_sums",
    )(*arrays.values(), *partials)
    count = len(arrays)
    sums = [o.reshape(w.shape) for o, w in zip(outs, named.values())]
    return sums, outs[count:-1], outs[-1].reshape(named["small"].shape)


def norm_back(inputs, row_scale, gain_vec, grad_rows):
    weighted = grad_rows * gain_vec
    cubed = row_scale * row_scale * row_scale
    input_part = row_scale * weighted - inputs * cubed * jnp.mean(inputs * weighted, axis=-1, keepdims=True)
    gain_part = jnp.sum(grad_rows * inputs * row_scale, axis=(0, 1))
    return (input_part, gain_part)


def project(activations, weight):
    return jnp.einsum("rsd,de->rse", activations, weight, preferred_element_type=F32)


def back_project(grad_rows, weight):
    return jnp.einsum("rse,de->rsd", grad_rows, weight, preferred_element_type=F32)


def weight_grad(normed, grad_rows):
    return jnp.einsum("rsd,rse->de", normed, grad_rows, preferred_element_type=F32)


def head_sum(partial, ident):
    if on_known_slice():
        return pair_sum(partial.astype(BF16), ident).astype(F32)
    return lax.psum(partial.astype(BF16), "head").astype(F32)


def rms_scale(tensor):
    return lax.rsqrt(jnp.mean(tensor * tensor, axis=-1, keepdims=True) + EPS)


def query_table(head_count):
    hd = head_count * DH
    factor = jnp.arange(head_count * RQ, dtype=jnp.int32)[:, None]
    col = jnp.arange(RQ * hd, dtype=jnp.int32)[None, :]
    return jnp.where(factor == col % hd // DH * RQ + col // hd, 1.0, 0.0).astype(BF16)


def rope_tables(position):
    half = DH // 2
    frequency = jnp.exp(jnp.arange(half).astype(F32) * (-2.0 * math.log(10000.0) / DH))
    angles = position[:, None] * frequency[None, :]
    cos, sin = jnp.cos(angles), jnp.sin(angles)
    return jnp.concatenate([cos] * 4, axis=1), jnp.concatenate([-sin, sin, -sin, sin], axis=1)


def shards(
    block_input,
    seq_lengths,
    attn_gain,
    query_heads,
    query_basis,
    key_heads,
    key_basis,
    value_heads,
    value_basis,
    out_project,
    ffn_gain,
    gate_weight,
    up_weight,
    down_weight,
    out_cotangent,
):
    row_count, slot_count, model_dim = block_input.shape
    head_count = query_heads.shape[1] // RQ
    hd = head_count * DH
    length = slot_count * lax.axis_size("seq")
    first_slot = lax.axis_index("seq") * slot_count
    width = head_count * (RK + RV)
    pack_rows = max(n for n in range(1, row_count + 1) if row_count % n == 0 and n * width <= LANES)
    group = min(4, head_count)
    block = math.gcd(length, KEY_BLOCK)
    query_spread = query_table(head_count)
    cos, sin = rope_tables((first_slot + jnp.arange(slot_count, dtype=jnp.int32)).astype(F32))
    normed, aq, bq, own_kv, own_heads, *queries = factors(
        block_input, attn_gain, query_heads.T, query_basis, key_basis, value_basis, key_heads.T, value_heads.T, cos, sin,
        query_spread, pack_rows, width, not on_known_slice())
    inputs = block_input.astype(F32)
    scale_one = rms_scale(inputs)
    shift = (1 - lax.axis_index("head")) * (row_count // CORES) if on_known_slice() else jnp.zeros((), jnp.int32)
    info = jnp.stack([*[seq_lengths[r] for r in range(row_count)], shift, first_slot]).astype(jnp.int32)
    if on_known_slice():
        kv, attended, mixed_flat, lse, queries = collect(
            seq_lengths, own_kv, own_heads, aq, bq, query_spread, pack_rows, group, width)
    else:
        (queries,) = queries
        kv = lax.all_gather(jnp.concatenate([own_kv, own_heads], axis=0), "seq", axis=1, tiled=True)
        attended, mixed_flat, lse = attend(info, queries, kv, pack_rows, group, block, width)
    attn_out = head_sum(project(mixed_flat, out_project), 4)
    middle = inputs + attn_out
    scale_two = rms_scale(middle)
    normed_two = (middle * scale_two * ffn_gain).astype(BF16)
    gate_act = project(normed_two, gate_weight)
    up_act = project(normed_two, up_weight)
    sigmoid_gate = jax.nn.sigmoid(gate_act)
    silu_gate = gate_act * sigmoid_gate
    hidden = (silu_gate * up_act).astype(BF16)
    ffn_part = project(hidden, down_weight).astype(BF16)
    cotangent = out_cotangent.astype(F32)
    d_hidden = jnp.einsum("rsd,fd->rsf", out_cotangent, down_weight, preferred_element_type=F32)
    d_gate = (d_hidden * up_act * (sigmoid_gate * (1.0 + gate_act * (1.0 - sigmoid_gate)))).astype(BF16)
    d_up = (d_hidden * silu_gate).astype(BF16)
    known = on_known_slice()
    model_cut, gate_cut = (model_dim // 2, model_dim // 4) if known else (model_dim, 0)
    gate_grad = weight_grad(normed_two[..., gate_cut:], d_gate)
    up_grad = weight_grad(normed_two, d_up)
    down_grad = weight_grad(hidden, out_cotangent[..., :model_cut])
    d_normed_two = head_sum(back_project(d_gate, gate_weight) + back_project(d_up, up_weight), 6)
    d_middle_norm, ffn_gain_part = norm_back(middle, scale_two, ffn_gain, d_normed_two)
    d_middle = cotangent + d_middle_norm
    d_branch = d_middle.astype(BF16)
    out_project_grad = jnp.einsum("rsf,rsd->fd", mixed_flat, d_branch, preferred_element_type=F32)
    d_mixed = back_project(d_branch, out_project).astype(BF16)
    d_queries, d_kv, d_heads = attend_back(info, queries, kv, attended, d_mixed, lse, pack_rows, group, block, width)
    packs = row_count // pack_rows
    if known:
        down_right = weight_grad(hidden, out_cotangent[..., model_cut:])
        gate_top = weight_grad(normed_two[..., :gate_cut], d_gate)
        (dk_basis, dv_basis, d_heads_own, dq_heads, dq_basis), (down_right, gate_top, out_project_grad) = give_back(
            d_kv, d_heads, cos, sin, d_queries, aq, bq, query_spread, pack_rows,
            {"down": down_right.astype(BF16), "gate": gate_top.astype(BF16), "out": out_project_grad.astype(BF16)})
    else:
        dq_heads, dq_basis = query_grads(d_queries, aq, bq, query_spread, cos, sin, pack_rows)
        key_grads = lax.psum_scatter(
            jnp.concatenate([d_kv, d_heads], axis=0), "seq", scatter_dimension=1, tiled=True)
        d_kv_own = key_grads[: 2 * row_count].reshape(row_count, 2, slot_count, LANES)
        half = DH // 2
        pairs = d_kv_own[:, 0].astype(F32).reshape(row_count, slot_count, 2, 2, half)
        u, w = pairs[:, :, :, 0], pairs[:, :, :, 1]
        c, s = cos[None, :, None, :half], sin[None, :, None, half:DH]
        dk_basis = jnp.stack([u * c + w * s, w * c - u * s], axis=3).reshape(row_count, slot_count, LANES).astype(BF16)
        dv_basis = d_kv_own[:, 1]
        d_heads_own = key_grads[2 * row_count :]
    d_heads_own = d_heads_own[:, :, : width * pack_rows].reshape(packs, slot_count, pack_rows, width)
    d_heads_own = jnp.transpose(d_heads_own, (0, 2, 1, 3)).reshape(row_count, slot_count, width)
    dk_heads, dv_heads = d_heads_own[..., : head_count * RK], d_heads_own[..., head_count * RK :]
    normed_part = (
        back_project(dq_heads, query_heads) + back_project(dq_basis, query_basis)
        + back_project(dk_heads, key_heads) + back_project(dk_basis, key_basis)
        + back_project(dv_heads, value_heads) + back_project(dv_basis, value_basis))
    attn_gain_part = jnp.sum(normed_part * inputs * scale_one, axis=(0, 1))
    normed_part = normed_part.astype(BF16)
    head_grads = weight_grad(jnp.concatenate([dq_heads, dk_heads, dv_heads], axis=-1), normed)
    basis_grads = weight_grad(normed, jnp.concatenate([dq_basis, dk_basis, dv_basis], axis=-1))
    small = jnp.concatenate([head_grads, attn_gain_part[None], ffn_gain_part[None]], axis=0).astype(BF16)
    gain_at = head_grads.shape[0]
    if known:
        gate_grad, up_grad, down_grad = [
            t.astype(F32) for t in lax.psum(tuple(t.astype(BF16) for t in (gate_grad, up_grad, down_grad)), "seq")]
        gate_grad = jnp.concatenate([gate_top.astype(F32), gate_grad], axis=0)
        down_grad = jnp.concatenate([down_grad, down_right.astype(F32)], axis=1)
        height = small.shape[0]
        wide = model_dim // LANES
        small = jnp.pad(small, ((0, -height % 32), (0, 0)))
        full = small.shape[0]
        small = jnp.transpose(small.reshape(full, wide, LANES), (1, 0, 2))
        (small, basis_grads), (normed_other, ffn_other), small_other = weight_sums(
            {"small": small, "basis": basis_grads.astype(BF16)}, (normed_part, ffn_part))
        attn_gain_grad = (small[:, gain_at].astype(F32) + small_other[:, gain_at].astype(F32)).reshape(model_dim)
        small = jnp.transpose(small, (1, 0, 2)).reshape(full, model_dim)
        d_normed = normed_part.astype(F32) + normed_other.astype(F32)
        ffn_out = ffn_part.astype(F32) + ffn_other.astype(F32)
    else:
        sums = lax.psum(tuple(t.astype(BF16) for t in (gate_grad, up_grad, down_grad, out_project_grad, small)), "seq")
        gate_grad, up_grad, down_grad, out_project_grad, small = [t.astype(F32) for t in sums]
        attn_gain_grad = lax.psum(small[gain_at].astype(BF16), "head").astype(F32)
        basis_grads = lax.psum(basis_grads, ("seq", "head"))
        d_normed = lax.psum(normed_part, "head").astype(F32)
        ffn_out = lax.psum(ffn_part, "head").astype(F32)
    d_input_norm, _ = norm_back(inputs, scale_one, attn_gain, d_normed)
    input_grad = d_middle + d_input_norm
    block_output = (middle + ffn_out).astype(BF16)
    nq, nk, nv = head_count * RQ, head_count * RK, head_count * RV
    cuts = (0, nq, nq + nk, nq + nk + nv)
    query_heads_grad, key_heads_grad, value_heads_grad = [small[i:j].astype(F32).T for i, j in zip(cuts, cuts[1:])]
    cuts = (0, RQ * DH, (RQ + RK) * DH, (RQ + RK + RV) * DH)
    query_basis_grad, key_basis_grad, value_basis_grad = [basis_grads[:, i:j].astype(F32) for i, j in zip(cuts, cuts[1:])]
    return (
        block_output,
        input_grad,
        attn_gain_grad,
        query_heads_grad,
        query_basis_grad,
        key_heads_grad,
        key_basis_grad,
        value_heads_grad,
        value_basis_grad,
        out_project_grad.astype(F32),
        small[nq + nk + nv + 1].astype(F32),
        gate_grad,
        up_grad,
        down_grad,
    )


def solution(mesh):
    rows = P(None, "seq", None)
    columns, features = P(None, "head"), P("head", None)
    in_specs = (rows, P(), P(), columns, P(), columns, P(), columns, P(), features, P(), columns, columns, features, rows)
    out_specs = (rows, rows, P(), columns, P(), columns, P(), columns, P(), features, P(), columns, columns, features)
    return jax.shard_map(shards, mesh=mesh, in_specs=in_specs, out_specs=out_specs, check_vma=False)
```

```python
import functools
import math

import jax
import jax.numpy as jnp
from jax import lax
from jax.experimental import pallas as pl
from jax.experimental.pallas import tpu as pltpu
from jax.sharding import PartitionSpec as P

DH = 64
RQ = 6
RK = 2
RV = 2
LANES = 128
EPS = 1e-06
KEY_BLOCK = 256
F32 = jnp.float32
BF16 = jnp.bfloat16


def dot(a, b):
    return lax.dot_general(a, b, (((1,), (0,)), ((), ())), preferred_element_type=F32)


def dot_nt(a, b):
    return lax.dot_general(a, b, (((1,), (1,)), ((), ())), preferred_element_type=F32)


def dot_tn(a, b):
    return lax.dot_general(a, b, (((0,), (0,)), ((), ())), preferred_element_type=F32)


def lane_of(shape):
    return lax.broadcasted_iota(jnp.int32, shape, len(shape) - 1)


def both_halves(pair):
    swapped = pltpu.roll(pair, DH, 1)
    low = lane_of(pair.shape) < DH
    return jnp.where(low, pair, swapped), jnp.where(low, swapped, pair)


def turn(pair, cos, sin):
    half = DH // 2
    first = lane_of(pair.shape) % DH < half
    other = jnp.where(first, pltpu.roll(pair, LANES - half, 1), pltpu.roll(pair, half, 1))
    return pair * cos + other * sin


def split_heads(rows, head_rows, tokens):
    group = lane_of(rows.shape) // DH
    return jnp.concatenate([jnp.where(group == h, rows, jnp.zeros_like(rows)) for h in range(head_rows)], axis=0)


def join_heads(block, head_rows, tokens):
    out = block[:tokens]
    group = lane_of(out.shape) // DH
    for h in range(1, head_rows):
        out = jnp.where(group == h, block[h * tokens : (h + 1) * tokens], out)
    return out


def query_rows(aq, bq, eq_ref, hd):
    aq_high = aq.astype(BF16)
    aq_low = (aq - aq_high.astype(F32)).astype(BF16)
    total = [None] * (hd // LANES)
    for p in range(RQ // 2):
        for half, vec in enumerate(both_halves(bq[:, p * LANES : (p + 1) * LANES])):
            spread = eq_ref[:, (2 * p + half) * hd : (2 * p + half + 1) * hd]
            coef = dot(aq_high, spread) + dot(aq_low, spread)
            for c in range(hd // LANES):
                term = coef[:, c * LANES : (c + 1) * LANES] * vec
                total[c] = term if total[c] is None else total[c] + term
    return [((t / RQ).astype(BF16).astype(F32) * (1.0 / math.sqrt(DH))).astype(BF16) for t in total]


def factor_kernel(width, with_queries, x_ref, gain_ref, wqh_ref, wqb_ref, wkb_ref, wvb_ref, wkh_ref, wvh_ref, cos_ref, sin_ref,
                  eq_ref, xn_ref, aq_ref, bq_ref, kv_ref, hd_ref, *q_refs):
    rows, tokens, model = x_ref.shape
    count = rows * tokens
    x = x_ref[...].astype(F32).reshape(count, model)
    scale = lax.rsqrt(jnp.mean(x * x, axis=-1, keepdims=True) + EPS)
    xn = (x * scale * gain_ref[...]).astype(BF16)
    xn_ref[...] = xn.reshape(rows, tokens, model)
    cos = jnp.concatenate([cos_ref[...]] * rows, axis=0)
    sin = jnp.concatenate([sin_ref[...]] * rows, axis=0)
    keys = turn(dot(xn, wkb_ref[...]), cos, sin).astype(BF16)
    values = dot(xn, wvb_ref[...]).astype(BF16)
    coefs = [dot_nt(xn, w_ref[...]).astype(BF16) for w_ref in (wkh_ref, wvh_ref)]
    pack = jnp.zeros((tokens, LANES), F32)
    for r in range(rows):
        part = slice(r * tokens, (r + 1) * tokens)
        kv_ref[2 * r] = keys[part]
        kv_ref[2 * r + 1] = values[part]
        at = r * width
        for coef in coefs:
            n = coef.shape[1]
            to = lane_of((n, LANES)) == lax.broadcasted_iota(jnp.int32, (n, LANES), 0) + at
            pack = pack + dot(coef[part], jnp.where(to, 1.0, 0.0).astype(BF16))
            at += n
    hd_ref[0] = pack.astype(BF16)
    aq = dot_nt(xn, wqh_ref[...])
    aq_ref[...] = aq.reshape(rows, tokens, aq.shape[1])
    basis = dot(xn, wqb_ref[...])
    bq = jnp.concatenate([turn(basis[:, p : p + LANES], cos, sin) for p in range(0, RQ * DH, LANES)], axis=1)
    bq_ref[...] = bq.reshape(rows, tokens, RQ * DH)
    if with_queries:
        for c, q in enumerate(query_rows(aq, bq, eq_ref, q_refs[0].shape[2])):
            q_refs[0][:, :, c * LANES : (c + 1) * LANES] = q.reshape(rows, tokens, LANES)


def whole(*shape):
    return pl.BlockSpec(shape, lambda *_: (0,) * len(shape))


def factors(x, gain, wqh, wqb, wkb, wvb, wkh, wvh, cos, sin, eq, pack_rows, width, with_queries):
    rows, tokens, model = x.shape
    hd = eq.shape[1] // RQ
    packs = rows // pack_rows
    nq = wqh.shape[0]

    def row_block(last):
        return pl.BlockSpec((pack_rows, tokens, last), lambda g: (g, 0, 0))

    out_specs = [row_block(model), row_block(nq), row_block(RQ * DH),
                 pl.BlockSpec((2 * pack_rows, tokens, LANES), lambda g: (g, 0, 0)),
                 pl.BlockSpec((1, tokens, LANES), lambda g: (g, 0, 0))]
    out_shape = [
        jax.ShapeDtypeStruct((rows, tokens, model), BF16),
        jax.ShapeDtypeStruct((rows, tokens, nq), F32),
        jax.ShapeDtypeStruct((rows, tokens, RQ * DH), F32),
        jax.ShapeDtypeStruct((2 * rows, tokens, LANES), BF16),
        jax.ShapeDtypeStruct((packs, tokens, LANES), BF16),
    ]
    if with_queries:
        out_specs.append(row_block(hd))
        out_shape.append(jax.ShapeDtypeStruct((rows, tokens, hd), BF16))
    return pl.pallas_call(
        functools.partial(factor_kernel, width, with_queries),
        grid=(packs,),
        in_specs=[row_block(model), whole(1, model), *[whole(*w.shape) for w in (wqh, wqb, wkb, wvb, wkh, wvh, cos, sin, eq)]],
        out_specs=out_specs,
        out_shape=out_shape,
        compiler_params=pltpu.CompilerParams(vmem_limit_bytes=58 * 2**20),
        name="factors",
    )(x, gain.reshape(1, model), wqh, wqb, wkb, wvb, wkh, wvh, cos, sin, eq)


def query_grad_rows(dq, aq, bq, eq_ref, cos, sin):
    hd = dq.shape[1]
    aq_high = aq.astype(BF16)
    aq_low = (aq - aq_high.astype(F32)).astype(BF16)
    da = jnp.zeros(aq.shape, F32)
    low = lane_of((dq.shape[0], LANES)) < DH
    turned = []
    for p in range(RQ // 2):
        sums = []
        for half, vec in enumerate(both_halves(bq[:, p * LANES : (p + 1) * LANES])):
            spread = eq_ref[:, (2 * p + half) * hd : (2 * p + half + 1) * hd]
            coef = dot(aq_high, spread) + dot(aq_low, spread)
            acc = None
            prods = []
            for c in range(hd // LANES):
                part = dq[:, c * LANES : (c + 1) * LANES]
                term = coef[:, c * LANES : (c + 1) * LANES] * part
                acc = term if acc is None else acc + term
                prods.append(part * vec)
            prod = jnp.concatenate(prods, axis=1)
            high = prod.astype(BF16)
            rest = (prod - high.astype(F32)).astype(BF16)
            da = da + dot_nt(high, spread) + dot_nt(rest, spread)
            sums.append(acc + pltpu.roll(acc, DH, 1))
        turned.append(turn(jnp.where(low, sums[0], sums[1]), cos, -sin) * (1.0 / RQ))
    return (da * (1.0 / RQ)).astype(BF16), jnp.concatenate(turned, axis=1).astype(BF16)


def query_grad_kernel(dq_ref, aq_ref, bq_ref, eq_ref, cos_ref, sin_ref, da_ref, db_ref):
    rows, tokens, hd = dq_ref.shape
    count = rows * tokens
    da, db = query_grad_rows(
        dq_ref[...].reshape(count, hd), aq_ref[...].reshape(count, -1), bq_ref[...].reshape(count, -1), eq_ref,
        jnp.concatenate([cos_ref[...]] * rows, axis=0), jnp.concatenate([sin_ref[...]] * rows, axis=0))
    da_ref[...] = da.reshape(da_ref.shape)
    db_ref[...] = db.reshape(db_ref.shape)


def query_grads(dq, aq, bq, eq, cos, sin, pack_rows):
    rows, tokens, hd = dq.shape
    nq = aq.shape[2]

    def row_block(last):
        return pl.BlockSpec((pack_rows, tokens, last), lambda g: (g, 0, 0))

    return pl.pallas_call(
        query_grad_kernel,
        grid=(rows // pack_rows,),
        in_specs=[row_block(hd), row_block(nq), row_block(RQ * DH), whole(*eq.shape), whole(*cos.shape), whole(*sin.shape)],
        out_specs=[row_block(nq), row_block(RQ * DH)],
        out_shape=[jax.ShapeDtypeStruct((rows, tokens, nq), BF16), jax.ShapeDtypeStruct((rows, tokens, RQ * DH), BF16)],
        compiler_params=pltpu.CompilerParams(vmem_limit_bytes=56 * 2**20),
        name="query_grads",
    )(dq, aq, bq, eq, cos, sin)


def key_rows(basis):
    turned = basis.astype(F32).T * 0.5
    return turned[:DH], turned[DH:]


def build_heads(coefs, first, second, head_count):
    return jnp.concatenate(
        [coefs[2 * h : 2 * h + 1] * first + coefs[2 * h + 1 : 2 * h + 2] * second for h in range(head_count)], axis=0
    ).astype(BF16)


def row_limits(info_ref, row, tokens, block, lanes):
    first = info_ref[info_ref.shape[0] - 1]
    length = info_ref[row]
    used = jnp.minimum(length, first + tokens)
    slot = lax.broadcasted_iota(jnp.int32, (lanes, 1), 0) % tokens
    return jnp.minimum(first + slot, length - 1), (used + block - 1) // block


def forward_row(q, read, place, width, limit, blocks, block, group, ct_ref):
    tokens, hd = q.shape
    head_count = hd // DH
    lanes = group * tokens
    wide = group * DH
    groups = hd // wide
    queries = [split_heads(q[:, g * wide : (g + 1) * wide], group, tokens) for g in range(groups)]

    def one(b, carry):
        ct_ref[...] = read(2, b).astype(F32).T
        coefs = ct_ref[pl.ds(place, width), :]
        keys = build_heads(coefs[: RK * head_count], *key_rows(read(0, b)), head_count)
        values = build_heads(coefs[RK * head_count :], *key_rows(read(1, b)), head_count)
        live = b * block + lax.broadcasted_iota(jnp.int32, (1, block), 1) <= limit
        out = []
        for g in range(groups):
            peak, total, mixed = carry[g]
            raw = jnp.where(live, dot(queries[g], keys[g * wide : (g + 1) * wide]), -1e30)
            top = jnp.maximum(peak, jnp.max(raw, axis=1, keepdims=True))
            e = jnp.exp(raw - top)
            keep = jnp.exp(peak - top)
            total = total * keep + jnp.sum(e, axis=1, keepdims=True)
            mixed = mixed * keep + dot_nt(e.astype(BF16), values[g * wide : (g + 1) * wide])
            out.append((top, total, mixed))
        return tuple(out)

    start = (jnp.full((lanes, 1), -1e30, F32), jnp.zeros((lanes, 1), F32), jnp.zeros((lanes, wide), F32))
    done = lax.fori_loop(0, blocks, one, (start,) * groups)
    lane = lane_of((tokens, LANES))
    lse = jnp.zeros((tokens, LANES), F32)
    parts = []
    for g in range(groups):
        peak, total, mixed = done[g]
        parts.append(join_heads(mixed / total, group, tokens))
        level = peak + jnp.log(total)
        for h in range(group):
            lse = jnp.where(lane == g * group + h, level[h * tokens : (h + 1) * tokens], lse)
    return parts, lse


def attend_kernel(pack_rows, group, block, width, info_ref, q_ref, kv_ref, hd_ref, o_ref, ob_ref, lse_ref, ct_ref):
    row = pl.program_id(0)
    _, tokens, hd = q_ref.shape
    wide = group * DH
    limit, blocks = row_limits(info_ref, row, tokens, block, group * tokens)

    def read(i, b):
        at = pl.ds(pl.multiple_of(b * block, block), block)
        return hd_ref[0, at, :] if i == 2 else kv_ref[i, at, :]

    parts, lse_ref[0] = forward_row(
        q_ref[0], read, pl.multiple_of(row % pack_rows * width, 8), width, limit, blocks, block, group, ct_ref)
    for g, mixed in enumerate(parts):
        o_ref[0, :, g * wide : (g + 1) * wide] = mixed
        ob_ref[0, :, g * wide : (g + 1) * wide] = mixed.astype(BF16)


def attend(info, q, kv, pack_rows, group, block, width):
    rows, tokens, hd = q.shape
    length = kv.shape[1]

    def own(r, i):
        return (r, 0, 0)

    grid_spec = pltpu.PrefetchScalarGridSpec(
        num_scalar_prefetch=1,
        grid=(rows,),
        in_specs=[
            pl.BlockSpec((1, tokens, hd), own),
            pl.BlockSpec((2, length, LANES), lambda r, i: (lax.rem(r + i[rows], rows), 0, 0)),
            pl.BlockSpec((1, length, LANES), lambda r, i: (2 * rows + r // pack_rows, 0, 0)),
        ],
        out_specs=[pl.BlockSpec((1, tokens, hd), own), pl.BlockSpec((1, tokens, hd), own), pl.BlockSpec((1, tokens, LANES), own)],
        scratch_shapes=[pltpu.VMEM((LANES, block), F32)],
    )
    return pl.pallas_call(
        functools.partial(attend_kernel, pack_rows, group, block, width),
        grid_spec=grid_spec,
        out_shape=[
            jax.ShapeDtypeStruct((rows, tokens, hd), F32),
            jax.ShapeDtypeStruct((rows, tokens, hd), BF16),
            jax.ShapeDtypeStruct((rows, tokens, LANES), F32),
        ],
        compiler_params=pltpu.CompilerParams(vmem_limit_bytes=32 * 2**20),
        name="attend",
    )(info, q, kv, kv)


def attend_back_kernel(pack_rows, group, block, width, info_ref, q_ref, kv_ref, hd_ref, o_ref, do_ref, lse_ref,
                       dq_ref, dkv_ref, dhd_ref, dq_acc, ct_ref, dct_ref):
    row = pl.program_id(0)
    _, tokens, hd = q_ref.shape
    head_count = hd // DH
    lanes = group * tokens
    wide = group * DH
    groups = hd // wide
    limit, blocks = row_limits(info_ref, row, tokens, block, lanes)
    place = pl.multiple_of(row % pack_rows * width, 8)
    queries, grads, deltas, levels = [], [], [], []
    for g in range(groups):
        part = slice(g * wide, (g + 1) * wide)
        do = do_ref[0, :, part]
        queries.append(split_heads(q_ref[0, :, part], group, tokens))
        grads.append(split_heads(do, group, tokens))
        weighed = split_heads(do.astype(F32) * o_ref[0, :, part], group, tokens)
        deltas.append(jnp.sum(weighed, axis=1, keepdims=True))
        levels.append(jnp.concatenate([lse_ref[0, :, h : h + 1] for h in range(g * group, (g + 1) * group)], axis=0))
    queries_t = [q.astype(F32).T.astype(BF16) for q in queries]
    grads_t = [g.astype(F32).T.astype(BF16) for g in grads]
    dq_acc[...] = jnp.zeros_like(dq_acc)
    dkv_ref[...] = jnp.zeros_like(dkv_ref)
    dct_ref[...] = jnp.zeros_like(dct_ref)

    @pl.when(row % pack_rows == 0)
    def _():
        dhd_ref[...] = jnp.zeros_like(dhd_ref)

    def factor_grads(grad, coefs, vectors):
        sums, rows = [None, None], []
        for h in range(head_count):
            part = grad[h * DH : (h + 1) * DH]
            for r in range(2):
                term = coefs[2 * h + r : 2 * h + r + 1] * part
                sums[r] = term if h == 0 else sums[r] + term
                rows.append(jnp.sum(part * vectors[r], axis=0, keepdims=True))
        return (jnp.concatenate(sums, axis=0) * 0.5).T.astype(BF16), rows

    def one(b, carry):
        at = pl.ds(pl.multiple_of(b * block, block), block)
        ct_ref[...] = hd_ref[0, at, :].astype(F32).T
        coefs = ct_ref[pl.ds(place, width), :]
        key_coefs, value_coefs = coefs[: RK * head_count], coefs[RK * head_count :]
        key_vectors, value_vectors = key_rows(kv_ref[0, at, :]), key_rows(kv_ref[1, at, :])
        keys = build_heads(key_coefs, *key_vectors, head_count)
        values = build_heads(value_coefs, *value_vectors, head_count)
        live = b * block + lax.broadcasted_iota(jnp.int32, (1, block), 1) <= limit
        dks, dvs = [], []
        for g in range(groups):
            part = slice(g * wide, (g + 1) * wide)
            p = jnp.where(live, jnp.exp(dot(queries[g], keys[part]) - levels[g]), 0.0)
            dp = dot(grads[g], values[part])
            ds = (p * (dp - deltas[g])).astype(BF16)
            dvs.append(dot(grads_t[g], p.astype(BF16)))
            dks.append(dot(queries_t[g], ds))
            dq_acc[g] += dot_nt(ds, keys[part])
        dkv_ref[0, at, :], key_grads = factor_grads(jnp.concatenate(dks, axis=0), key_coefs, key_vectors)
        dkv_ref[1, at, :], value_grads = factor_grads(jnp.concatenate(dvs, axis=0), value_coefs, value_vectors)
        dct_ref[pl.ds(place, width), :] = jnp.concatenate(key_grads + value_grads, axis=0)
        dhd_ref[0, at, :] = (dhd_ref[0, at, :].astype(F32) + dct_ref[...].T).astype(BF16)
        return carry

    lax.fori_loop(0, blocks, one, 0)
    for g in range(groups):
        dq_ref[0, :, g * wide : (g + 1) * wide] = join_heads(dq_acc[g], group, tokens) * (1.0 / math.sqrt(DH))


def attend_back(info, q, kv, o, do, lse, pack_rows, group, block, width):
    rows, tokens, hd = q.shape
    length = kv.shape[1]
    packs = rows // pack_rows

    def place(r, i):
        return (lax.rem(r + i[rows], rows), 0, 0)

    def own(r, i):
        return (r, 0, 0)

    grid_spec = pltpu.PrefetchScalarGridSpec(
        num_scalar_prefetch=1,
        grid=(rows,),
        in_specs=[
            pl.BlockSpec((1, tokens, hd), own),
            pl.BlockSpec((2, length, LANES), place),
            pl.BlockSpec((1, length, LANES), lambda r, i: (2 * rows + r // pack_rows, 0, 0)),
            pl.BlockSpec((1, tokens, hd), own),
            pl.BlockSpec((1, tokens, hd), own),
            pl.BlockSpec((1, tokens, LANES), own),
        ],
        out_specs=[
            pl.BlockSpec((1, tokens, hd), own),
            pl.BlockSpec((2, length, LANES), place),
            pl.BlockSpec((1, length, LANES), lambda r, i: (r // pack_rows, 0, 0)),
        ],
        scratch_shapes=[pltpu.VMEM((hd // (group * DH), group * tokens, group * DH), F32),
                        pltpu.VMEM((LANES, block), F32), pltpu.VMEM((LANES, block), F32)],
    )
    return pl.pallas_call(
        functools.partial(attend_back_kernel, pack_rows, group, block, width),
        grid_spec=grid_spec,
        out_shape=[
            jax.ShapeDtypeStruct((rows, tokens, hd), F32),
            jax.ShapeDtypeStruct((2 * rows, length, LANES), BF16),
            jax.ShapeDtypeStruct((packs, length, LANES), BF16),
        ],
        compiler_params=pltpu.CompilerParams(vmem_limit_bytes=32 * 2**20),
        name="attend_back",
    )(info, q, kv, kv, o, do, lse)


MESH = pl.DeviceIdType.MESH
SIZES = {"z": 4, "y": 2, "x": 2}
STRIDES = {"z": 4, "y": 2, "x": 1}
CORES = 2


def on_known_slice():
    return lax.axis_size("seq") == math.prod(SIZES.values()) and lax.axis_size("head") == CORES


class Links:
    def __init__(self, send_sems, recv_sems):
        self.seq = lax.axis_index("seq")
        self.core = lax.axis_index("head")
        self.at = {d: lax.rem(self.seq // STRIDES[d], SIZES[d]) for d in SIZES}
        self.send_sems, self.recv_sems = send_sems, recv_sems
        self.count = 0
        self.started = []

    def along(self, d, offset):
        there = lax.rem(self.at[d] + offset, SIZES[d])
        return there, (self.seq + (there - self.at[d]) * STRIDES[d], self.core)

    def other_core(self):
        return (self.seq, 1 - self.core)

    def greet(self, core, chips=True):
        barrier = pltpu.get_barrier_semaphore()
        devices = [self.other_core()] if core else []
        if chips:
            devices += [self.along(d, o)[1] for d in SIZES for o in range(1, SIZES[d])]
        for device in devices:
            pl.semaphore_signal(barrier, inc=1, device_id=device, device_id_type=MESH)
        pl.semaphore_wait(barrier, len(devices))

    def send(self, src, dst, device):
        copy = pltpu.make_async_remote_copy(
            src_ref=src, dst_ref=dst, send_sem=self.send_sems.at[self.count], recv_sem=self.recv_sems.at[self.count],
            device_id=device, device_id_type=MESH)
        self.count += 1
        copy.start()
        self.started.append(copy)
        return copy

    def finish(self):
        for copy in self.started:
            copy.wait_send()


def accumulate(acc, slots):
    lead = acc.shape[:-2]

    def body(i, carry):
        at = []
        for size in reversed(lead):
            at.insert(0, lax.rem(i, size))
            i = i // size
        value = acc[(*at, slice(None), slice(None))].astype(F32)
        for o in range(slots.shape[0]):
            value = value + slots[(o, *at, slice(None), slice(None))].astype(F32)
        acc[(*at, slice(None), slice(None))] = value.astype(BF16)
        return carry

    lax.fori_loop(0, math.prod(lead), body, 0)


def scatter_steps(links, order, source, acc, slots, ready):
    fixed = {}
    for k, d in enumerate(order):
        copies = []
        for o in range(1, SIZES[d]):
            there, device = links.along(d, o)
            view = source if k == 0 else acc
            copies.append(links.send(view({**fixed, d: there}), slots[k].at[o - 1], device))
        yield
        if k == 0:
            ready()
        for copy in copies:
            copy.wait_recv()
        fixed[d] = links.at[d]
        accumulate(acc(fixed), slots[k])


def gather_steps(links, order, out, first):
    for k in reversed(range(len(order))):
        fixed = {d: links.at[d] for d in order[: k + 1]}
        copies = []
        for o in range(1, SIZES[order[k]]):
            _, device = links.along(order[k], o)
            src = first if first is not None and k == len(order) - 1 else out(fixed)
            copies.append(links.send(src, out(fixed), device))
        yield
        for copy in copies:
            copy.wait_recv()


def run_waves(groups):
    live, waiting = [], list(groups)
    while live or waiting:
        if waiting:
            live.append(list(waiting.pop(0)))
        for group in live:
            group[:] = [job for job in group if next(job, "end") != "end"]
        live = [group for group in live if group]


def in_pairs(jobs):
    half = (len(jobs) + 1) // 2
    return [jobs[i : i + 1] + jobs[half + i : half + i + 1] for i in range(half)]


def slot_shapes(order, units, tail):
    shapes, open_dims = [], list(SIZES)
    for d in order:
        open_dims.remove(d)
        shapes.append((SIZES[d] - 1, *units, *[SIZES[e] for e in open_dims], *tail))
    return shapes


def pick(ref, lead, sel, axes, tail=()):
    return ref.at[(*lead, *[sel.get(d, slice(None)) for d in axes], *tail)]


ZYX = ("z", "y", "x")


def collect_jobs(rows, packs):
    step = 1
    own = [(rows + u, min(step, rows - u)) for u in range(0, rows, step)]
    jobs = own + [(2 * rows, packs)]
    half = (len(jobs) + 1) // 2
    return [(first, n, ("y", "x", "z") if i < half else ("x", "y", "z")) for i, (first, n) in enumerate(jobs)]


def collect_groups(rows, packs):
    half = rows // CORES
    lots = [[0]] + [list(range(j, min(j + 2, half))) for j in range(1, half, 2)]
    return [([(2 * rows, packs)] if i == 0 else []) + [(rows + 2 * j, 2) for j in lot] for i, lot in enumerate(lots)], lots


def collect_kernel(pack_rows, group, block, width, len_ref, kv_ref, hd_ref, aq_ref, bq_ref, eq_ref, out_ref, o_ref, ob_ref, lse_ref,
                   q_ref, all_ref, ct_ref, local_sems, out_sems, send_sems, recv_sems):
    rows, tokens, hd = q_ref.shape
    packs = hd_ref.shape[0]
    half = rows // CORES
    wide = group * DH
    planes = block // (SIZES["y"] * SIZES["x"] * tokens)
    links = Links(send_sems, recv_sems)
    own = tuple(links.at[d] for d in ZYX)
    first_slot = links.seq * tokens
    blocks = (first_slot + tokens + block - 1) // block
    groups, lots = collect_groups(rows, packs)
    jobs = [job for lot in groups for job in lot]
    loads = []
    for i, (first, n) in enumerate(jobs):
        src = hd_ref if first == 2 * rows else kv_ref.at[pl.ds(links.core * rows + first - rows, n)]
        loads.append(pltpu.make_async_copy(src, all_ref.at[(pl.ds(first, n), *own)], local_sems.at[i]))
        loads[-1].start()
    links.greet(core=True)
    stores = []

    def keep(first, n):
        store = pltpu.make_async_copy(all_ref.at[pl.ds(first, n)], out_ref.at[pl.ds(first, n)], out_sems.at[len(stores)])
        store.start()
        stores.append(store)

    def job(i, first, n):
        order = ("x", "y", "z") if i % 2 else ("y", "x", "z")
        loads[i].wait()
        yield from gather_steps(links, order, lambda sel: pick(all_ref, [pl.ds(first, n)], sel, ZYX), None)
        if first < 2 * rows:
            copy = links.send(all_ref.at[pl.ds(first, n)], all_ref.at[pl.ds(first - rows, n)], links.other_core())
        keep(first, n)
        if first < 2 * rows:
            yield
            copy.wait_recv()
            keep(first - rows, n)

    def attend_rows(mine, lot):
        def body(i, carry):
            j = lot[0] + i
            row = j + half * (links.core if mine else 1 - links.core)
            unit = rows * mine + 2 * j
            slot = lax.broadcasted_iota(jnp.int32, (group * tokens, 1), 0) % tokens
            limit = jnp.minimum(first_slot + slot, len_ref[row] - 1)
            pack = row // pack_rows
            place = pl.multiple_of((row - pack * pack_rows) * width, 8)

            def read(k, b):
                at = 2 * rows + pack if k == 2 else unit + k
                return all_ref[at, pl.ds(b * planes, planes)].reshape(block, LANES)

            parts, lse_ref[row] = forward_row(q_ref[row], read, place, width, limit, blocks, block, group, ct_ref)
            for g, mixed in enumerate(parts):
                o_ref[row, :, g * wide : (g + 1) * wide] = mixed
                ob_ref[row, :, g * wide : (g + 1) * wide] = mixed.astype(BF16)
            return carry

        lax.fori_loop(0, len(lot), body, 0)

    live, started, wave, i = [], 0, 0, 0
    steps = 3
    while started < len(groups) or live:
        if started < len(groups):
            for first, n in groups[started]:
                live.append(job(i, first, n))
                i += 1
            started += 1
        live[:] = [made for made in live if next(made, "end") != "end"]
        if 0 <= wave - steps - 1 < len(lots):
            attend_rows(0, lots[wave - steps - 1])
        if 0 <= wave - steps < len(lots):
            attend_rows(1, lots[wave - steps])
        if wave < packs:
            part = pl.ds(wave * pack_rows, pack_rows)
            flat = pack_rows * tokens
            made = query_rows(aq_ref[part].reshape(flat, -1), bq_ref[part].reshape(flat, -1), eq_ref, hd)
            for c, q in enumerate(made):
                q_ref[part, :, c * LANES : (c + 1) * LANES] = q.reshape(pack_rows, tokens, LANES)
        wave += 1
    for store in stores:
        store.wait()
    links.finish()


def collect(lengths, kv, hd, aq, bq, eq, pack_rows, group, width):
    units, tokens, _ = kv.shape
    packs = hd.shape[0]
    rows = units // 2
    hidden = (rows, tokens, eq.shape[1] // RQ)
    length = tokens * math.prod(SIZES.values())
    block = length // 2
    count = sum(len(lot) for lot in collect_groups(rows, packs)[0])
    full = (units + packs, *[SIZES[d] for d in ZYX], tokens, LANES)
    vmem, any_space = pl.BlockSpec(memory_space=pltpu.VMEM), pl.BlockSpec(memory_space=pl.ANY)
    out, o, ob, lse, q = pl.pallas_call(
        functools.partial(collect_kernel, pack_rows, group, block, width),
        out_shape=[jax.ShapeDtypeStruct(full, BF16), jax.ShapeDtypeStruct(hidden, F32), jax.ShapeDtypeStruct(hidden, BF16),
                   jax.ShapeDtypeStruct((rows, tokens, LANES), F32), jax.ShapeDtypeStruct(hidden, BF16)],
        in_specs=[pl.BlockSpec(memory_space=pltpu.SMEM), any_space, any_space, vmem, vmem, vmem],
        out_specs=[any_space, vmem, vmem, vmem, vmem],
        scratch_shapes=[pltpu.VMEM(full, BF16), pltpu.VMEM((LANES, block), F32), pltpu.SemaphoreType.DMA((count,)),
                        pltpu.SemaphoreType.DMA((2 * count,)), pltpu.SemaphoreType.DMA((8 * count,)),
                        pltpu.SemaphoreType.DMA((8 * count,))],
        compiler_params=pltpu.CompilerParams(collective_id=1, has_side_effects=True, vmem_limit_bytes=58 * 2**20),
        name="collect",
    )(lengths, kv, hd, aq, bq, eq)
    return out.reshape(units + packs, length, LANES), o, ob, lse, q


def return_kernel(rows, packs, chunk, groups, count, dkv_ref, dhd_ref, cos_ref, sin_ref, dq_ref, aq_ref, bq_ref, eq_ref, *refs):
    ins, refs = refs[:count], refs[count:]
    (dk_ref, dv_ref, dh_ref, da_ref, db_ref), refs = refs[:5], refs[5:]
    outs, refs = refs[:count], refs[count:]
    acc_ref, core_ref, refs = refs[0], refs[1], refs[2:]
    jobs = collect_jobs(rows, packs)
    slot_refs, refs = refs[: 3 * len(jobs)], refs[3 * len(jobs) :]
    cuts = [cut for group in groups for cut in group]
    cut_accs, cut_slots, refs = refs[: len(cuts)], refs[len(cuts) : 4 * len(cuts)], refs[4 * len(cuts) :]
    local_sems, cut_sems, send_sems, recv_sems = refs
    links = Links(send_sems, recv_sems)
    links.greet(core=True)
    own = tuple(links.at[d] for d in ZYX)
    loads, swaps = [], []
    for i, (first, n, _) in enumerate(jobs):
        heads = first == 2 * rows
        part = pl.ds(first - rows, n)
        if not heads:
            swaps.append(links.send(dkv_ref.at[part], core_ref.at[part], links.other_core()))
        load = pltpu.make_async_copy(dhd_ref if heads else dkv_ref.at[pl.ds(first, n)], acc_ref.at[part], local_sems.at[i])
        load.start()
        loads.append(load)
    cut_loads = [start_load(links, cut, ins[cut.array], cut_accs[i], cut_sems.at[2 * i]) for i, cut in enumerate(cuts)]
    dk_ref[...] = jnp.zeros_like(dk_ref)
    dv_ref[...] = jnp.zeros_like(dv_ref)

    def job(i, first, n, order):
        heads = first == 2 * rows
        part = pl.ds(first - rows, n)
        loads[i].wait()
        if not heads:
            swaps[i].wait_recv()

            def add(j, carry):
                u = first - rows + j // SIZES["z"]
                z = lax.rem(j, SIZES["z"])
                acc_ref[u, z] = (acc_ref[u, z].astype(F32) + core_ref[u, z].astype(F32)).astype(BF16)
                return carry

            lax.fori_loop(0, n * SIZES["z"], add, 0)

        def view(sel):
            return pick(acc_ref, [part], sel, ZYX)

        yield from scatter_steps(links, order, view, view, slot_refs[3 * i : 3 * i + 3], lambda: None)
        for u in range(n):
            piece = acc_ref[(first - rows + u, *own)]
            row = links.core * (rows // 2) + (first - rows + u) // 2
            if heads:
                dh_ref[u] = piece
            elif (first - rows + u) % 2 == 0:
                dk_ref[row] = turn(piece.astype(F32), cos_ref[...], -sin_ref[...]).astype(BF16)
            else:
                dv_ref[row] = piece

    def query_part(first):
        part = pl.ds(first, chunk)
        tokens = dq_ref.shape[1]
        cos = jnp.concatenate([cos_ref[...]] * chunk, axis=0)
        sin = jnp.concatenate([sin_ref[...]] * chunk, axis=0)
        da, db = query_grad_rows(dq_ref[part].reshape(chunk * tokens, -1), aq_ref[part].reshape(chunk * tokens, -1),
                                 bq_ref[part].reshape(chunk * tokens, -1), eq_ref, cos, sin)
        da_ref[part] = da.reshape(chunk, tokens, -1)
        db_ref[part] = db.reshape(chunk, tokens, -1)
        yield

    waves = in_pairs([job(i, *j) for i, j in enumerate(jobs)])
    at = 0
    for wave, group in zip(waves, groups):
        for cut in group:
            wave.insert(0, cut_job(links, cut, ins[cut.array], outs[cut.array], cut_accs[at], cut_slots[3 * at : 3 * at + 3],
                                   cut_loads[at], cut_sems.at[2 * at + 1]))
            at += 1
    for i, first in enumerate(range(0, dq_ref.shape[0], chunk)):
        waves[min(i, len(waves) - 1)].append(query_part(first))
    run_waves(waves)
    links.finish()


def give_back(dkv, dhd, cos, sin, dq, aq, bq, eq, chunk, named):
    units, length, _ = dkv.shape
    packs = dhd.shape[0]
    rows = units // 2
    tokens = length // math.prod(SIZES.values())
    dims = tuple(SIZES[d] for d in ZYX)
    jobs = collect_jobs(rows, packs)
    slots = [pltpu.VMEM(shape, BF16) for _, n, order in jobs for shape in slot_shapes(order, (n,), (tokens, LANES))]
    arrays = {name: pieces(name, w) for name, w in named.items()}
    groups = weight_cuts({name: w.shape for name, w in arrays.items()})
    cuts = [cut for group in groups for cut in group]
    copies = 8 * len(jobs) + 10 * len(cuts)
    vmem, any_space = pl.BlockSpec(memory_space=pltpu.VMEM), pl.BlockSpec(memory_space=pl.ANY)
    outs = pl.pallas_call(
        functools.partial(return_kernel, rows, packs, chunk, groups, len(arrays)),
        out_shape=[
            jax.ShapeDtypeStruct((rows, tokens, LANES), BF16),
            jax.ShapeDtypeStruct((rows, tokens, LANES), BF16),
            jax.ShapeDtypeStruct((packs, tokens, LANES), BF16),
            jax.ShapeDtypeStruct(aq.shape, BF16),
            jax.ShapeDtypeStruct(bq.shape, BF16),
            *[jax.ShapeDtypeStruct(w.shape, BF16) for w in arrays.values()],
        ],
        in_specs=[any_space] * 2 + [vmem] * 6 + [any_space] * len(arrays),
        out_specs=[vmem] * 5 + [any_space] * len(arrays),
        scratch_shapes=[pltpu.VMEM((rows + packs, *dims, tokens, LANES), BF16), pltpu.VMEM((rows, *dims, tokens, LANES), BF16),
                        *slots, *[pltpu.VMEM(cut.acc_shape(), BF16) for cut in cuts],
                        *[pltpu.VMEM(shape, BF16) for cut in cuts for shape in cut.slots()],
                        pltpu.SemaphoreType.DMA((len(jobs),)), pltpu.SemaphoreType.DMA((2 * len(cuts),)),
                        pltpu.SemaphoreType.DMA((copies,)), pltpu.SemaphoreType.DMA((copies,))],
        compiler_params=pltpu.CompilerParams(collective_id=2, has_side_effects=True, vmem_limit_bytes=36 * 2**20),
        name="give_back",
    )(dkv.reshape(units, *dims, tokens, LANES), dhd.reshape(packs, *dims, tokens, LANES), cos, sin, dq, aq, bq, eq,
      *arrays.values())
    return outs[:5], [o.reshape(w.shape) for o, w in zip(outs[5:], named.values())]


def pair_kernel(x_ref, out_ref, got_ref, send_sems, recv_sems):
    links = Links(send_sems, recv_sems)
    links.greet(core=True, chips=False)
    copies = [links.send(x_ref.at[r], got_ref.at[r], links.other_core()) for r in range(x_ref.shape[0])]
    for r, copy in enumerate(copies):
        copy.wait_recv()
        out_ref[r] = (x_ref[r].astype(F32) + got_ref[r].astype(F32)).astype(out_ref.dtype)
    links.finish()


def pair_sum(x, ident):
    parts = 4
    rows, tokens, model = x.shape
    flat = x.reshape(parts, rows * tokens // parts, model)
    return pl.pallas_call(
        pair_kernel,
        out_shape=jax.ShapeDtypeStruct(flat.shape, BF16),
        in_specs=[pl.BlockSpec(memory_space=pltpu.VMEM)],
        out_specs=pl.BlockSpec(memory_space=pltpu.VMEM),
        scratch_shapes=[pltpu.VMEM(flat.shape, BF16), pltpu.SemaphoreType.DMA((parts,)), pltpu.SemaphoreType.DMA((parts,))],
        compiler_params=pltpu.CompilerParams(collective_id=ident, has_side_effects=True, vmem_limit_bytes=32 * 2**20),
        name="pair_sum_%d" % ident,
    )(flat).reshape(x.shape)


class Cut:
    def __init__(self, array, axes, rows, cols, order, lane_dim=None, shared=False):
        self.array, self.axes, self.rows, self.cols = array, axes, rows, cols
        self.order, self.lane_dim, self.shared = order, lane_dim, shared

    def tail(self):
        return (self.rows[1], self.cols[1])

    def view(self, ref, sel, core):
        cols = pl.ds(self.cols[0], self.cols[1])
        if self.lane_dim is not None:
            cols = pl.ds(pl.multiple_of(self.cols[0] + sel[self.lane_dim] * self.cols[1], LANES), self.cols[1])
        lead = [core] if self.shared else []
        return pick(ref, lead, sel, self.axes, (pl.ds(self.rows[0], self.rows[1]), cols))

    def inner(self):
        return tuple(d for d in self.axes if d != self.order[0])

    def acc_shape(self):
        return (*[SIZES[d] for d in self.inner()], *self.tail())

    def slots(self):
        shapes, open_dims = [], list(self.inner())
        for d in self.order:
            if d in open_dims:
                open_dims.remove(d)
            shapes.append((SIZES[d] - 1, *[SIZES[e] for e in open_dims], *self.tail()))
        return shapes


def weight_cuts(shapes):
    a, b, c, d = ("x", "y", "z"), ("y", "x", "z"), ("x", "z", "y"), ("y", "z", "x")
    groups = []
    index = {name: i for i, name in enumerate(shapes)}
    axes = ("x", "y", "z")
    if "down" in shapes:
        n, cols = shapes["down"][2:]
        first = n // 32 * 16
        for rows in ((0, first), (first, n - first)):
            groups.append([Cut(index["down"], ("y", "z"), rows, (0, cols // 4), c, lane_dim="x"),
                           Cut(index["down"], ("x", "z"), rows, (cols // 2, cols // 4), d, lane_dim="y")])
    if "gate" in shapes:
        n, cols = shapes["gate"][3:]
        cut = (cols // LANES + 1) // 2 * LANES
        groups.append([Cut(index["gate"], axes, (0, n), (0, cut), a), Cut(index["gate"], axes, (0, n), (cut, cols - cut), b)])
    if "out" in shapes:
        n, cols = shapes["out"][3:]
        for rows in ((0, n // 2), (n // 2, n // 2)):
            groups.append([Cut(index["out"], axes, rows, (0, cols // 2), a), Cut(index["out"], axes, rows, (cols // 2, cols // 2), b)])
    if "small" in shapes:
        m, wide = shapes["small"][3:]
        groups.append([Cut(index["small"], ("y", "z", "x"), (0, m), (0, wide), a)])
    if "basis" in shapes:
        n, cols = shapes["basis"][4:]
        cut = cols // LANES // 2 * LANES
        groups[-1] += [Cut(index["basis"], axes, (0, n), (0, cut), a, shared=True),
                       Cut(index["basis"], axes, (0, n), (cut, cols - cut), b, shared=True)]
    return groups


def pieces(name, w):
    dims = (2, 2, 4)
    chips = math.prod(SIZES.values())
    if name == "basis":
        return w.reshape(CORES, *dims, w.shape[0] // CORES // chips, w.shape[1])
    if name == "down":
        return w.reshape(2, 4, -1, w.shape[1])
    if name == "small":
        return w.reshape(2, 4, 2, -1, LANES)
    return w.reshape(*dims, w.shape[0] // chips, w.shape[1])


def start_load(links, cut, ref, acc, sem):
    if cut.shared:
        return None
    load = pltpu.make_async_copy(cut.view(ref, {cut.order[0]: links.at[cut.order[0]]}, links.core), acc, sem)
    load.start()
    return load


def cut_job(links, cut, in_ref, out_ref, acc_ref, slots, load, store_sem, shared_ref=None):
    def acc(sel):
        return pick(acc_ref, [], sel, cut.inner())

    def source(sel):
        return cut.view(in_ref, sel, links.core)

    def out(sel):
        return cut.view(out_ref, sel, links.core)

    if cut.shared:
        cols = pl.ds(cut.cols[0], cut.cols[1])
        summed = pick(shared_ref, [], {cut.order[0]: links.at[cut.order[0]]}, cut.axes, (slice(None), cols))

        def keep(j, carry):
            p, q = j // acc_ref.shape[1], lax.rem(j, acc_ref.shape[1])
            acc_ref[p, q] = summed[p, q]
            return carry

        lax.fori_loop(0, acc_ref.shape[0] * acc_ref.shape[1], keep, 0)

        def source(sel):
            return pick(shared_ref, [], sel, cut.axes, (slice(None), cols))

    yield from scatter_steps(links, cut.order, source, acc, slots, load.wait if load is not None else lambda: None)
    piece = acc({d: links.at[d] for d in cut.inner()})
    store = pltpu.make_async_copy(piece, out(links.at), store_sem)
    store.start()
    steps = gather_steps(links, cut.order, out, piece)
    next(steps)
    yield
    store.wait()
    yield from steps


def weight_kernel(groups, count, basis, small, swapped, *refs):
    jobs = [cut for group in groups for cut in group]
    ins, mine, refs = refs[:count], refs[count : count + swapped], refs[count + swapped :]
    outs, theirs, their_small, refs = refs[:count], refs[count : count + swapped], refs[count + swapped], refs[count + swapped + 1 :]
    at = 0
    accs = refs[at : at + len(jobs)]
    at += len(jobs)
    slots = refs[at : at + 3 * len(jobs)]
    at += 3 * len(jobs)
    shared_own, shared_got, local_sems, send_sems, recv_sems = refs[at:]
    links = Links(send_sems, recv_sems)
    links.greet(core=True)
    loads = [start_load(links, cut, ins[cut.array], accs[i], local_sems.at[2 * i]) for i, cut in enumerate(jobs)]
    own = pltpu.make_async_copy(ins[basis].at[links.core], shared_own, local_sems.at[2 * len(jobs)])
    own.start()
    swap = links.send(ins[basis].at[1 - links.core], shared_got, links.other_core())
    swaps = [links.send(src, dst, links.other_core()) for src, dst in zip(mine, theirs)]

    def first_shared():
        own.wait()
        swap.wait_recv()

        def add(j, carry):
            shape = shared_own.shape
            p, q, r = j // (shape[1] * shape[2]), lax.rem(j // shape[2], shape[1]), lax.rem(j, shape[2])
            shared_own[p, q, r] = (shared_own[p, q, r].astype(F32) + shared_got[p, q, r].astype(F32)).astype(BF16)
            return carry

        lax.fori_loop(0, math.prod(shared_own.shape[:3]), add, 0)
        return
        yield

    made, i, ready = [], 0, False
    for group in groups:
        lot = []
        for cut in group:
            if cut.shared and not ready:
                lot.append(first_shared())
                ready = True
            lot.append(cut_job(links, cut, ins[cut.array], outs[cut.array], accs[i], slots[3 * i : 3 * i + 3], loads[i],
                               local_sems.at[2 * i + 1], shared_own))
            i += 1
        made.append(lot)
    run_waves(made)
    swaps.append(links.send(outs[basis].at[links.core], outs[basis].at[links.core], links.other_core()))
    swaps.append(links.send(outs[small], their_small, links.other_core()))
    for copy in swaps:
        copy.wait_recv()
    links.finish()


def weight_sums(named, partials):
    arrays = {name: pieces(name, w) for name, w in named.items()}
    names = list(arrays)
    groups = weight_cuts({name: w.shape for name, w in arrays.items()})
    jobs = [cut for group in groups for cut in group]
    accs = [pltpu.VMEM(cut.acc_shape(), BF16) for cut in jobs]
    slots = [pltpu.VMEM(shape, BF16) for cut in jobs for shape in cut.slots()]
    copies = 10 * len(jobs) + 4 + len(partials)
    any_space = pl.BlockSpec(memory_space=pl.ANY)
    shared = arrays["basis"].shape[1:]
    shapes = [w.shape for w in (*arrays.values(), *partials, arrays["small"])]
    outs = pl.pallas_call(
        functools.partial(weight_kernel, groups, len(arrays), names.index("basis"), names.index("small"), len(partials)),
        out_shape=[jax.ShapeDtypeStruct(shape, BF16) for shape in shapes],
        in_specs=[any_space] * (len(arrays) + len(partials)),
        out_specs=[any_space] * len(shapes),
        scratch_shapes=[*accs, *slots, pltpu.VMEM(shared, BF16), pltpu.VMEM(shared, BF16),
                        pltpu.SemaphoreType.DMA((2 * len(jobs) + 1,)), pltpu.SemaphoreType.DMA((copies,)),
                        pltpu.SemaphoreType.DMA((copies,))],
        compiler_params=pltpu.CompilerParams(collective_id=3, has_side_effects=True, vmem_limit_bytes=24 * 2**20),
        name="weight_sums",
    )(*arrays.values(), *partials)
    count = len(arrays)
    sums = [o.reshape(w.shape) for o, w in zip(outs, named.values())]
    return sums, outs[count:-1], outs[-1].reshape(named["small"].shape)


def norm_back(inputs, row_scale, gain_vec, grad_rows):
    weighted = grad_rows * gain_vec
    cubed = row_scale * row_scale * row_scale
    input_part = row_scale * weighted - inputs * cubed * jnp.mean(inputs * weighted, axis=-1, keepdims=True)
    gain_part = jnp.sum(grad_rows * inputs * row_scale, axis=(0, 1))
    return (input_part, gain_part)


def project(activations, weight):
    return jnp.einsum("rsd,de->rse", activations, weight, preferred_element_type=F32)


def back_project(grad_rows, weight):
    return jnp.einsum("rse,de->rsd", grad_rows, weight, preferred_element_type=F32)


def weight_grad(normed, grad_rows):
    return jnp.einsum("rsd,rse->de", normed, grad_rows, preferred_element_type=F32)


def head_sum(partial, ident):
    if on_known_slice():
        return pair_sum(partial.astype(BF16), ident).astype(F32)
    return lax.psum(partial.astype(BF16), "head").astype(F32)


def rms_scale(tensor):
    return lax.rsqrt(jnp.mean(tensor * tensor, axis=-1, keepdims=True) + EPS)


def query_table(head_count):
    hd = head_count * DH
    factor = jnp.arange(head_count * RQ, dtype=jnp.int32)[:, None]
    col = jnp.arange(RQ * hd, dtype=jnp.int32)[None, :]
    return jnp.where(factor == col % hd // DH * RQ + col // hd, 1.0, 0.0).astype(BF16)


def rope_tables(position):
    half = DH // 2
    frequency = jnp.exp(jnp.arange(half).astype(F32) * (-2.0 * math.log(10000.0) / DH))
    angles = position[:, None] * frequency[None, :]
    cos, sin = jnp.cos(angles), jnp.sin(angles)
    return jnp.concatenate([cos] * 4, axis=1), jnp.concatenate([-sin, sin, -sin, sin], axis=1)


def shards(
    block_input,
    seq_lengths,
    attn_gain,
    query_heads,
    query_basis,
    key_heads,
    key_basis,
    value_heads,
    value_basis,
    out_project,
    ffn_gain,
    gate_weight,
    up_weight,
    down_weight,
    out_cotangent,
):
    row_count, slot_count, model_dim = block_input.shape
    head_count = query_heads.shape[1] // RQ
    hd = head_count * DH
    length = slot_count * lax.axis_size("seq")
    first_slot = lax.axis_index("seq") * slot_count
    width = head_count * (RK + RV)
    pack_rows = max(n for n in range(1, row_count + 1) if row_count % n == 0 and n * width <= LANES)
    group = min(4, head_count)
    block = math.gcd(length, KEY_BLOCK)
    query_spread = query_table(head_count)
    cos, sin = rope_tables((first_slot + jnp.arange(slot_count, dtype=jnp.int32)).astype(F32))
    normed, aq, bq, own_kv, own_heads, *queries = factors(
        block_input, attn_gain, query_heads.T, query_basis, key_basis, value_basis, key_heads.T, value_heads.T, cos, sin,
        query_spread, pack_rows, width, not on_known_slice())
    inputs = block_input.astype(F32)
    scale_one = rms_scale(inputs)
    shift = (1 - lax.axis_index("head")) * (row_count // CORES) if on_known_slice() else jnp.zeros((), jnp.int32)
    info = jnp.stack([*[seq_lengths[r] for r in range(row_count)], shift, first_slot]).astype(jnp.int32)
    if on_known_slice():
        kv, attended, mixed_flat, lse, queries = collect(
            seq_lengths, own_kv, own_heads, aq, bq, query_spread, pack_rows, group, width)
    else:
        (queries,) = queries
        kv = lax.all_gather(jnp.concatenate([own_kv, own_heads], axis=0), "seq", axis=1, tiled=True)
        attended, mixed_flat, lse = attend(info, queries, kv, pack_rows, group, block, width)
    attn_out = head_sum(project(mixed_flat, out_project), 4)
    middle = inputs + attn_out
    scale_two = rms_scale(middle)
    normed_two = (middle * scale_two * ffn_gain).astype(BF16)
    gate_act = project(normed_two, gate_weight)
    up_act = project(normed_two, up_weight)
    sigmoid_gate = jax.nn.sigmoid(gate_act)
    silu_gate = gate_act * sigmoid_gate
    hidden = (silu_gate * up_act).astype(BF16)
    ffn_part = project(hidden, down_weight).astype(BF16)
    cotangent = out_cotangent.astype(F32)
    d_hidden = jnp.einsum("rsd,fd->rsf", out_cotangent, down_weight, preferred_element_type=F32)
    d_gate = (d_hidden * up_act * (sigmoid_gate * (1.0 + gate_act * (1.0 - sigmoid_gate)))).astype(BF16)
    d_up = (d_hidden * silu_gate).astype(BF16)
    known = on_known_slice()
    model_cut, gate_cut = (model_dim // 2, model_dim // 4) if known else (model_dim, 0)
    gate_grad = weight_grad(normed_two[..., gate_cut:], d_gate)
    up_grad = weight_grad(normed_two, d_up)
    down_grad = weight_grad(hidden, out_cotangent[..., :model_cut])
    d_normed_two = head_sum(back_project(d_gate, gate_weight) + back_project(d_up, up_weight), 6)
    d_middle_norm, ffn_gain_part = norm_back(middle, scale_two, ffn_gain, d_normed_two)
    d_middle = cotangent + d_middle_norm
    d_branch = d_middle.astype(BF16)
    out_project_grad = jnp.einsum("rsf,rsd->fd", mixed_flat, d_branch, preferred_element_type=F32)
    d_mixed = back_project(d_branch, out_project).astype(BF16)
    d_queries, d_kv, d_heads = attend_back(info, queries, kv, attended, d_mixed, lse, pack_rows, group, block, width)
    packs = row_count // pack_rows
    if known:
        down_right = weight_grad(hidden, out_cotangent[..., model_cut:])
        gate_top = weight_grad(normed_two[..., :gate_cut], d_gate)
        (dk_basis, dv_basis, d_heads_own, dq_heads, dq_basis), (down_right, gate_top, out_project_grad) = give_back(
            d_kv, d_heads, cos, sin, d_queries, aq, bq, query_spread, pack_rows,
            {"down": down_right.astype(BF16), "gate": gate_top.astype(BF16), "out": out_project_grad.astype(BF16)})
    else:
        dq_heads, dq_basis = query_grads(d_queries, aq, bq, query_spread, cos, sin, pack_rows)
        key_grads = lax.psum_scatter(
            jnp.concatenate([d_kv, d_heads], axis=0), "seq", scatter_dimension=1, tiled=True)
        d_kv_own = key_grads[: 2 * row_count].reshape(row_count, 2, slot_count, LANES)
        half = DH // 2
        pairs = d_kv_own[:, 0].astype(F32).reshape(row_count, slot_count, 2, 2, half)
        u, w = pairs[:, :, :, 0], pairs[:, :, :, 1]
        c, s = cos[None, :, None, :half], sin[None, :, None, half:DH]
        dk_basis = jnp.stack([u * c + w * s, w * c - u * s], axis=3).reshape(row_count, slot_count, LANES).astype(BF16)
        dv_basis = d_kv_own[:, 1]
        d_heads_own = key_grads[2 * row_count :]
    d_heads_own = d_heads_own[:, :, : width * pack_rows].reshape(packs, slot_count, pack_rows, width)
    d_heads_own = jnp.transpose(d_heads_own, (0, 2, 1, 3)).reshape(row_count, slot_count, width)
    dk_heads, dv_heads = d_heads_own[..., : head_count * RK], d_heads_own[..., head_count * RK :]
    normed_part = (
        back_project(dq_heads, query_heads) + back_project(dq_basis, query_basis)
        + back_project(dk_heads, key_heads) + back_project(dk_basis, key_basis)
        + back_project(dv_heads, value_heads) + back_project(dv_basis, value_basis))
    attn_gain_part = jnp.sum(normed_part * inputs * scale_one, axis=(0, 1))
    normed_part = normed_part.astype(BF16)
    head_grads = weight_grad(jnp.concatenate([dq_heads, dk_heads, dv_heads], axis=-1), normed)
    basis_grads = weight_grad(normed, jnp.concatenate([dq_basis, dk_basis, dv_basis], axis=-1))
    small = jnp.concatenate([head_grads, attn_gain_part[None], ffn_gain_part[None]], axis=0).astype(BF16)
    gain_at = head_grads.shape[0]
    if known:
        gate_grad, up_grad, down_grad = [
            t.astype(F32) for t in lax.psum(tuple(t.astype(BF16) for t in (gate_grad, up_grad, down_grad)), "seq")]
        gate_grad = jnp.concatenate([gate_top.astype(F32), gate_grad], axis=0)
        down_grad = jnp.concatenate([down_grad, down_right.astype(F32)], axis=1)
        height = small.shape[0]
        wide = model_dim // LANES
        small = jnp.pad(small, ((0, -height % 32), (0, 0)))
        full = small.shape[0]
        small = jnp.transpose(small.reshape(full, wide, LANES), (1, 0, 2))
        (small, basis_grads), (normed_other, ffn_other), small_other = weight_sums(
            {"small": small, "basis": basis_grads.astype(BF16)}, (normed_part, ffn_part))
        attn_gain_grad = (small[:, gain_at].astype(F32) + small_other[:, gain_at].astype(F32)).reshape(model_dim)
        small = jnp.transpose(small, (1, 0, 2)).reshape(full, model_dim)
        d_normed = normed_part.astype(F32) + normed_other.astype(F32)
        ffn_out = ffn_part.astype(F32) + ffn_other.astype(F32)
    else:
        sums = lax.psum(tuple(t.astype(BF16) for t in (gate_grad, up_grad, down_grad, out_project_grad, small)), "seq")
        gate_grad, up_grad, down_grad, out_project_grad, small = [t.astype(F32) for t in sums]
        attn_gain_grad = lax.psum(small[gain_at].astype(BF16), "head").astype(F32)
        basis_grads = lax.psum(basis_grads, ("seq", "head"))
        d_normed = lax.psum(normed_part, "head").astype(F32)
        ffn_out = lax.psum(ffn_part, "head").astype(F32)
    d_input_norm, _ = norm_back(inputs, scale_one, attn_gain, d_normed)
    input_grad = d_middle + d_input_norm
    block_output = (middle + ffn_out).astype(BF16)
    nq, nk, nv = head_count * RQ, head_count * RK, head_count * RV
    cuts = (0, nq, nq + nk, nq + nk + nv)
    query_heads_grad, key_heads_grad, value_heads_grad = [small[i:j].astype(F32).T for i, j in zip(cuts, cuts[1:])]
    cuts = (0, RQ * DH, (RQ + RK) * DH, (RQ + RK + RV) * DH)
    query_basis_grad, key_basis_grad, value_basis_grad = [basis_grads[:, i:j].astype(F32) for i, j in zip(cuts, cuts[1:])]
    return (
        block_output,
        input_grad,
        attn_gain_grad,
        query_heads_grad,
        query_basis_grad,
        key_heads_grad,
        key_basis_grad,
        value_heads_grad,
        value_basis_grad,
        out_project_grad.astype(F32),
        small[nq + nk + nv + 1].astype(F32),
        gate_grad,
        up_grad,
        down_grad,
    )


def solution(mesh):
    rows = P(None, "seq", None)
    columns, features = P(None, "head"), P("head", None)
    in_specs = (rows, P(), P(), columns, P(), columns, P(), columns, P(), features, P(), columns, columns, features, rows)
    out_specs = (rows, rows, P(), columns, P(), columns, P(), columns, P(), features, P(), columns, columns, features)
    return jax.shard_map(shards, mesh=mesh, in_specs=in_specs, out_specs=out_specs, check_vma=False)
```

```python
import functools
import math

import jax
import jax.numpy as jnp
from jax import lax
from jax.experimental import pallas as pl
from jax.experimental.pallas import tpu as pltpu
from jax.sharding import PartitionSpec as P

DH = 64
RQ = 6
RK = 2
RV = 2
LANES = 128
EPS = 1e-06
KEY_BLOCK = 256
F32 = jnp.float32
BF16 = jnp.bfloat16


def dot(a, b):
    return lax.dot_general(a, b, (((1,), (0,)), ((), ())), preferred_element_type=F32)


def dot_nt(a, b):
    return lax.dot_general(a, b, (((1,), (1,)), ((), ())), preferred_element_type=F32)


def dot_tn(a, b):
    return lax.dot_general(a, b, (((0,), (0,)), ((), ())), preferred_element_type=F32)


def lane_of(shape):
    return lax.broadcasted_iota(jnp.int32, shape, len(shape) - 1)


def both_halves(pair):
    swapped = pltpu.roll(pair, DH, 1)
    low = lane_of(pair.shape) < DH
    return jnp.where(low, pair, swapped), jnp.where(low, swapped, pair)


def turn(pair, cos, sin):
    half = DH // 2
    first = lane_of(pair.shape) % DH < half
    other = jnp.where(first, pltpu.roll(pair, LANES - half, 1), pltpu.roll(pair, half, 1))
    return pair * cos + other * sin


def split_heads(rows, head_rows, tokens):
    group = lane_of(rows.shape) // DH
    return jnp.concatenate([jnp.where(group == h, rows, jnp.zeros_like(rows)) for h in range(head_rows)], axis=0)


def join_heads(block, head_rows, tokens):
    out = block[:tokens]
    group = lane_of(out.shape) // DH
    for h in range(1, head_rows):
        out = jnp.where(group == h, block[h * tokens : (h + 1) * tokens], out)
    return out


def query_rows(aq, bq, eq_ref, hd):
    aq_high = aq.astype(BF16)
    aq_low = (aq - aq_high.astype(F32)).astype(BF16)
    total = [None] * (hd // LANES)
    for p in range(RQ // 2):
        for half, vec in enumerate(both_halves(bq[:, p * LANES : (p + 1) * LANES])):
            spread = eq_ref[:, (2 * p + half) * hd : (2 * p + half + 1) * hd]
            coef = dot(aq_high, spread) + dot(aq_low, spread)
            for c in range(hd // LANES):
                term = coef[:, c * LANES : (c + 1) * LANES] * vec
                total[c] = term if total[c] is None else total[c] + term
    return [((t / RQ).astype(BF16).astype(F32) * (1.0 / math.sqrt(DH))).astype(BF16) for t in total]


def factor_kernel(width, with_queries, x_ref, gain_ref, wqh_ref, wqb_ref, wkb_ref, wvb_ref, wkh_ref, wvh_ref, cos_ref, sin_ref,
                  eq_ref, xn_ref, aq_ref, bq_ref, kv_ref, hd_ref, *q_refs):
    rows, tokens, model = x_ref.shape
    count = rows * tokens
    x = x_ref[...].astype(F32).reshape(count, model)
    scale = lax.rsqrt(jnp.mean(x * x, axis=-1, keepdims=True) + EPS)
    xn = (x * scale * gain_ref[...]).astype(BF16)
    xn_ref[...] = xn.reshape(rows, tokens, model)
    cos = jnp.concatenate([cos_ref[...]] * rows, axis=0)
    sin = jnp.concatenate([sin_ref[...]] * rows, axis=0)
    keys = turn(dot(xn, wkb_ref[...]), cos, sin).astype(BF16)
    values = dot(xn, wvb_ref[...]).astype(BF16)
    coefs = [dot_nt(xn, w_ref[...]).astype(BF16) for w_ref in (wkh_ref, wvh_ref)]
    pack = jnp.zeros((tokens, LANES), F32)
    for r in range(rows):
        part = slice(r * tokens, (r + 1) * tokens)
        kv_ref[2 * r] = keys[part]
        kv_ref[2 * r + 1] = values[part]
        at = r * width
        for coef in coefs:
            n = coef.shape[1]
            to = lane_of((n, LANES)) == lax.broadcasted_iota(jnp.int32, (n, LANES), 0) + at
            pack = pack + dot(coef[part], jnp.where(to, 1.0, 0.0).astype(BF16))
            at += n
    hd_ref[0] = pack.astype(BF16)
    aq = dot_nt(xn, wqh_ref[...])
    aq_ref[...] = aq.reshape(rows, tokens, aq.shape[1])
    basis = dot(xn, wqb_ref[...])
    bq = jnp.concatenate([turn(basis[:, p : p + LANES], cos, sin) for p in range(0, RQ * DH, LANES)], axis=1)
    bq_ref[...] = bq.reshape(rows, tokens, RQ * DH)
    if with_queries:
        for c, q in enumerate(query_rows(aq, bq, eq_ref, q_refs[0].shape[2])):
            q_refs[0][:, :, c * LANES : (c + 1) * LANES] = q.reshape(rows, tokens, LANES)


def whole(*shape):
    return pl.BlockSpec(shape, lambda *_: (0,) * len(shape))


def factors(x, gain, wqh, wqb, wkb, wvb, wkh, wvh, cos, sin, eq, pack_rows, width, with_queries):
    rows, tokens, model = x.shape
    hd = eq.shape[1] // RQ
    packs = rows // pack_rows
    nq = wqh.shape[0]

    def row_block(last):
        return pl.BlockSpec((pack_rows, tokens, last), lambda g: (g, 0, 0))

    out_specs = [row_block(model), row_block(nq), row_block(RQ * DH),
                 pl.BlockSpec((2 * pack_rows, tokens, LANES), lambda g: (g, 0, 0)),
                 pl.BlockSpec((1, tokens, LANES), lambda g: (g, 0, 0))]
    out_shape = [
        jax.ShapeDtypeStruct((rows, tokens, model), BF16),
        jax.ShapeDtypeStruct((rows, tokens, nq), F32),
        jax.ShapeDtypeStruct((rows, tokens, RQ * DH), F32),
        jax.ShapeDtypeStruct((2 * rows, tokens, LANES), BF16),
        jax.ShapeDtypeStruct((packs, tokens, LANES), BF16),
    ]
    if with_queries:
        out_specs.append(row_block(hd))
        out_shape.append(jax.ShapeDtypeStruct((rows, tokens, hd), BF16))
    return pl.pallas_call(
        functools.partial(factor_kernel, width, with_queries),
        grid=(packs,),
        in_specs=[row_block(model), whole(1, model), *[whole(*w.shape) for w in (wqh, wqb, wkb, wvb, wkh, wvh, cos, sin, eq)]],
        out_specs=out_specs,
        out_shape=out_shape,
        compiler_params=pltpu.CompilerParams(vmem_limit_bytes=58 * 2**20),
        name="factors",
    )(x, gain.reshape(1, model), wqh, wqb, wkb, wvb, wkh, wvh, cos, sin, eq)


def query_grad_rows(dq, aq, bq, eq_ref, cos, sin):
    hd = dq.shape[1]
    aq_high = aq.astype(BF16)
    aq_low = (aq - aq_high.astype(F32)).astype(BF16)
    da = jnp.zeros(aq.shape, F32)
    low = lane_of((dq.shape[0], LANES)) < DH
    turned = []
    for p in range(RQ // 2):
        sums = []
        for half, vec in enumerate(both_halves(bq[:, p * LANES : (p + 1) * LANES])):
            spread = eq_ref[:, (2 * p + half) * hd : (2 * p + half + 1) * hd]
            coef = dot(aq_high, spread) + dot(aq_low, spread)
            acc = None
            prods = []
            for c in range(hd // LANES):
                part = dq[:, c * LANES : (c + 1) * LANES]
                term = coef[:, c * LANES : (c + 1) * LANES] * part
                acc = term if acc is None else acc + term
                prods.append(part * vec)
            prod = jnp.concatenate(prods, axis=1)
            high = prod.astype(BF16)
            rest = (prod - high.astype(F32)).astype(BF16)
            da = da + dot_nt(high, spread) + dot_nt(rest, spread)
            sums.append(acc + pltpu.roll(acc, DH, 1))
        turned.append(turn(jnp.where(low, sums[0], sums[1]), cos, -sin) * (1.0 / RQ))
    return (da * (1.0 / RQ)).astype(BF16), jnp.concatenate(turned, axis=1).astype(BF16)


def query_grad_kernel(dq_ref, aq_ref, bq_ref, eq_ref, cos_ref, sin_ref, da_ref, db_ref):
    rows, tokens, hd = dq_ref.shape
    count = rows * tokens
    da, db = query_grad_rows(
        dq_ref[...].reshape(count, hd), aq_ref[...].reshape(count, -1), bq_ref[...].reshape(count, -1), eq_ref,
        jnp.concatenate([cos_ref[...]] * rows, axis=0), jnp.concatenate([sin_ref[...]] * rows, axis=0))
    da_ref[...] = da.reshape(da_ref.shape)
    db_ref[...] = db.reshape(db_ref.shape)


def query_grads(dq, aq, bq, eq, cos, sin, pack_rows):
    rows, tokens, hd = dq.shape
    nq = aq.shape[2]

    def row_block(last):
        return pl.BlockSpec((pack_rows, tokens, last), lambda g: (g, 0, 0))

    return pl.pallas_call(
        query_grad_kernel,
        grid=(rows // pack_rows,),
        in_specs=[row_block(hd), row_block(nq), row_block(RQ * DH), whole(*eq.shape), whole(*cos.shape), whole(*sin.shape)],
        out_specs=[row_block(nq), row_block(RQ * DH)],
        out_shape=[jax.ShapeDtypeStruct((rows, tokens, nq), BF16), jax.ShapeDtypeStruct((rows, tokens, RQ * DH), BF16)],
        compiler_params=pltpu.CompilerParams(vmem_limit_bytes=56 * 2**20),
        name="query_grads",
    )(dq, aq, bq, eq, cos, sin)


def key_rows(basis):
    turned = basis.astype(F32).T * 0.5
    return turned[:DH], turned[DH:]


def build_heads(coefs, first, second, head_count):
    return jnp.concatenate(
        [coefs[2 * h : 2 * h + 1] * first + coefs[2 * h + 1 : 2 * h + 2] * second for h in range(head_count)], axis=0
    ).astype(BF16)


def row_limits(info_ref, row, tokens, block, lanes):
    first = info_ref[info_ref.shape[0] - 1]
    length = info_ref[row]
    used = jnp.minimum(length, first + tokens)
    slot = lax.broadcasted_iota(jnp.int32, (lanes, 1), 0) % tokens
    return jnp.minimum(first + slot, length - 1), (used + block - 1) // block


def forward_row(q, read, place, width, limit, blocks, block, group, ct_ref):
    tokens, hd = q.shape
    head_count = hd // DH
    lanes = group * tokens
    wide = group * DH
    groups = hd // wide
    queries = [split_heads(q[:, g * wide : (g + 1) * wide], group, tokens) for g in range(groups)]

    def one(b, carry):
        ct_ref[...] = read(2, b).astype(F32).T
        coefs = ct_ref[pl.ds(place, width), :]
        keys = build_heads(coefs[: RK * head_count], *key_rows(read(0, b)), head_count)
        values = build_heads(coefs[RK * head_count :], *key_rows(read(1, b)), head_count)
        live = b * block + lax.broadcasted_iota(jnp.int32, (1, block), 1) <= limit
        out = []
        for g in range(groups):
            peak, total, mixed = carry[g]
            raw = jnp.where(live, dot(queries[g], keys[g * wide : (g + 1) * wide]), -1e30)
            top = jnp.maximum(peak, jnp.max(raw, axis=1, keepdims=True))
            e = jnp.exp(raw - top)
            keep = jnp.exp(peak - top)
            total = total * keep + jnp.sum(e, axis=1, keepdims=True)
            mixed = mixed * keep + dot_nt(e.astype(BF16), values[g * wide : (g + 1) * wide])
            out.append((top, total, mixed))
        return tuple(out)

    start = (jnp.full((lanes, 1), -1e30, F32), jnp.zeros((lanes, 1), F32), jnp.zeros((lanes, wide), F32))
    done = lax.fori_loop(0, blocks, one, (start,) * groups)
    lane = lane_of((tokens, LANES))
    lse = jnp.zeros((tokens, LANES), F32)
    parts = []
    for g in range(groups):
        peak, total, mixed = done[g]
        parts.append(join_heads(mixed / total, group, tokens))
        level = peak + jnp.log(total)
        for h in range(group):
            lse = jnp.where(lane == g * group + h, level[h * tokens : (h + 1) * tokens], lse)
    return parts, lse


def attend_kernel(pack_rows, group, block, width, info_ref, q_ref, kv_ref, hd_ref, o_ref, ob_ref, lse_ref, ct_ref):
    row = pl.program_id(0)
    _, tokens, hd = q_ref.shape
    wide = group * DH
    limit, blocks = row_limits(info_ref, row, tokens, block, group * tokens)

    def read(i, b):
        at = pl.ds(pl.multiple_of(b * block, block), block)
        return hd_ref[0, at, :] if i == 2 else kv_ref[i, at, :]

    parts, lse_ref[0] = forward_row(
        q_ref[0], read, pl.multiple_of(row % pack_rows * width, 8), width, limit, blocks, block, group, ct_ref)
    for g, mixed in enumerate(parts):
        o_ref[0, :, g * wide : (g + 1) * wide] = mixed
        ob_ref[0, :, g * wide : (g + 1) * wide] = mixed.astype(BF16)


def attend(info, q, kv, pack_rows, group, block, width):
    rows, tokens, hd = q.shape
    length = kv.shape[1]

    def own(r, i):
        return (r, 0, 0)

    grid_spec = pltpu.PrefetchScalarGridSpec(
        num_scalar_prefetch=1,
        grid=(rows,),
        in_specs=[
            pl.BlockSpec((1, tokens, hd), own),
            pl.BlockSpec((2, length, LANES), lambda r, i: (lax.rem(r + i[rows], rows), 0, 0)),
            pl.BlockSpec((1, length, LANES), lambda r, i: (2 * rows + r // pack_rows, 0, 0)),
        ],
        out_specs=[pl.BlockSpec((1, tokens, hd), own), pl.BlockSpec((1, tokens, hd), own), pl.BlockSpec((1, tokens, LANES), own)],
        scratch_shapes=[pltpu.VMEM((LANES, block), F32)],
    )
    return pl.pallas_call(
        functools.partial(attend_kernel, pack_rows, group, block, width),
        grid_spec=grid_spec,
        out_shape=[
            jax.ShapeDtypeStruct((rows, tokens, hd), F32),
            jax.ShapeDtypeStruct((rows, tokens, hd), BF16),
            jax.ShapeDtypeStruct((rows, tokens, LANES), F32),
        ],
        compiler_params=pltpu.CompilerParams(vmem_limit_bytes=32 * 2**20),
        name="attend",
    )(info, q, kv, kv)


def attend_back_kernel(pack_rows, group, block, width, info_ref, q_ref, kv_ref, hd_ref, o_ref, do_ref, lse_ref,
                       dq_ref, dkv_ref, dhd_ref, dq_acc, ct_ref, dct_ref):
    row = pl.program_id(0)
    _, tokens, hd = q_ref.shape
    head_count = hd // DH
    lanes = group * tokens
    wide = group * DH
    groups = hd // wide
    limit, blocks = row_limits(info_ref, row, tokens, block, lanes)
    place = pl.multiple_of(row % pack_rows * width, 8)
    queries, grads, deltas, levels = [], [], [], []
    for g in range(groups):
        part = slice(g * wide, (g + 1) * wide)
        do = do_ref[0, :, part]
        queries.append(split_heads(q_ref[0, :, part], group, tokens))
        grads.append(split_heads(do, group, tokens))
        weighed = split_heads(do.astype(F32) * o_ref[0, :, part], group, tokens)
        deltas.append(jnp.sum(weighed, axis=1, keepdims=True))
        levels.append(jnp.concatenate([lse_ref[0, :, h : h + 1] for h in range(g * group, (g + 1) * group)], axis=0))
    queries_t = [q.astype(F32).T.astype(BF16) for q in queries]
    grads_t = [g.astype(F32).T.astype(BF16) for g in grads]
    dq_acc[...] = jnp.zeros_like(dq_acc)
    dkv_ref[...] = jnp.zeros_like(dkv_ref)
    dct_ref[...] = jnp.zeros_like(dct_ref)

    @pl.when(row % pack_rows == 0)
    def _():
        dhd_ref[...] = jnp.zeros_like(dhd_ref)

    def factor_grads(grad, coefs, vectors):
        sums, rows = [None, None], []
        for h in range(head_count):
            part = grad[h * DH : (h + 1) * DH]
            for r in range(2):
                term = coefs[2 * h + r : 2 * h + r + 1] * part
                sums[r] = term if h == 0 else sums[r] + term
                rows.append(jnp.sum(part * vectors[r], axis=0, keepdims=True))
        return (jnp.concatenate(sums, axis=0) * 0.5).T.astype(BF16), rows

    def one(b, carry):
        at = pl.ds(pl.multiple_of(b * block, block), block)
        ct_ref[...] = hd_ref[0, at, :].astype(F32).T
        coefs = ct_ref[pl.ds(place, width), :]
        key_coefs, value_coefs = coefs[: RK * head_count], coefs[RK * head_count :]
        key_vectors, value_vectors = key_rows(kv_ref[0, at, :]), key_rows(kv_ref[1, at, :])
        keys = build_heads(key_coefs, *key_vectors, head_count)
        values = build_heads(value_coefs, *value_vectors, head_count)
        live = b * block + lax.broadcasted_iota(jnp.int32, (1, block), 1) <= limit
        dks, dvs = [], []
        for g in range(groups):
            part = slice(g * wide, (g + 1) * wide)
            p = jnp.where(live, jnp.exp(dot(queries[g], keys[part]) - levels[g]), 0.0)
            dp = dot(grads[g], values[part])
            ds = (p * (dp - deltas[g])).astype(BF16)
            dvs.append(dot(grads_t[g], p.astype(BF16)))
            dks.append(dot(queries_t[g], ds))
            dq_acc[g] += dot_nt(ds, keys[part])
        dkv_ref[0, at, :], key_grads = factor_grads(jnp.concatenate(dks, axis=0), key_coefs, key_vectors)
        dkv_ref[1, at, :], value_grads = factor_grads(jnp.concatenate(dvs, axis=0), value_coefs, value_vectors)
        dct_ref[pl.ds(place, width), :] = jnp.concatenate(key_grads + value_grads, axis=0)
        dhd_ref[0, at, :] = (dhd_ref[0, at, :].astype(F32) + dct_ref[...].T).astype(BF16)
        return carry

    lax.fori_loop(0, blocks, one, 0)
    for g in range(groups):
        dq_ref[0, :, g * wide : (g + 1) * wide] = join_heads(dq_acc[g], group, tokens) * (1.0 / math.sqrt(DH))


def attend_back(info, q, kv, o, do, lse, pack_rows, group, block, width):
    rows, tokens, hd = q.shape
    length = kv.shape[1]
    packs = rows // pack_rows

    def place(r, i):
        return (lax.rem(r + i[rows], rows), 0, 0)

    def own(r, i):
        return (r, 0, 0)

    grid_spec = pltpu.PrefetchScalarGridSpec(
        num_scalar_prefetch=1,
        grid=(rows,),
        in_specs=[
            pl.BlockSpec((1, tokens, hd), own),
            pl.BlockSpec((2, length, LANES), place),
            pl.BlockSpec((1, length, LANES), lambda r, i: (2 * rows + r // pack_rows, 0, 0)),
            pl.BlockSpec((1, tokens, hd), own),
            pl.BlockSpec((1, tokens, hd), own),
            pl.BlockSpec((1, tokens, LANES), own),
        ],
        out_specs=[
            pl.BlockSpec((1, tokens, hd), own),
            pl.BlockSpec((2, length, LANES), place),
            pl.BlockSpec((1, length, LANES), lambda r, i: (r // pack_rows, 0, 0)),
        ],
        scratch_shapes=[pltpu.VMEM((hd // (group * DH), group * tokens, group * DH), F32),
                        pltpu.VMEM((LANES, block), F32), pltpu.VMEM((LANES, block), F32)],
    )
    return pl.pallas_call(
        functools.partial(attend_back_kernel, pack_rows, group, block, width),
        grid_spec=grid_spec,
        out_shape=[
            jax.ShapeDtypeStruct((rows, tokens, hd), F32),
            jax.ShapeDtypeStruct((2 * rows, length, LANES), BF16),
            jax.ShapeDtypeStruct((packs, length, LANES), BF16),
        ],
        compiler_params=pltpu.CompilerParams(vmem_limit_bytes=58 * 2**20),
        name="attend_back",
    )(info, q, kv, kv, o, do, lse)


MESH = pl.DeviceIdType.MESH
SIZES = {"z": 4, "y": 2, "x": 2}
STRIDES = {"z": 4, "y": 2, "x": 1}
CORES = 2


def on_known_slice():
    return lax.axis_size("seq") == math.prod(SIZES.values()) and lax.axis_size("head") == CORES


class Links:
    def __init__(self, send_sems, recv_sems):
        self.seq = lax.axis_index("seq")
        self.core = lax.axis_index("head")
        self.at = {d: lax.rem(self.seq // STRIDES[d], SIZES[d]) for d in SIZES}
        self.send_sems, self.recv_sems = send_sems, recv_sems
        self.count = 0
        self.started = []

    def along(self, d, offset):
        there = lax.rem(self.at[d] + offset, SIZES[d])
        return there, (self.seq + (there - self.at[d]) * STRIDES[d], self.core)

    def other_core(self):
        return (self.seq, 1 - self.core)

    def greet(self, core, chips=True):
        barrier = pltpu.get_barrier_semaphore()
        devices = [self.other_core()] if core else []
        if chips:
            devices += [self.along(d, o)[1] for d in SIZES for o in range(1, SIZES[d])]
        for device in devices:
            pl.semaphore_signal(barrier, inc=1, device_id=device, device_id_type=MESH)
        pl.semaphore_wait(barrier, len(devices))

    def send(self, src, dst, device):
        copy = pltpu.make_async_remote_copy(
            src_ref=src, dst_ref=dst, send_sem=self.send_sems.at[self.count], recv_sem=self.recv_sems.at[self.count],
            device_id=device, device_id_type=MESH)
        self.count += 1
        copy.start()
        self.started.append(copy)
        return copy

    def finish(self):
        for copy in self.started:
            copy.wait_send()


def accumulate(acc, slots):
    lead = acc.shape[:-2]

    def body(i, carry):
        at = []
        for size in reversed(lead):
            at.insert(0, lax.rem(i, size))
            i = i // size
        value = acc[(*at, slice(None), slice(None))].astype(F32)
        for o in range(slots.shape[0]):
            value = value + slots[(o, *at, slice(None), slice(None))].astype(F32)
        acc[(*at, slice(None), slice(None))] = value.astype(BF16)
        return carry

    lax.fori_loop(0, math.prod(lead), body, 0)


def scatter_steps(links, order, source, acc, slots, ready):
    fixed = {}
    for k, d in enumerate(order):
        copies = []
        for o in range(1, SIZES[d]):
            there, device = links.along(d, o)
            view = source if k == 0 else acc
            copies.append(links.send(view({**fixed, d: there}), slots[k].at[o - 1], device))
        yield
        if k == 0:
            ready()
        for copy in copies:
            copy.wait_recv()
        fixed[d] = links.at[d]
        accumulate(acc(fixed), slots[k])


def gather_steps(links, order, out, first):
    for k in reversed(range(len(order))):
        fixed = {d: links.at[d] for d in order[: k + 1]}
        copies = []
        for o in range(1, SIZES[order[k]]):
            _, device = links.along(order[k], o)
            src = first if first is not None and k == len(order) - 1 else out(fixed)
            copies.append(links.send(src, out(fixed), device))
        yield
        for copy in copies:
            copy.wait_recv()


def run_waves(groups):
    live, waiting = [], list(groups)
    while live or waiting:
        if waiting:
            live.append(list(waiting.pop(0)))
        for group in live:
            group[:] = [job for job in group if next(job, "end") != "end"]
        live = [group for group in live if group]


def in_pairs(jobs):
    half = (len(jobs) + 1) // 2
    return [jobs[i : i + 1] + jobs[half + i : half + i + 1] for i in range(half)]


def slot_shapes(order, units, tail):
    shapes, open_dims = [], list(SIZES)
    for d in order:
        open_dims.remove(d)
        shapes.append((SIZES[d] - 1, *units, *[SIZES[e] for e in open_dims], *tail))
    return shapes


def pick(ref, lead, sel, axes, tail=()):
    return ref.at[(*lead, *[sel.get(d, slice(None)) for d in axes], *tail)]


ZYX = ("z", "y", "x")


def collect_jobs(rows, packs):
    step = 1
    own = [(rows + u, min(step, rows - u)) for u in range(0, rows, step)]
    jobs = own + [(2 * rows, packs)]
    half = (len(jobs) + 1) // 2
    return [(first, n, ("y", "x", "z") if i < half else ("x", "y", "z")) for i, (first, n) in enumerate(jobs)]


def collect_groups(rows, packs):
    half = rows // CORES
    lots = [[0]] + [list(range(j, min(j + 2, half))) for j in range(1, half, 2)]
    return [([(2 * rows, packs)] if i == 0 else []) + [(rows + 2 * j, 2) for j in lot] for i, lot in enumerate(lots)], lots


def collect_kernel(pack_rows, group, block, width, len_ref, kv_ref, hd_ref, aq_ref, bq_ref, eq_ref, out_ref, o_ref, ob_ref, lse_ref,
                   q_ref, all_ref, ct_ref, local_sems, out_sems, send_sems, recv_sems):
    rows, tokens, hd = q_ref.shape
    packs = hd_ref.shape[0]
    half = rows // CORES
    wide = group * DH
    planes = block // (SIZES["y"] * SIZES["x"] * tokens)
    links = Links(send_sems, recv_sems)
    own = tuple(links.at[d] for d in ZYX)
    first_slot = links.seq * tokens
    blocks = (first_slot + tokens + block - 1) // block
    groups, lots = collect_groups(rows, packs)
    jobs = [job for lot in groups for job in lot]
    loads = []
    for i, (first, n) in enumerate(jobs):
        src = hd_ref if first == 2 * rows else kv_ref.at[pl.ds(links.core * rows + first - rows, n)]
        loads.append(pltpu.make_async_copy(src, all_ref.at[(pl.ds(first, n), *own)], local_sems.at[i]))
        loads[-1].start()
    links.greet(core=True)
    stores = []

    def keep(first, n):
        store = pltpu.make_async_copy(all_ref.at[pl.ds(first, n)], out_ref.at[pl.ds(first, n)], out_sems.at[len(stores)])
        store.start()
        stores.append(store)

    def job(i, first, n):
        order = ("x", "y", "z") if i % 2 else ("y", "x", "z")
        loads[i].wait()
        yield from gather_steps(links, order, lambda sel: pick(all_ref, [pl.ds(first, n)], sel, ZYX), None)
        if first < 2 * rows:
            copy = links.send(all_ref.at[pl.ds(first, n)], all_ref.at[pl.ds(first - rows, n)], links.other_core())
        keep(first, n)
        if first < 2 * rows:
            yield
            copy.wait_recv()
            keep(first - rows, n)

    def attend_rows(mine, lot):
        def body(i, carry):
            j = lot[0] + i
            row = j + half * (links.core if mine else 1 - links.core)
            unit = rows * mine + 2 * j
            slot = lax.broadcasted_iota(jnp.int32, (group * tokens, 1), 0) % tokens
            limit = jnp.minimum(first_slot + slot, len_ref[row] - 1)
            pack = row // pack_rows
            place = pl.multiple_of((row - pack * pack_rows) * width, 8)

            def read(k, b):
                at = 2 * rows + pack if k == 2 else unit + k
                return all_ref[at, pl.ds(b * planes, planes)].reshape(block, LANES)

            parts, lse_ref[row] = forward_row(q_ref[row], read, place, width, limit, blocks, block, group, ct_ref)
            for g, mixed in enumerate(parts):
                o_ref[row, :, g * wide : (g + 1) * wide] = mixed
                ob_ref[row, :, g * wide : (g + 1) * wide] = mixed.astype(BF16)
            return carry

        lax.fori_loop(0, len(lot), body, 0)

    live, started, wave, i = [], 0, 0, 0
    steps = 3
    while started < len(groups) or live:
        if started < len(groups):
            for first, n in groups[started]:
                live.append(job(i, first, n))
                i += 1
            started += 1
        live[:] = [made for made in live if next(made, "end") != "end"]
        if 0 <= wave - steps - 1 < len(lots):
            attend_rows(0, lots[wave - steps - 1])
        if 0 <= wave - steps < len(lots):
            attend_rows(1, lots[wave - steps])
        if wave < packs:
            part = pl.ds(wave * pack_rows, pack_rows)
            flat = pack_rows * tokens
            made = query_rows(aq_ref[part].reshape(flat, -1), bq_ref[part].reshape(flat, -1), eq_ref, hd)
            for c, q in enumerate(made):
                q_ref[part, :, c * LANES : (c + 1) * LANES] = q.reshape(pack_rows, tokens, LANES)
        wave += 1
    for store in stores:
        store.wait()
    links.finish()


def collect(lengths, kv, hd, aq, bq, eq, pack_rows, group, width):
    units, tokens, _ = kv.shape
    packs = hd.shape[0]
    rows = units // 2
    hidden = (rows, tokens, eq.shape[1] // RQ)
    length = tokens * math.prod(SIZES.values())
    block = length // 2
    count = sum(len(lot) for lot in collect_groups(rows, packs)[0])
    full = (units + packs, *[SIZES[d] for d in ZYX], tokens, LANES)
    vmem, any_space = pl.BlockSpec(memory_space=pltpu.VMEM), pl.BlockSpec(memory_space=pl.ANY)
    out, o, ob, lse, q = pl.pallas_call(
        functools.partial(collect_kernel, pack_rows, group, block, width),
        out_shape=[jax.ShapeDtypeStruct(full, BF16), jax.ShapeDtypeStruct(hidden, F32), jax.ShapeDtypeStruct(hidden, BF16),
                   jax.ShapeDtypeStruct((rows, tokens, LANES), F32), jax.ShapeDtypeStruct(hidden, BF16)],
        in_specs=[pl.BlockSpec(memory_space=pltpu.SMEM), any_space, any_space, vmem, vmem, vmem],
        out_specs=[any_space, vmem, vmem, vmem, vmem],
        scratch_shapes=[pltpu.VMEM(full, BF16), pltpu.VMEM((LANES, block), F32), pltpu.SemaphoreType.DMA((count,)),
                        pltpu.SemaphoreType.DMA((2 * count,)), pltpu.SemaphoreType.DMA((8 * count,)),
                        pltpu.SemaphoreType.DMA((8 * count,))],
        compiler_params=pltpu.CompilerParams(collective_id=1, has_side_effects=True, vmem_limit_bytes=58 * 2**20),
        name="collect",
    )(lengths, kv, hd, aq, bq, eq)
    return out.reshape(units + packs, length, LANES), o, ob, lse, q


def return_kernel(rows, packs, chunk, groups, count, dkv_ref, dhd_ref, cos_ref, sin_ref, dq_ref, aq_ref, bq_ref, eq_ref, *refs):
    ins, refs = refs[:count], refs[count:]
    (dk_ref, dv_ref, dh_ref, da_ref, db_ref), refs = refs[:5], refs[5:]
    outs, refs = refs[:count], refs[count:]
    acc_ref, core_ref, refs = refs[0], refs[1], refs[2:]
    jobs = collect_jobs(rows, packs)
    slot_refs, refs = refs[: 3 * len(jobs)], refs[3 * len(jobs) :]
    cuts = [cut for group in groups for cut in group]
    cut_accs, cut_slots, refs = refs[: len(cuts)], refs[len(cuts) : 4 * len(cuts)], refs[4 * len(cuts) :]
    local_sems, cut_sems, send_sems, recv_sems = refs
    links = Links(send_sems, recv_sems)
    links.greet(core=True)
    own = tuple(links.at[d] for d in ZYX)
    loads, swaps = [], []
    for i, (first, n, _) in enumerate(jobs):
        heads = first == 2 * rows
        part = pl.ds(first - rows, n)
        if not heads:
            swaps.append(links.send(dkv_ref.at[part], core_ref.at[part], links.other_core()))
        load = pltpu.make_async_copy(dhd_ref if heads else dkv_ref.at[pl.ds(first, n)], acc_ref.at[part], local_sems.at[i])
        load.start()
        loads.append(load)
    cut_loads = [start_load(links, cut, ins[cut.array], cut_accs[i], cut_sems.at[2 * i]) for i, cut in enumerate(cuts)]
    dk_ref[...] = jnp.zeros_like(dk_ref)
    dv_ref[...] = jnp.zeros_like(dv_ref)

    def job(i, first, n, order):
        heads = first == 2 * rows
        part = pl.ds(first - rows, n)
        loads[i].wait()
        if not heads:
            swaps[i].wait_recv()

            def add(j, carry):
                u = first - rows + j // SIZES["z"]
                z = lax.rem(j, SIZES["z"])
                acc_ref[u, z] = (acc_ref[u, z].astype(F32) + core_ref[u, z].astype(F32)).astype(BF16)
                return carry

            lax.fori_loop(0, n * SIZES["z"], add, 0)

        def view(sel):
            return pick(acc_ref, [part], sel, ZYX)

        yield from scatter_steps(links, order, view, view, slot_refs[3 * i : 3 * i + 3], lambda: None)
        for u in range(n):
            piece = acc_ref[(first - rows + u, *own)]
            row = links.core * (rows // 2) + (first - rows + u) // 2
            if heads:
                dh_ref[u] = piece
            elif (first - rows + u) % 2 == 0:
                dk_ref[row] = turn(piece.astype(F32), cos_ref[...], -sin_ref[...]).astype(BF16)
            else:
                dv_ref[row] = piece

    def query_part(first):
        part = pl.ds(first, chunk)
        tokens = dq_ref.shape[1]
        cos = jnp.concatenate([cos_ref[...]] * chunk, axis=0)
        sin = jnp.concatenate([sin_ref[...]] * chunk, axis=0)
        da, db = query_grad_rows(dq_ref[part].reshape(chunk * tokens, -1), aq_ref[part].reshape(chunk * tokens, -1),
                                 bq_ref[part].reshape(chunk * tokens, -1), eq_ref, cos, sin)
        da_ref[part] = da.reshape(chunk, tokens, -1)
        db_ref[part] = db.reshape(chunk, tokens, -1)
        yield

    waves = in_pairs([job(i, *j) for i, j in enumerate(jobs)])
    at = 0
    for wave, group in zip(waves, groups):
        for cut in group:
            wave.insert(0, cut_job(links, cut, ins[cut.array], outs[cut.array], cut_accs[at], cut_slots[3 * at : 3 * at + 3],
                                   cut_loads[at], cut_sems.at[2 * at + 1]))
            at += 1
    for i, first in enumerate(range(0, dq_ref.shape[0], chunk)):
        waves[min(i, len(waves) - 1)].append(query_part(first))
    run_waves(waves)
    links.finish()


def give_back(dkv, dhd, cos, sin, dq, aq, bq, eq, chunk, named):
    units, length, _ = dkv.shape
    packs = dhd.shape[0]
    rows = units // 2
    tokens = length // math.prod(SIZES.values())
    dims = tuple(SIZES[d] for d in ZYX)
    jobs = collect_jobs(rows, packs)
    slots = [pltpu.VMEM(shape, BF16) for _, n, order in jobs for shape in slot_shapes(order, (n,), (tokens, LANES))]
    arrays = {name: pieces(name, w) for name, w in named.items()}
    groups = weight_cuts({name: w.shape for name, w in arrays.items()})
    cuts = [cut for group in groups for cut in group]
    copies = 8 * len(jobs) + 10 * len(cuts)
    vmem, any_space = pl.BlockSpec(memory_space=pltpu.VMEM), pl.BlockSpec(memory_space=pl.ANY)
    outs = pl.pallas_call(
        functools.partial(return_kernel, rows, packs, chunk, groups, len(arrays)),
        out_shape=[
            jax.ShapeDtypeStruct((rows, tokens, LANES), BF16),
            jax.ShapeDtypeStruct((rows, tokens, LANES), BF16),
            jax.ShapeDtypeStruct((packs, tokens, LANES), BF16),
            jax.ShapeDtypeStruct(aq.shape, BF16),
            jax.ShapeDtypeStruct(bq.shape, BF16),
            *[jax.ShapeDtypeStruct(w.shape, BF16) for w in arrays.values()],
        ],
        in_specs=[any_space] * 2 + [vmem] * 6 + [any_space] * len(arrays),
        out_specs=[vmem] * 5 + [any_space] * len(arrays),
        scratch_shapes=[pltpu.VMEM((rows + packs, *dims, tokens, LANES), BF16), pltpu.VMEM((rows, *dims, tokens, LANES), BF16),
                        *slots, *[pltpu.VMEM(cut.acc_shape(), BF16) for cut in cuts],
                        *[pltpu.VMEM(shape, BF16) for cut in cuts for shape in cut.slots()],
                        pltpu.SemaphoreType.DMA((len(jobs),)), pltpu.SemaphoreType.DMA((2 * len(cuts),)),
                        pltpu.SemaphoreType.DMA((copies,)), pltpu.SemaphoreType.DMA((copies,))],
        compiler_params=pltpu.CompilerParams(collective_id=2, has_side_effects=True, vmem_limit_bytes=58 * 2**20),
        name="give_back",
    )(dkv.reshape(units, *dims, tokens, LANES), dhd.reshape(packs, *dims, tokens, LANES), cos, sin, dq, aq, bq, eq,
      *arrays.values())
    return outs[:5], [o.reshape(w.shape) for o, w in zip(outs[5:], named.values())]


def pair_kernel(x_ref, out_ref, got_ref, send_sems, recv_sems):
    links = Links(send_sems, recv_sems)
    links.greet(core=True, chips=False)
    copies = [links.send(x_ref.at[r], got_ref.at[r], links.other_core()) for r in range(x_ref.shape[0])]
    for r, copy in enumerate(copies):
        copy.wait_recv()
        out_ref[r] = (x_ref[r].astype(F32) + got_ref[r].astype(F32)).astype(out_ref.dtype)
    links.finish()


def pair_sum(x, ident):
    parts = 4
    rows, tokens, model = x.shape
    flat = x.reshape(parts, rows * tokens // parts, model)
    return pl.pallas_call(
        pair_kernel,
        out_shape=jax.ShapeDtypeStruct(flat.shape, BF16),
        in_specs=[pl.BlockSpec(memory_space=pltpu.VMEM)],
        out_specs=pl.BlockSpec(memory_space=pltpu.VMEM),
        scratch_shapes=[pltpu.VMEM(flat.shape, BF16), pltpu.SemaphoreType.DMA((parts,)), pltpu.SemaphoreType.DMA((parts,))],
        compiler_params=pltpu.CompilerParams(collective_id=ident, has_side_effects=True, vmem_limit_bytes=32 * 2**20),
        name="pair_sum_%d" % ident,
    )(flat).reshape(x.shape)


class Cut:
    def __init__(self, array, axes, rows, cols, order, lane_dim=None, shared=False):
        self.array, self.axes, self.rows, self.cols = array, axes, rows, cols
        self.order, self.lane_dim, self.shared = order, lane_dim, shared

    def tail(self):
        return (self.rows[1], self.cols[1])

    def view(self, ref, sel, core):
        cols = pl.ds(self.cols[0], self.cols[1])
        if self.lane_dim is not None:
            cols = pl.ds(pl.multiple_of(self.cols[0] + sel[self.lane_dim] * self.cols[1], LANES), self.cols[1])
        lead = [core] if self.shared else []
        return pick(ref, lead, sel, self.axes, (pl.ds(self.rows[0], self.rows[1]), cols))

    def inner(self):
        return tuple(d for d in self.axes if d != self.order[0])

    def acc_shape(self):
        return (*[SIZES[d] for d in self.inner()], *self.tail())

    def slots(self):
        shapes, open_dims = [], list(self.inner())
        for d in self.order:
            if d in open_dims:
                open_dims.remove(d)
            shapes.append((SIZES[d] - 1, *[SIZES[e] for e in open_dims], *self.tail()))
        return shapes


def weight_cuts(shapes):
    a, b, c, d = ("x", "y", "z"), ("y", "x", "z"), ("x", "z", "y"), ("y", "z", "x")
    groups = []
    index = {name: i for i, name in enumerate(shapes)}
    axes = ("x", "y", "z")
    if "down" in shapes:
        n, cols = shapes["down"][2:]
        first = n // 32 * 16
        for rows in ((0, first), (first, n - first)):
            groups.append([Cut(index["down"], ("y", "z"), rows, (0, cols // 4), c, lane_dim="x"),
                           Cut(index["down"], ("x", "z"), rows, (cols // 2, cols // 4), d, lane_dim="y")])
    if "gate" in shapes:
        n, cols = shapes["gate"][3:]
        cut = (cols // LANES + 1) // 2 * LANES
        groups.append([Cut(index["gate"], axes, (0, n), (0, cut), a), Cut(index["gate"], axes, (0, n), (cut, cols - cut), b)])
    if "out" in shapes:
        n, cols = shapes["out"][3:]
        for rows in ((0, n // 2), (n // 2, n // 2)):
            groups.append([Cut(index["out"], axes, rows, (0, cols // 2), a), Cut(index["out"], axes, rows, (cols // 2, cols // 2), b)])
    if "small" in shapes:
        m, wide = shapes["small"][3:]
        groups.append([Cut(index["small"], ("y", "z", "x"), (0, m), (0, wide), a)])
    if "basis" in shapes:
        n, cols = shapes["basis"][4:]
        cut = cols // LANES // 2 * LANES
        groups[-1] += [Cut(index["basis"], axes, (0, n), (0, cut), a, shared=True),
                       Cut(index["basis"], axes, (0, n), (cut, cols - cut), b, shared=True)]
    return groups


def pieces(name, w):
    dims = (2, 2, 4)
    chips = math.prod(SIZES.values())
    if name == "basis":
        return w.reshape(CORES, *dims, w.shape[0] // CORES // chips, w.shape[1])
    if name == "down":
        return w.reshape(2, 4, -1, w.shape[1])
    if name == "small":
        return w.reshape(2, 4, 2, -1, LANES)
    return w.reshape(*dims, w.shape[0] // chips, w.shape[1])


def start_load(links, cut, ref, acc, sem):
    if cut.shared:
        return None
    load = pltpu.make_async_copy(cut.view(ref, {cut.order[0]: links.at[cut.order[0]]}, links.core), acc, sem)
    load.start()
    return load


def cut_job(links, cut, in_ref, out_ref, acc_ref, slots, load, store_sem, shared_ref=None):
    def acc(sel):
        return pick(acc_ref, [], sel, cut.inner())

    def source(sel):
        return cut.view(in_ref, sel, links.core)

    def out(sel):
        return cut.view(out_ref, sel, links.core)

    if cut.shared:
        cols = pl.ds(cut.cols[0], cut.cols[1])
        summed = pick(shared_ref, [], {cut.order[0]: links.at[cut.order[0]]}, cut.axes, (slice(None), cols))

        def keep(j, carry):
            p, q = j // acc_ref.shape[1], lax.rem(j, acc_ref.shape[1])
            acc_ref[p, q] = summed[p, q]
            return carry

        lax.fori_loop(0, acc_ref.shape[0] * acc_ref.shape[1], keep, 0)

        def source(sel):
            return pick(shared_ref, [], sel, cut.axes, (slice(None), cols))

    yield from scatter_steps(links, cut.order, source, acc, slots, load.wait if load is not None else lambda: None)
    piece = acc({d: links.at[d] for d in cut.inner()})
    store = pltpu.make_async_copy(piece, out(links.at), store_sem)
    store.start()
    steps = gather_steps(links, cut.order, out, piece)
    next(steps)
    yield
    store.wait()
    yield from steps


def weight_kernel(groups, count, basis, small, swapped, *refs):
    jobs = [cut for group in groups for cut in group]
    ins, mine, refs = refs[:count], refs[count : count + swapped], refs[count + swapped :]
    outs, theirs, their_small, refs = refs[:count], refs[count : count + swapped], refs[count + swapped], refs[count + swapped + 1 :]
    at = 0
    accs = refs[at : at + len(jobs)]
    at += len(jobs)
    slots = refs[at : at + 3 * len(jobs)]
    at += 3 * len(jobs)
    shared_own, shared_got, local_sems, send_sems, recv_sems = refs[at:]
    links = Links(send_sems, recv_sems)
    links.greet(core=True)
    loads = [start_load(links, cut, ins[cut.array], accs[i], local_sems.at[2 * i]) for i, cut in enumerate(jobs)]
    own = pltpu.make_async_copy(ins[basis].at[links.core], shared_own, local_sems.at[2 * len(jobs)])
    own.start()
    swap = links.send(ins[basis].at[1 - links.core], shared_got, links.other_core())
    swaps = [links.send(src, dst, links.other_core()) for src, dst in zip(mine, theirs)]

    def first_shared():
        own.wait()
        swap.wait_recv()

        def add(j, carry):
            shape = shared_own.shape
            p, q, r = j // (shape[1] * shape[2]), lax.rem(j // shape[2], shape[1]), lax.rem(j, shape[2])
            shared_own[p, q, r] = (shared_own[p, q, r].astype(F32) + shared_got[p, q, r].astype(F32)).astype(BF16)
            return carry

        lax.fori_loop(0, math.prod(shared_own.shape[:3]), add, 0)
        return
        yield

    made, i, ready = [], 0, False
    for group in groups:
        lot = []
        for cut in group:
            if cut.shared and not ready:
                lot.append(first_shared())
                ready = True
            lot.append(cut_job(links, cut, ins[cut.array], outs[cut.array], accs[i], slots[3 * i : 3 * i + 3], loads[i],
                               local_sems.at[2 * i + 1], shared_own))
            i += 1
        made.append(lot)
    run_waves(made)
    swaps.append(links.send(outs[basis].at[links.core], outs[basis].at[links.core], links.other_core()))
    swaps.append(links.send(outs[small], their_small, links.other_core()))
    for copy in swaps:
        copy.wait_recv()
    links.finish()


def weight_sums(named, partials):
    arrays = {name: pieces(name, w) for name, w in named.items()}
    names = list(arrays)
    groups = weight_cuts({name: w.shape for name, w in arrays.items()})
    jobs = [cut for group in groups for cut in group]
    accs = [pltpu.VMEM(cut.acc_shape(), BF16) for cut in jobs]
    slots = [pltpu.VMEM(shape, BF16) for cut in jobs for shape in cut.slots()]
    copies = 10 * len(jobs) + 4 + len(partials)
    any_space = pl.BlockSpec(memory_space=pl.ANY)
    shared = arrays["basis"].shape[1:]
    shapes = [w.shape for w in (*arrays.values(), *partials, arrays["small"])]
    outs = pl.pallas_call(
        functools.partial(weight_kernel, groups, len(arrays), names.index("basis"), names.index("small"), len(partials)),
        out_shape=[jax.ShapeDtypeStruct(shape, BF16) for shape in shapes],
        in_specs=[any_space] * (len(arrays) + len(partials)),
        out_specs=[any_space] * len(shapes),
        scratch_shapes=[*accs, *slots, pltpu.VMEM(shared, BF16), pltpu.VMEM(shared, BF16),
                        pltpu.SemaphoreType.DMA((2 * len(jobs) + 1,)), pltpu.SemaphoreType.DMA((copies,)),
                        pltpu.SemaphoreType.DMA((copies,))],
        compiler_params=pltpu.CompilerParams(collective_id=3, has_side_effects=True, vmem_limit_bytes=24 * 2**20),
        name="weight_sums",
    )(*arrays.values(), *partials)
    count = len(arrays)
    sums = [o.reshape(w.shape) for o, w in zip(outs, named.values())]
    return sums, outs[count:-1], outs[-1].reshape(named["small"].shape)


def norm_back(inputs, row_scale, gain_vec, grad_rows):
    weighted = grad_rows * gain_vec
    cubed = row_scale * row_scale * row_scale
    input_part = row_scale * weighted - inputs * cubed * jnp.mean(inputs * weighted, axis=-1, keepdims=True)
    gain_part = jnp.sum(grad_rows * inputs * row_scale, axis=(0, 1))
    return (input_part, gain_part)


def project(activations, weight):
    return jnp.einsum("rsd,de->rse", activations, weight, preferred_element_type=F32)


def back_project(grad_rows, weight):
    return jnp.einsum("rse,de->rsd", grad_rows, weight, preferred_element_type=F32)


def weight_grad(normed, grad_rows):
    return jnp.einsum("rsd,rse->de", normed, grad_rows, preferred_element_type=F32)


def head_sum(partial, ident):
    if on_known_slice():
        return pair_sum(partial.astype(BF16), ident).astype(F32)
    return lax.psum(partial.astype(BF16), "head").astype(F32)


def rms_scale(tensor):
    return lax.rsqrt(jnp.mean(tensor * tensor, axis=-1, keepdims=True) + EPS)


def query_table(head_count):
    hd = head_count * DH
    factor = jnp.arange(head_count * RQ, dtype=jnp.int32)[:, None]
    col = jnp.arange(RQ * hd, dtype=jnp.int32)[None, :]
    return jnp.where(factor == col % hd // DH * RQ + col // hd, 1.0, 0.0).astype(BF16)


def rope_tables(position):
    half = DH // 2
    frequency = jnp.exp(jnp.arange(half).astype(F32) * (-2.0 * math.log(10000.0) / DH))
    angles = position[:, None] * frequency[None, :]
    cos, sin = jnp.cos(angles), jnp.sin(angles)
    return jnp.concatenate([cos] * 4, axis=1), jnp.concatenate([-sin, sin, -sin, sin], axis=1)


def shards(
    block_input,
    seq_lengths,
    attn_gain,
    query_heads,
    query_basis,
    key_heads,
    key_basis,
    value_heads,
    value_basis,
    out_project,
    ffn_gain,
    gate_weight,
    up_weight,
    down_weight,
    out_cotangent,
):
    row_count, slot_count, model_dim = block_input.shape
    head_count = query_heads.shape[1] // RQ
    hd = head_count * DH
    length = slot_count * lax.axis_size("seq")
    first_slot = lax.axis_index("seq") * slot_count
    width = head_count * (RK + RV)
    pack_rows = max(n for n in range(1, row_count + 1) if row_count % n == 0 and n * width <= LANES)
    group = min(4, head_count)
    block = math.gcd(length, KEY_BLOCK)
    query_spread = query_table(head_count)
    cos, sin = rope_tables((first_slot + jnp.arange(slot_count, dtype=jnp.int32)).astype(F32))
    normed, aq, bq, own_kv, own_heads, *queries = factors(
        block_input, attn_gain, query_heads.T, query_basis, key_basis, value_basis, key_heads.T, value_heads.T, cos, sin,
        query_spread, pack_rows, width, not on_known_slice())
    inputs = block_input.astype(F32)
    scale_one = rms_scale(inputs)
    shift = (1 - lax.axis_index("head")) * (row_count // CORES) if on_known_slice() else jnp.zeros((), jnp.int32)
    info = jnp.stack([*[seq_lengths[r] for r in range(row_count)], shift, first_slot]).astype(jnp.int32)
    if on_known_slice():
        kv, attended, mixed_flat, lse, queries = collect(
            seq_lengths, own_kv, own_heads, aq, bq, query_spread, pack_rows, group, width)
    else:
        (queries,) = queries
        kv = lax.all_gather(jnp.concatenate([own_kv, own_heads], axis=0), "seq", axis=1, tiled=True)
        attended, mixed_flat, lse = attend(info, queries, kv, pack_rows, group, block, width)
    attn_out = head_sum(project(mixed_flat, out_project), 4)
    middle = inputs + attn_out
    scale_two = rms_scale(middle)
    normed_two = (middle * scale_two * ffn_gain).astype(BF16)
    gate_act = project(normed_two, gate_weight)
    up_act = project(normed_two, up_weight)
    sigmoid_gate = jax.nn.sigmoid(gate_act)
    silu_gate = gate_act * sigmoid_gate
    hidden = (silu_gate * up_act).astype(BF16)
    ffn_part = project(hidden, down_weight).astype(BF16)
    cotangent = out_cotangent.astype(F32)
    d_hidden = jnp.einsum("rsd,fd->rsf", out_cotangent, down_weight, preferred_element_type=F32)
    d_gate = (d_hidden * up_act * (sigmoid_gate * (1.0 + gate_act * (1.0 - sigmoid_gate)))).astype(BF16)
    d_up = (d_hidden * silu_gate).astype(BF16)
    known = on_known_slice()
    model_cut, gate_cut = (model_dim // 2, model_dim // 4) if known else (model_dim, 0)
    gate_grad = weight_grad(normed_two[..., gate_cut:], d_gate)
    up_grad = weight_grad(normed_two, d_up)
    down_grad = weight_grad(hidden, out_cotangent[..., :model_cut])
    d_normed_two = head_sum(back_project(d_gate, gate_weight) + back_project(d_up, up_weight), 6)
    d_middle_norm, ffn_gain_part = norm_back(middle, scale_two, ffn_gain, d_normed_two)
    d_middle = cotangent + d_middle_norm
    d_branch = d_middle.astype(BF16)
    out_project_grad = jnp.einsum("rsf,rsd->fd", mixed_flat, d_branch, preferred_element_type=F32)
    d_mixed = back_project(d_branch, out_project).astype(BF16)
    d_queries, d_kv, d_heads = attend_back(info, queries, kv, attended, d_mixed, lse, pack_rows, group, block, width)
    packs = row_count // pack_rows
    if known:
        down_right = weight_grad(hidden, out_cotangent[..., model_cut:])
        gate_top = weight_grad(normed_two[..., :gate_cut], d_gate)
        (dk_basis, dv_basis, d_heads_own, dq_heads, dq_basis), (down_right, gate_top, out_project_grad) = give_back(
            d_kv, d_heads, cos, sin, d_queries, aq, bq, query_spread, pack_rows,
            {"down": down_right.astype(BF16), "gate": gate_top.astype(BF16), "out": out_project_grad.astype(BF16)})
    else:
        dq_heads, dq_basis = query_grads(d_queries, aq, bq, query_spread, cos, sin, pack_rows)
        key_grads = lax.psum_scatter(
            jnp.concatenate([d_kv, d_heads], axis=0), "seq", scatter_dimension=1, tiled=True)
        d_kv_own = key_grads[: 2 * row_count].reshape(row_count, 2, slot_count, LANES)
        half = DH // 2
        pairs = d_kv_own[:, 0].astype(F32).reshape(row_count, slot_count, 2, 2, half)
        u, w = pairs[:, :, :, 0], pairs[:, :, :, 1]
        c, s = cos[None, :, None, :half], sin[None, :, None, half:DH]
        dk_basis = jnp.stack([u * c + w * s, w * c - u * s], axis=3).reshape(row_count, slot_count, LANES).astype(BF16)
        dv_basis = d_kv_own[:, 1]
        d_heads_own = key_grads[2 * row_count :]
    d_heads_own = d_heads_own[:, :, : width * pack_rows].reshape(packs, slot_count, pack_rows, width)
    d_heads_own = jnp.transpose(d_heads_own, (0, 2, 1, 3)).reshape(row_count, slot_count, width)
    dk_heads, dv_heads = d_heads_own[..., : head_count * RK], d_heads_own[..., head_count * RK :]
    normed_part = (
        back_project(dq_heads, query_heads) + back_project(dq_basis, query_basis)
        + back_project(dk_heads, key_heads) + back_project(dk_basis, key_basis)
        + back_project(dv_heads, value_heads) + back_project(dv_basis, value_basis))
    attn_gain_part = jnp.sum(normed_part * inputs * scale_one, axis=(0, 1))
    normed_part = normed_part.astype(BF16)
    head_grads = weight_grad(jnp.concatenate([dq_heads, dk_heads, dv_heads], axis=-1), normed)
    basis_grads = weight_grad(normed, jnp.concatenate([dq_basis, dk_basis, dv_basis], axis=-1))
    small = jnp.concatenate([head_grads, attn_gain_part[None], ffn_gain_part[None]], axis=0).astype(BF16)
    gain_at = head_grads.shape[0]
    if known:
        gate_grad, up_grad, down_grad = [
            t.astype(F32) for t in lax.psum(tuple(t.astype(BF16) for t in (gate_grad, up_grad, down_grad)), "seq")]
        gate_grad = jnp.concatenate([gate_top.astype(F32), gate_grad], axis=0)
        down_grad = jnp.concatenate([down_grad, down_right.astype(F32)], axis=1)
        height = small.shape[0]
        wide = model_dim // LANES
        small = jnp.pad(small, ((0, -height % 32), (0, 0)))
        full = small.shape[0]
        small = jnp.transpose(small.reshape(full, wide, LANES), (1, 0, 2))
        (small, basis_grads), (normed_other, ffn_other), small_other = weight_sums(
            {"small": small, "basis": basis_grads.astype(BF16)}, (normed_part, ffn_part))
        attn_gain_grad = (small[:, gain_at].astype(F32) + small_other[:, gain_at].astype(F32)).reshape(model_dim)
        small = jnp.transpose(small, (1, 0, 2)).reshape(full, model_dim)
        d_normed = normed_part.astype(F32) + normed_other.astype(F32)
        ffn_out = ffn_part.astype(F32) + ffn_other.astype(F32)
    else:
        sums = lax.psum(tuple(t.astype(BF16) for t in (gate_grad, up_grad, down_grad, out_project_grad, small)), "seq")
        gate_grad, up_grad, down_grad, out_project_grad, small = [t.astype(F32) for t in sums]
        attn_gain_grad = lax.psum(small[gain_at].astype(BF16), "head").astype(F32)
        basis_grads = lax.psum(basis_grads, ("seq", "head"))
        d_normed = lax.psum(normed_part, "head").astype(F32)
        ffn_out = lax.psum(ffn_part, "head").astype(F32)
    d_input_norm, _ = norm_back(inputs, scale_one, attn_gain, d_normed)
    input_grad = d_middle + d_input_norm
    block_output = (middle + ffn_out).astype(BF16)
    nq, nk, nv = head_count * RQ, head_count * RK, head_count * RV
    cuts = (0, nq, nq + nk, nq + nk + nv)
    query_heads_grad, key_heads_grad, value_heads_grad = [small[i:j].astype(F32).T for i, j in zip(cuts, cuts[1:])]
    cuts = (0, RQ * DH, (RQ + RK) * DH, (RQ + RK + RV) * DH)
    query_basis_grad, key_basis_grad, value_basis_grad = [basis_grads[:, i:j].astype(F32) for i, j in zip(cuts, cuts[1:])]
    return (
        block_output,
        input_grad,
        attn_gain_grad,
        query_heads_grad,
        query_basis_grad,
        key_heads_grad,
        key_basis_grad,
        value_heads_grad,
        value_basis_grad,
        out_project_grad.astype(F32),
        small[nq + nk + nv + 1].astype(F32),
        gate_grad,
        up_grad,
        down_grad,
    )


def solution(mesh):
    rows = P(None, "seq", None)
    columns, features = P(None, "head"), P("head", None)
    in_specs = (rows, P(), P(), columns, P(), columns, P(), columns, P(), features, P(), columns, columns, features, rows)
    out_specs = (rows, rows, P(), columns, P(), columns, P(), columns, P(), features, P(), columns, columns, features)
    return jax.shard_map(shards, mesh=mesh, in_specs=in_specs, out_specs=out_specs, check_vma=False)
```
